256 devices in a mesh: tiles: 32 (over z, x_hi, core), lat: 8 (over x_lo, y).
Axes of the slice: x: 4 (x_hi: 2, x_lo: 2; x = x_hi * 2 + x_lo), y: 4, z: 8, core: 2. Of those that a mesh axis runs over, the one named last changes fastest.
Arguments:
- ocean_state: bfloat16 [8, 64, 16, 3200], P('lat', 'tiles'), may hold values from -6 to 6
- land_mask: int32 [8, 64, 256], P('lat', 'tiles'), may hold values 0 or 1
- wet_count: int32 [8, 32], P('lat', 'tiles'), may hold values from 0 to 2, as said below
- neighbours: int32 [8, 64, 4], P('lat', 'tiles'), may hold values from -1 to 8, as said below
- kern_one: bfloat16 [7, 7, 200], replicated, may hold values from -0.875 to 0.875
- w_in_one: bfloat16 [200, 800], replicated, may hold values from -0.4375 to 0.4375
- w_out_one: bfloat16 [800, 200], replicated, may hold values from -0.21875 to 0.21875
- w_down: bfloat16 [800, 400], replicated, may hold values from -0.21875 to 0.21875
- kern_two: bfloat16 [7, 7, 400], replicated, may hold values from -0.875 to 0.875
- w_in_two: bfloat16 [400, 1600], replicated, may hold values from -0.3125 to 0.3125
- w_out_two: bfloat16 [1600, 400], replicated, may hold values from -0.15625 to 0.15625
- w_up: bfloat16 [400, 800], replicated, may hold values from -0.3125 to 0.3125
- cotangent: bfloat16 [8, 64, 16, 3200], P('lat', 'tiles'), may hold values from -0.0234375 to 0.0234375
Outputs:
- prediction: bfloat16 [8, 64, 16, 3200], P('lat', 'tiles')
- grads: float32 [2293760], P(('tiles', 'lat'))
The draws below stay inside these ranges and needn't reach their ends.
Inputs may be any that keep to these rules, and one draw needn't show every extreme that they name: wet_count[b, g] counts the filled slots of group g in band b, slots 0 to wet_count - 1 of the group. Groups g and g + N/2 of a band (N groups) hold 2 tiles together, and one group, the same in every band, holds 2. `neighbours`: an entry of an empty slot, or one whose neighbour is land, off the grid's northern or southern edge, is -1. West and east entries use codes 0 to 2, north and south entries codes 0, 3 and 4. Bands hold 2 tile rows and every group 1 tile columns of its band, the same columns in every band, periodic from west to east; entries are mutual.
All inputs are finite; a program needn't handle non-finite values. No bound on the sum of `land_mask` on one device may be relied on, other than what follows from the above.
Results may differ from the reference program's by a relative error of at most 0.014.
Values may be sent and summed in bfloat16 or wider, within the bound.
No kernel may reach another device: no remote copies, remote signals or barrier semaphores. Data moves between devices by JAX's collectives and lax.ppermute only.
A program may use at most 128 MiB of HBM per device.

```python
import jax
import jax.numpy as jnp
from jax import lax

C1 = 200
C2 = 400
KERNEL = 7
TS1 = 16
ROWS_BAND = 2
COLS_DEV = 1
HOME = 2
CAP = 1
TILES = 64
GRAD_LEN = 2293760
N_TILES = 32
N_LAT = 8


def tile_layout(key):
    pair_count = N_TILES // 2
    share = HOME // 2
    key_shift, key_full, key_order = jax.random.split(key, 3)
    shifts = jax.random.randint(key_shift, (N_LAT, pair_count), -share, share + 1)
    chosen = jax.random.randint(key_full, (1, 1), 0, pair_count)
    shifts = jnp.where(jnp.arange(pair_count)[None, :] == chosen, share, shifts)
    counts = jnp.concatenate([share + shifts, share - shifts], axis=1).astype(jnp.int32)
    scores = jax.random.randint(key_order, (N_LAT, N_TILES, HOME), 0, 1 << 20) * HOME + jnp.arange(HOME)[None, None, :]
    ranks = jnp.argsort(jnp.argsort(scores, axis=-1), axis=-1)
    wetness = ranks < counts[:, :, None]
    slot_ids = jnp.cumsum(wetness.astype(jnp.int32), axis=-1) - 1
    return (counts, wetness, slot_ids)


def draw_wet_count(key, part):
    counts, wetness, slot_ids = tile_layout(key)
    return counts


def draw_neighbours(key, part):
    counts, wetness, slot_ids = tile_layout(key)
    values = jnp.where(wetness, slot_ids, -1).reshape(N_LAT, N_TILES, COLS_DEV, ROWS_BAND)
    column_ids = jnp.arange(COLS_DEV)[None, None, :, None]
    row_ids = jnp.arange(ROWS_BAND)[None, None, None, :]
    band_ids = jnp.arange(N_LAT)[:, None, None, None]
    from_west = jnp.roll(values, 1, axis=1)
    from_east = jnp.roll(values, -1, axis=1)
    west = jnp.concatenate([from_west[:, :, -1:, :], values[:, :, :-1, :]], axis=2)
    west_source = jnp.where(column_ids == 0, 1, 0)
    east = jnp.concatenate([values[:, :, 1:, :], from_east[:, :, :1, :]], axis=2)
    east_source = jnp.where(column_ids == COLS_DEV - 1, 2, 0)
    above = jnp.roll(values, 1, axis=0)
    below = jnp.roll(values, -1, axis=0)
    north = jnp.where(row_ids > 0, jnp.roll(values, 1, axis=3), above[..., ROWS_BAND - 1:ROWS_BAND])
    north = jnp.where((row_ids == 0) & (band_ids == 0), -1, north)
    north_source = jnp.where(row_ids > 0, 0, 3)
    south = jnp.where(row_ids < ROWS_BAND - 1, jnp.roll(values, -1, axis=3), below[..., 0:1])
    south = jnp.where((row_ids == ROWS_BAND - 1) & (band_ids == N_LAT - 1), -1, south)
    south_source = jnp.where(row_ids < ROWS_BAND - 1, 0, 4)

    def encode(target, source):
        return jnp.where(target >= 0, source * HOME + target, -1)
    codes = jnp.stack([encode(west, west_source), encode(east, east_source), encode(north, north_source), encode(south, south_source)], axis=-1)
    codes = codes.reshape(N_LAT, N_TILES, HOME, 4)
    onehot = (slot_ids[:, :, None, :] == jnp.arange(HOME)[None, None, :, None]) & wetness[:, :, None, :]
    per_slot = jnp.sum(jnp.where(onehot[..., None], codes[:, :, None, :, :] + 1, 0), axis=3) - 1
    return per_slot.reshape(N_LAT, N_TILES * HOME, 4).astype(jnp.int32)


def set_ends(result, rng, low, top_value):
    place = [jax.random.randint(jax.random.fold_in(rng, axis), (), 0, length) for axis, length in enumerate(result.shape)]
    widest = result.shape.index(max(result.shape))
    beside = place[:widest] + [(place[widest] + 1) % result.shape[widest]] + place[widest + 1:]
    return result.at[tuple(place)].set(low).at[tuple(beside)].set(top_value)


def shard_levels(key, shape, cuts, smallest, largest):
    loudness = 1.0
    for dim, parts in cuts:
        steps = jax.random.uniform(jax.random.fold_in(jax.random.fold_in(key, 6), dim), (parts,), jnp.float32, smallest / len(cuts), largest / len(cuts))
        loudness = loudness * jnp.repeat(jnp.exp(steps), shape[dim] // parts).reshape((-1,) + (1,) * (len(shape) - 1 - dim))
    return loudness


def bell_draw(own_key, shape, width, reach, shards=(), kind=jnp.bfloat16):
    values = width * jax.random.normal(own_key, shape, jnp.float32)
    if shards:
        values = values * shard_levels(own_key, shape, shards, -0.22, 0.18)
    return jnp.clip(values, -reach, reach).astype(kind)


def setup_inputs(seed: int = 0) -> dict:
    splits = jax.random.split(jax.random.key(seed), 14)
    return {
        "ocean_state": bell_draw(splits[0], (N_LAT, TILES, TS1, TS1 * C1), 1.0, 6.0, ((0, 8), (1, 32))),
        "land_mask": set_ends((jax.random.randint(splits[1], (N_LAT, TILES, TS1 * TS1), 0, 8) < 7).astype(jnp.int32), jax.random.fold_in(splits[1], 1), 0, 1),
        "wet_count": draw_wet_count(jax.random.fold_in(splits[13], 71), 0),
        "neighbours": draw_neighbours(jax.random.fold_in(splits[13], 71), 0),
        "kern_one": bell_draw(splits[4], (KERNEL, KERNEL, C1), (KERNEL * KERNEL) ** -0.5, 0.875),
        "w_in_one": bell_draw(splits[5], (C1, 4 * C1), C1 ** -0.5, 0.4375),
        "w_out_one": bell_draw(splits[6], (4 * C1, C1), (4 * C1) ** -0.5, 0.21875),
        "w_down": bell_draw(splits[7], (4 * C1, C2), (4 * C1) ** -0.5, 0.21875),
        "kern_two": bell_draw(splits[8], (KERNEL, KERNEL, C2), (KERNEL * KERNEL) ** -0.5, 0.875),
        "w_in_two": bell_draw(splits[9], (C2, 4 * C2), C2 ** -0.5, 0.3125),
        "w_out_two": bell_draw(splits[10], (4 * C2, C2), (4 * C2) ** -0.5, 0.15625),
        "w_up": bell_draw(splits[11], (C2, 4 * C1), C2 ** -0.5, 0.3125),
        "cotangent": bell_draw(splits[12], (N_LAT, TILES, TS1, TS1 * C1), ((N_LAT * N_TILES * CAP * TS1 * TS1) ** -0.5), 0.0234375, ((0, 8), (1, 32))),
    }


EPSILON = 1e-06
TANH_SCALE = 0.7978845608028654
CUBIC = 0.044715

def product(left, right):
    return jnp.dot(left, right, preferred_element_type=jnp.float32)

def gelu_tanh(values):
    return 0.5 * values * (1.0 + jnp.tanh(TANH_SCALE * (values + CUBIC * values * values * values)))

def gelu_slope(values):
    inner = jnp.tanh(TANH_SCALE * (values + CUBIC * values * values * values))
    return 0.5 * (1.0 + inner) + 0.5 * values * (1.0 - inner * inner) * TANH_SCALE * (1.0 + 3.0 * CUBIC * values * values)

def layer_norm(rows):
    center = rows - lax.optimization_barrier(jnp.mean(rows, axis=-1, keepdims=True))
    scale = lax.rsqrt(lax.optimization_barrier(jnp.mean(center * center, axis=-1, keepdims=True)) + EPSILON)
    return (center * scale, scale)

def norm_back(grad_norm, normed, scale):
    mean_grad = lax.optimization_barrier(jnp.mean(grad_norm, axis=-1, keepdims=True))
    mean_cross = lax.optimization_barrier(jnp.mean(grad_norm * normed, axis=-1, keepdims=True))
    return (grad_norm - mean_grad - normed * mean_cross) * scale

def depthwise(widened, kernel, patch_side_span, feature_number, flipped):
    number = widened.shape[0]
    extent = kernel.shape[0]
    canvas = widened.reshape(number, patch_side_span + extent - 1, patch_side_span + extent - 1, feature_number)
    running = jnp.zeros((number, patch_side_span, patch_side_span, feature_number), jnp.float32)
    for row_off in range(extent):
        for col_off in range(extent):
            if flipped:
                weight_tap = kernel[extent - 1 - row_off, extent - 1 - col_off]
            else:
                weight_tap = kernel[row_off, col_off]
            window = canvas[:, row_off:row_off + patch_side_span, col_off:col_off + patch_side_span, :]
            running = running + window.astype(jnp.float32) * weight_tap.astype(jnp.float32)
    return running.reshape(-1, feature_number)

def kernel_grad(widened, delta, patch_side_span, feature_number, extent):
    number = widened.shape[0]
    canvas = widened.reshape(number, patch_side_span + extent - 1, patch_side_span + extent - 1, feature_number)
    delta_grid = delta.reshape(number, patch_side_span, patch_side_span, feature_number)
    gradient_rows = []
    for row_off in range(extent):
        row_list = []
        for col_off in range(extent):
            window = canvas[:, row_off:row_off + patch_side_span, col_off:col_off + patch_side_span, :]
            row_list.append(lax.optimization_barrier(jnp.sum(window.astype(jnp.float32) * delta_grid, axis=(0, 1, 2))))
        gradient_rows.append(jnp.stack(row_list))
    return jnp.stack(gradient_rows)

def blocks_of(rows, number, patch_side_span, feature_number):
    coarse_side = patch_side_span // 2
    shaped = rows.reshape(number, coarse_side, 2, coarse_side, 2, feature_number)
    return shaped.transpose(0, 1, 3, 2, 4, 5).reshape(-1, 4 * feature_number)

def cells_of(blocks, number, patch_side_span, feature_number):
    coarse_side = patch_side_span // 2
    shaped = blocks.reshape(number, coarse_side, coarse_side, 2, 2, feature_number)
    return shaped.transpose(0, 1, 3, 2, 4, 5).reshape(-1, feature_number)

def mlp_forward(normed_b, w_in, w_out):
    pre_act = product(normed_b, w_in)
    hidden = gelu_tanh(pre_act).astype(jnp.bfloat16)
    return (product(hidden, w_out), hidden, pre_act)

def mlp_backward(delta, normed_b, hidden, pre_act, w_in, w_out):
    target_derivative = product(hidden.T, delta)
    grad_pre = (product(delta, w_out.T) * gelu_slope(pre_act)).astype(jnp.bfloat16)
    source_derivative = product(normed_b.T, grad_pre)
    return (target_derivative, source_derivative, product(grad_pre, w_in.T))

def extend(tile_field, entries, patch_side_span, feature_number):
    latitude_strip_number = tile_field.shape[0]
    patch_number = tile_field.shape[1]
    group_count = patch_number // HOME
    group_ids = jnp.arange(patch_number, dtype=jnp.int32) // HOME
    band_ids = jnp.arange(latitude_strip_number, dtype=jnp.int32)
    present = entries >= 0
    source = jnp.clip(entries // HOME, 0, 4)
    group_step = jnp.asarray([0, -1, 1, 0, 0], jnp.int32)[source]
    band_step = jnp.asarray([0, 0, 0, -1, 1], jnp.int32)[source]
    source_group = (group_ids[None, :, None] + group_step) % group_count
    source_band = jnp.clip(band_ids[:, None, None] + band_step, 0, latitude_strip_number - 1)
    row_index = jnp.where(present, source_band * patch_number + source_group * HOME + entries % HOME, 0).astype(jnp.int32)

    def fetch(stacked, which):
        fetched = jnp.take(stacked, row_index[..., which].reshape(-1), axis=0)
        fetched = fetched.reshape((latitude_strip_number, patch_number) + stacked.shape[1:])
        return jnp.where(present[..., which][..., None, None], fetched, jnp.zeros_like(fetched))
    stacked = tile_field.reshape((latitude_strip_number * patch_number,) + tile_field.shape[2:])
    widened = jnp.concatenate([fetch(stacked[:, :, (patch_side_span - 3) * feature_number:], 0), tile_field, fetch(stacked[:, :, :3 * feature_number], 1)], axis=3)
    stacked_wide = widened.reshape((latitude_strip_number * patch_number,) + widened.shape[2:])
    return jnp.concatenate([fetch(stacked_wide[:, patch_side_span - 3:], 2), widened, fetch(stacked_wide[:, :3], 3)], axis=2)

def reference(ocean_state, land_mask, wet_count, neighbours, kern_one, w_in_one, w_out_one, w_down, kern_two, w_in_two, w_out_two, w_up, cotangent):
    latitude_strip_number = N_LAT
    patch_number = N_TILES * HOME
    patch_side_span = TS1
    coarse_side = TS1 // 2
    feature_number = C1
    coarse_channels = C2
    extent = KERNEL
    filled = (jnp.arange(HOME, dtype=jnp.int32)[None, None, :] < wet_count[:, :, None]).reshape(latitude_strip_number, patch_number).astype(jnp.float32)
    mask_fine = land_mask.astype(jnp.float32) * filled[:, :, None]
    rough_wet_lattice = mask_fine.reshape(latitude_strip_number, patch_number, coarse_side, 2, coarse_side, 2).max(axis=(3, 5)).reshape(latitude_strip_number, -1, 1)
    line_wet_items = mask_fine.reshape(latitude_strip_number, -1, 1)
    fields = (ocean_state.reshape(latitude_strip_number, -1, feature_number).astype(jnp.float32) * line_wet_items).astype(jnp.bfloat16)
    wet_adjoint_values = (cotangent.reshape(latitude_strip_number, -1, feature_number).astype(jnp.float32) * line_wet_items).astype(jnp.bfloat16)
    widened_one = extend(fields.reshape(latitude_strip_number, patch_number, patch_side_span, patch_side_span * feature_number), neighbours, patch_side_span, feature_number)

    def first_level(inputs):
        widened, field_rows, initial_wet_flags, mask_two = inputs
        normed, scale = layer_norm(depthwise(widened, kern_one, patch_side_span, feature_number, False))
        branch, hidden, pre_act = mlp_forward(normed.astype(jnp.bfloat16), w_in_one, w_out_one)
        sharpest_scale = (initial_wet_flags * (field_rows.astype(jnp.float32) + branch)).astype(jnp.bfloat16)
        coarse = (mask_two * product(blocks_of(sharpest_scale, patch_number, patch_side_span, feature_number), w_down)).astype(jnp.bfloat16)
        return (sharpest_scale, coarse)
    sharpest_scale_items, rough_scale_items = lax.map(first_level, (widened_one, fields, line_wet_items, rough_wet_lattice))
    broadened_two = extend(rough_scale_items.reshape(latitude_strip_number, patch_number, coarse_side, coarse_side * coarse_channels), neighbours, coarse_side, coarse_channels)

    def reduced_detail_scale(inputs):
        widened, coarse, sharpest_scale, initial_wet_flags, mask_two, masked_cot = inputs
        normed, scale = layer_norm(depthwise(widened, kern_two, coarse_side, coarse_channels, False))
        normed_b = normed.astype(jnp.bfloat16)
        branch, hidden, pre_act = mlp_forward(normed_b, w_in_two, w_out_two)
        level_two = (mask_two * (coarse.astype(jnp.float32) + branch)).astype(jnp.bfloat16)
        lifted_state = cells_of(product(level_two, w_up), patch_number, patch_side_span, feature_number)
        prediction = (initial_wet_flags * (sharpest_scale.astype(jnp.float32) + lifted_state)).astype(jnp.bfloat16)
        cot_blocks = blocks_of(masked_cot, patch_number, patch_side_span, feature_number)
        ascending_derivative = product(level_two.T, cot_blocks)
        change_two = (mask_two * product(cot_blocks, w_up.T)).astype(jnp.bfloat16)
        target_derivative, source_derivative, grad_norm = mlp_backward(change_two, normed_b, hidden, pre_act, w_in_two, w_out_two)
        reverse_step_two = norm_back(grad_norm, normed, scale).astype(jnp.bfloat16)
        filter_derivative = kernel_grad(widened, reverse_step_two.astype(jnp.float32), coarse_side, coarse_channels, extent)
        return (prediction, change_two, reverse_step_two, ascending_derivative, target_derivative, source_derivative, filter_derivative)
    prediction, change_two_items, reverse_step_two_items, ascending_derivative, target_derivative_two, source_derivative_two, filter_derivative_two = lax.map(reduced_detail_scale, (broadened_two, rough_scale_items, sharpest_scale_items, line_wet_items, rough_wet_lattice, wet_adjoint_values))
    widened_back = extend(reverse_step_two_items.reshape(latitude_strip_number, patch_number, coarse_side, coarse_side * coarse_channels), neighbours, coarse_side, coarse_channels)

    def first_back(inputs):
        widened_delta, change_two, masked_cot, sharpest_scale, widened, initial_wet_flags, mask_two = inputs
        delta_coarse = (mask_two * (change_two.astype(jnp.float32) + depthwise(widened_delta, kern_two, coarse_side, coarse_channels, True))).astype(jnp.bfloat16)
        grad_down = product(blocks_of(sharpest_scale, patch_number, patch_side_span, feature_number).T, delta_coarse)
        spread = cells_of(product(delta_coarse, w_down.T), patch_number, patch_side_span, feature_number)
        delta_one = (initial_wet_flags * (masked_cot.astype(jnp.float32) + spread)).astype(jnp.bfloat16)
        normed, scale = layer_norm(depthwise(widened, kern_one, patch_side_span, feature_number, False))
        normed_b = normed.astype(jnp.bfloat16)
        branch, hidden, pre_act = mlp_forward(normed_b, w_in_one, w_out_one)
        target_derivative, source_derivative, grad_norm = mlp_backward(delta_one, normed_b, hidden, pre_act, w_in_one, w_out_one)
        back_one = norm_back(grad_norm, normed, scale)
        filter_derivative = kernel_grad(widened, back_one, patch_side_span, feature_number, extent)
        return (grad_down, target_derivative, source_derivative, filter_derivative)
    grad_down, grad_out_one, grad_in_one, grad_kern_one = lax.map(first_back, (widened_back, change_two_items, wet_adjoint_values, sharpest_scale_items, widened_one, line_wet_items, rough_wet_lattice))
    pieces = (grad_kern_one, grad_in_one, grad_out_one, grad_down, filter_derivative_two, source_derivative_two, target_derivative_two, ascending_derivative)
    unrolled_state = jnp.concatenate([lax.optimization_barrier(jnp.sum(piece, axis=0)).reshape(-1) for piece in pieces])
    unrolled_state = jnp.concatenate([unrolled_state, jnp.zeros((GRAD_LEN - unrolled_state.shape[0],), jnp.float32)])
    return (prediction.reshape(latitude_strip_number, patch_number, patch_side_span, patch_side_span * feature_number), unrolled_state)
```

```python
import functools

import jax
import jax.numpy as jnp
import numpy as np
from jax import lax
from jax.experimental import pallas as pl
from jax.experimental.pallas import tpu as pltpu
from jax.sharding import Mesh
from jax.sharding import PartitionSpec as P

TILES = ("z", "xh", "c")
LAT = ("xl", "y")
EPSILON = 1e-06
TANH_SCALE = 0.7978845608028654
CUBIC = 0.044715
LANES = 128
PIECE = 70
HELD = 72
UNIT = 3200
SOURCE_PART = np.array(
    [[2, 0, -1, -1, -1], [1, -1, 3, -1, -1], [2, -1, -1, 0, -1], [1, -1, -1, -1, 3]], dtype=np.int32
)


def with_halo(array, sides, width, wrap):
    for axis, dim in sides:
        size, length = (lax.axis_size(axis), array.shape[dim])
        up = [(i, (i + 1) % size) for i in range(size if wrap else size - 1)]
        down = [(j, i) for i, j in up]
        last = lax.slice_in_dim(array, length - width, length, axis=dim)
        initial = lax.slice_in_dim(array, 0, width, axis=dim)
        before = lax.ppermute(last, axis, up)
        after = lax.ppermute(initial, axis, down)
        array = jnp.concatenate([before, array, after], axis=dim)
    return array


def product(left, right):
    return jnp.dot(left, right, preferred_element_type=jnp.float32)


def gelu_tanh(values):
    return 0.5 * values * (1.0 + jnp.tanh(TANH_SCALE * (values + CUBIC * values * values * values)))


def gelu_slope(values):
    inner = jnp.tanh(TANH_SCALE * (values + CUBIC * values * values * values))
    return 0.5 * (1.0 + inner) + 0.5 * values * (1.0 - inner * inner) * TANH_SCALE * (
        1.0 + 3.0 * CUBIC * values * values
    )


def layer_norm(rows):
    center = rows - jnp.mean(rows, axis=-1, keepdims=True)
    scale = lax.rsqrt(jnp.mean(center * center, axis=-1, keepdims=True) + EPSILON)
    return (center * scale, scale)


def norm_back(grad_norm, normed, scale):
    mean_grad = jnp.mean(grad_norm, axis=-1, keepdims=True)
    mean_cross = jnp.mean(grad_norm * normed, axis=-1, keepdims=True)
    return (grad_norm - mean_grad - normed * mean_cross) * scale


def depthwise(widened, kernel, patch_side_span, feature_number, flipped):
    number = widened.shape[0]
    extent = kernel.shape[0]
    canvas = widened.reshape(
        number, patch_side_span + extent - 1, patch_side_span + extent - 1, feature_number
    )
    running = jnp.zeros((number, patch_side_span, patch_side_span, feature_number), jnp.float32)
    for row_off in range(extent):
        for col_off in range(extent):
            if flipped:
                weight_tap = kernel[extent - 1 - row_off, extent - 1 - col_off]
            else:
                weight_tap = kernel[row_off, col_off]
            window = canvas[
                :, row_off : row_off + patch_side_span, col_off : col_off + patch_side_span, :
            ]
            running = running + window.astype(jnp.float32) * weight_tap.astype(jnp.float32)
    return running.reshape(-1, feature_number)


def kernel_grad(widened, delta, patch_side_span, feature_number, extent):
    number = widened.shape[0]
    canvas = widened.reshape(
        number, patch_side_span + extent - 1, patch_side_span + extent - 1, feature_number
    )
    delta_grid = delta.reshape(number, patch_side_span, patch_side_span, feature_number)
    gradient_rows = []
    for row_off in range(extent):
        row_list = []
        for col_off in range(extent):
            window = canvas[
                :, row_off : row_off + patch_side_span, col_off : col_off + patch_side_span, :
            ]
            row_list.append(jnp.sum(window.astype(jnp.float32) * delta_grid, axis=(0, 1, 2)))
        gradient_rows.append(jnp.stack(row_list))
    return jnp.stack(gradient_rows)


def blocks_of(rows, number, patch_side_span, feature_number):
    coarse_side = patch_side_span // 2
    shaped = rows.reshape(number, coarse_side, 2, coarse_side, 2, feature_number)
    return shaped.transpose(0, 1, 3, 2, 4, 5).reshape(-1, 4 * feature_number)


def cells_of(blocks, number, patch_side_span, feature_number):
    coarse_side = patch_side_span // 2
    shaped = blocks.reshape(number, coarse_side, coarse_side, 2, 2, feature_number)
    return shaped.transpose(0, 1, 3, 2, 4, 5).reshape(-1, feature_number)


def mlp_forward(normed_b, w_in, w_out):
    pre_act = product(normed_b, w_in)
    hidden = gelu_tanh(pre_act).astype(jnp.bfloat16)
    return (product(hidden, w_out), hidden, pre_act)


def mlp_backward(delta, normed_b, hidden, pre_act, w_in, w_out):
    target_derivative = product(hidden.T, delta)
    grad_pre = (product(delta, w_out.T) * gelu_slope(pre_act)).astype(jnp.bfloat16)
    source_derivative = product(normed_b.T, grad_pre)
    return (target_derivative, source_derivative, product(grad_pre, w_in.T))


def pick_rows(stacked, entry_col, direction, place_number):
    present = entry_col >= 0
    source = jnp.clip(entry_col // place_number, 0, 4)
    pool_part = jnp.maximum(jnp.asarray(SOURCE_PART)[direction][source], 0)
    row_index = jnp.where(present, pool_part * place_number + entry_col % place_number, 0)
    fetched = jnp.take(stacked, row_index, axis=0)
    return jnp.where(present[:, None, None], fetched, jnp.zeros_like(fetched))


def widen(tile_field, entries, patch_side_span, feature_number):
    place_number = tile_field.shape[0]
    west_rims = tile_field[:, :, : 3 * feature_number]
    east_rims = tile_field[:, :, (patch_side_span - 3) * feature_number :]
    beside = with_halo(jnp.stack([west_rims, east_rims]), ((TILES, 0),), 1, True)
    stacked = beside.reshape(4 * place_number, patch_side_span, 3 * feature_number)
    widened = jnp.concatenate(
        [
            pick_rows(stacked, entries[:, 0], 0, place_number),
            tile_field,
            pick_rows(stacked, entries[:, 1], 1, place_number),
        ],
        axis=2,
    )
    top_rows = widened[:, :3]
    bottom_rows = widened[:, patch_side_span - 3 :]
    banded = with_halo(jnp.stack([top_rows, bottom_rows]), ((LAT, 0),), 1, False)
    stacked_band = banded.reshape(4 * place_number, 3, widened.shape[2])
    return jnp.concatenate(
        [
            pick_rows(stacked_band, entries[:, 2], 2, place_number),
            widened,
            pick_rows(stacked_band, entries[:, 3], 3, place_number),
        ],
        axis=1,
    )


def lay_flat(flat, source, first_entry, rows, width, first_row):
    unit = UNIT // width
    count = rows // unit
    base = first_entry // LANES - first_row
    tiles = -(-width // LANES)
    lane = lax.broadcasted_iota(jnp.int32, (count, LANES), 1)
    parts = {}
    for a in range(unit):
        for t in range(tiles):
            value = source[t, pl.ds(a, count, stride=unit), :]
            place = first_entry % LANES + width * a + LANES * t
            shift = place % LANES
            if shift:
                value = pltpu.roll(value, shift, 1)
                low = jnp.where(lane >= shift, value, 0.0)
                high = jnp.where(lane < shift, value, 0.0)
                parts.setdefault(place // LANES, []).append(low)
                if not (t == tiles - 1 and shift + width - LANES * t <= LANES):
                    parts.setdefault(place // LANES + 1, []).append(high)
            else:
                parts.setdefault(place // LANES, []).append(value)
    merged = {j: functools.reduce(jnp.add, values) for j, values in parts.items()}
    for j in range(1, 25):
        flat[pl.ds(base + j, count, stride=25), :] = merged[j]
    head = merged[0]
    if 25 in merged:
        tail = merged[25]
        row = lax.broadcasted_iota(jnp.int32, (count, LANES), 0)
        before = pltpu.roll(tail, 1, 0) if count % 8 == 0 else jnp.concatenate([tail[-1:], tail[:-1]], axis=0)
        head = head + jnp.where(row > 0, before, 0.0)
    opening = flat[base : base + 1, :]
    flat[pl.ds(base, count, stride=25), :] = head
    flat[base : base + 1, :] = flat[base : base + 1, :] + opening
    if 25 in merged:
        flat[base + 25 * count : base + 25 * count + 1, :] = tail[count - 1 : count, :]
    else:
        flat[base + 25 * count : base + 25 * count + 1, :] = jnp.zeros((1, LANES), jnp.float32)


ROWS = 17920
SIZES = ((7 * 7, 200), (200, 800), (800, 200), (800, 400), (7 * 7, 400), (400, 1600), (1600, 400), (400, 800))


def pack_kernel(core_ref, *refs):
    sources, out, flat, held = refs[:8], refs[8], refs[9], refs[10]
    flat[0:8, :] = jnp.zeros((8, LANES), jnp.float32)
    first = 0
    for source, (rows, width) in zip(sources, SIZES):
        unit = UNIT // width
        padded = -(-rows // unit) * unit
        tiles = -(-width // LANES)
        for t in range(tiles):
            part = source[:, t * LANES : min(width, (t + 1) * LANES)]
            if (t + 1) * LANES > width:
                held[t, :padded, :] = jnp.zeros((padded, LANES), jnp.float32)
            elif padded > rows:
                held[t, rows - rows % 8 : padded, :] = jnp.zeros((padded - rows + rows % 8, LANES), jnp.float32)
            held[t, :rows, : part.shape[1]] = part
        lay_flat(flat, held, first, padded, width, 0)
        first += rows * width
    last = -(-first // LANES)
    flat[last:, :] = jnp.zeros((ROWS + 8 - last, LANES), jnp.float32)
    core = core_ref[0]
    for block in range(32):
        z, xh, c = block // 4, block // 2 % 2, block % 2
        slot = jnp.where(core == c, 0, 1)
        for xl in range(2):
            for y in range(4):
                start = block * 560 + (xl * 4 + y) * PIECE
                out[slot, y, xl, xh, z] = flat[start : start + HELD, :].astype(jnp.bfloat16)


def pack(core, pieces):
    return pl.pallas_call(
        pack_kernel,
        out_shape=jax.ShapeDtypeStruct((2, 4, 2, 2, 8, HELD, LANES), jnp.bfloat16),
        in_specs=[pl.BlockSpec(memory_space=pltpu.SMEM)] + [pl.BlockSpec(memory_space=pltpu.VMEM)] * 8,
        out_specs=pl.BlockSpec(memory_space=pltpu.VMEM),
        scratch_shapes=[
            pltpu.VMEM((ROWS + 8, LANES), jnp.float32),
            pltpu.VMEM((13, 1600, LANES), jnp.float32),
        ],
        compiler_params=pltpu.CompilerParams(vmem_limit_bytes=60 * 2**20),
    )(core, *pieces)


def wide(values):
    return values.astype(jnp.float32)


def reduce_scatter(pieces):
    core = lax.axis_index("c").reshape(1).astype(jnp.int32)
    halves = pack(core, pieces)
    got = lax.ppermute(halves[1], "c", [(0, 1), (1, 0)])
    total = (wide(halves[0]) + wide(got)).astype(jnp.bfloat16)
    for axes, count in ((("y",), 4), (("xl", "xh"), 4)):
        total = total.reshape((count,) + total.shape[len(axes):])
        got = lax.all_to_all(total, axes, 0, 0)
        total = wide(got).sum(axis=0).astype(jnp.bfloat16)
    got = lax.all_to_all(total, "z", 0, 0)
    return wide(got).sum(axis=0)[:PIECE].reshape(-1)


def local(
    ocean_state,
    land_mask,
    wet_count,
    neighbours,
    kern_one,
    w_in_one,
    w_out_one,
    w_down,
    kern_two,
    w_in_two,
    w_out_two,
    w_up,
    cotangent,
):
    place_number = ocean_state.shape[1]
    patch_side_span = ocean_state.shape[2]
    feature_number = ocean_state.shape[3] // patch_side_span
    coarse_side = patch_side_span // 2
    coarse_channels = w_down.shape[1]
    extent = kern_one.shape[0]
    fine_cells = patch_side_span * patch_side_span
    coarse_cells = coarse_side * coarse_side
    filled_count = wet_count[0, 0]
    slot_ids = jnp.arange(place_number, dtype=jnp.int32)
    filled = (slot_ids < filled_count).astype(jnp.float32)
    mask_fine = land_mask[0].astype(jnp.float32) * filled[:, None]
    rough_wet_lattice = (
        mask_fine.reshape(place_number, coarse_side, 2, coarse_side, 2)
        .max(axis=(2, 4))
        .reshape(-1, 1)
    )
    line_wet_items = mask_fine.reshape(-1, 1)
    fields = (
        ocean_state[0].reshape(-1, feature_number).astype(jnp.float32) * line_wet_items
    ).astype(jnp.bfloat16)
    entries = neighbours[0]
    widened_one = widen(
        fields.reshape(place_number, patch_side_span, patch_side_span * feature_number),
        entries,
        patch_side_span,
        feature_number,
    )
    normed_one, scale_one = layer_norm(
        depthwise(widened_one, kern_one, patch_side_span, feature_number, False)
    )
    work_one = (
        normed_one.astype(jnp.bfloat16)
        .reshape(place_number, fine_cells, feature_number)
        .reshape(-1, feature_number)
    )
    branch_work, hidden_one, pre_one = mlp_forward(work_one, w_in_one, w_out_one)
    branch_one = branch_work.reshape(-1, fine_cells, feature_number).reshape(-1, feature_number)
    sharpest_scale = (line_wet_items * (fields.astype(jnp.float32) + branch_one)).astype(
        jnp.bfloat16
    )
    fine_blocks = blocks_of(sharpest_scale, place_number, patch_side_span, feature_number)
    coarse = (rough_wet_lattice * product(fine_blocks, w_down)).astype(jnp.bfloat16)
    broadened_two = widen(
        coarse.reshape(place_number, coarse_side, coarse_side * coarse_channels),
        entries,
        coarse_side,
        coarse_channels,
    )
    normed_two, scale_two = layer_norm(
        depthwise(broadened_two, kern_two, coarse_side, coarse_channels, False)
    )
    work_two = (
        normed_two.astype(jnp.bfloat16)
        .reshape(place_number, coarse_cells, coarse_channels)
        .reshape(-1, coarse_channels)
    )
    branch_work_two, hidden_two, pre_two = mlp_forward(work_two, w_in_two, w_out_two)
    branch_two = branch_work_two.reshape(-1, coarse_cells, coarse_channels).reshape(
        -1, coarse_channels
    )
    level_two = (rough_wet_lattice * (coarse.astype(jnp.float32) + branch_two)).astype(jnp.bfloat16)
    lifted_state = cells_of(product(level_two, w_up), place_number, patch_side_span, feature_number)
    prediction = (line_wet_items * (sharpest_scale.astype(jnp.float32) + lifted_state)).astype(
        jnp.bfloat16
    )
    masked_cot = (
        cotangent[0].reshape(-1, feature_number).astype(jnp.float32) * line_wet_items
    ).astype(jnp.bfloat16)
    cot_blocks = blocks_of(masked_cot, place_number, patch_side_span, feature_number)
    ascending_derivative = product(level_two.T, cot_blocks)
    change_two = (rough_wet_lattice * product(cot_blocks, w_up.T)).astype(jnp.bfloat16)
    delta_work_two = change_two.reshape(place_number, coarse_cells, coarse_channels).reshape(
        -1, coarse_channels
    )
    target_derivative_two, source_derivative_two, dnorm_work_two = mlp_backward(
        delta_work_two, work_two, hidden_two, pre_two, w_in_two, w_out_two
    )
    dnorm_two = dnorm_work_two.reshape(-1, coarse_cells, coarse_channels).reshape(
        -1, coarse_channels
    )
    reverse_step_two = norm_back(dnorm_two, normed_two, scale_two).astype(jnp.bfloat16)
    filter_derivative_two = kernel_grad(
        broadened_two, reverse_step_two.astype(jnp.float32), coarse_side, coarse_channels, extent
    )
    widened_back = widen(
        reverse_step_two.reshape(place_number, coarse_side, coarse_side * coarse_channels),
        entries,
        coarse_side,
        coarse_channels,
    )
    delta_coarse = (
        rough_wet_lattice
        * (
            change_two.astype(jnp.float32)
            + depthwise(widened_back, kern_two, coarse_side, coarse_channels, True)
        )
    ).astype(jnp.bfloat16)
    grad_down = product(fine_blocks.T, delta_coarse)
    spread = cells_of(
        product(delta_coarse, w_down.T), place_number, patch_side_span, feature_number
    )
    delta_one = (line_wet_items * (masked_cot.astype(jnp.float32) + spread)).astype(jnp.bfloat16)
    delta_work_one = delta_one.reshape(place_number, fine_cells, feature_number).reshape(
        -1, feature_number
    )
    grad_out_one, grad_in_one, dnorm_work_one = mlp_backward(
        delta_work_one, work_one, hidden_one, pre_one, w_in_one, w_out_one
    )
    dnorm_one = dnorm_work_one.reshape(-1, fine_cells, feature_number).reshape(-1, feature_number)
    back_one = norm_back(dnorm_one, normed_one, scale_one)
    grad_kern_one = kernel_grad(widened_one, back_one, patch_side_span, feature_number, extent)
    pieces = (
        grad_kern_one,
        grad_in_one,
        grad_out_one,
        grad_down,
        filter_derivative_two,
        source_derivative_two,
        target_derivative_two,
        ascending_derivative,
    )
    gradient_portion = reduce_scatter([piece.reshape(-1, piece.shape[-1]) for piece in pieces])
    return (
        prediction.reshape(1, place_number, patch_side_span, patch_side_span * feature_number),
        gradient_portion,
    )


def solution(mesh):
    mesh = Mesh(mesh.devices.reshape(8, 2, 2, 2, 4), TILES + LAT)
    return jax.shard_map(
        local,
        mesh=mesh,
        in_specs=(
            P(LAT, TILES, None, None),
            P(LAT, TILES, None),
            P(LAT, TILES),
            P(LAT, TILES, None),
            P(),
            P(),
            P(),
            P(),
            P(),
            P(),
            P(),
            P(),
            P(LAT, TILES, None, None),
        ),
        out_specs=(P(LAT, TILES, None, None), P(TILES + LAT)),
        check_vma=False,
    )
```

```python
import functools

import jax
import jax.numpy as jnp
from jax import lax
from jax.experimental import pallas as pl
from jax.experimental.pallas import tpu as pltpu
from jax.sharding import Mesh
from jax.sharding import PartitionSpec as P

TILES = ("z", "xh", "c")
LAT = ("xl", "y")
EPSILON = 1e-06
TANH_SCALE = 0.7978845608028654
CUBIC = 0.044715
LANES = 128
PIECE = 70
HELD = 72
UNIT = 3200
BLOCK = 560
C1, C2 = 200, 400
SIDE, HALF = 16, 8
F32, BF16 = jnp.float32, jnp.bfloat16
SPLIT_ROW = 5040
SPLIT = 4


def call(body, outs, scratch=(), smem=0, flops=10**8):
    def run(*args):
        vmem = pl.BlockSpec(memory_space=pltpu.VMEM)
        specs = [pl.BlockSpec(memory_space=pltpu.SMEM)] * smem + [vmem] * (len(args) - smem)
        return pl.pallas_call(
            body,
            out_shape=[jax.ShapeDtypeStruct(shape, kind) for shape, kind in outs],
            in_specs=specs,
            out_specs=[vmem] * len(outs),
            scratch_shapes=[pltpu.VMEM(shape, kind) for shape, kind in scratch],
            compiler_params=pltpu.CompilerParams(vmem_limit_bytes=52 * 2**20),
            cost_estimate=pl.CostEstimate(flops=flops, bytes_accessed=4 * 10**6, transcendentals=0),
        )(*args)

    return run


def product(left, right):
    return jnp.dot(left, right, preferred_element_type=F32)


def product_nt(left, right):
    return lax.dot_general(left, right, (((1,), (1,)), ((), ())), preferred_element_type=F32)


def product_tn(left, right):
    return lax.dot_general(left, right, (((0,), (0,)), ((), ())), preferred_element_type=F32)


def gelu_parts(values):
    square = values * values
    inner = jnp.tanh(TANH_SCALE * (values + CUBIC * square * values))
    half = 0.5 * (1.0 + inner)
    slope = half + 0.5 * values * (1.0 - inner * inner) * (TANH_SCALE * (1.0 + 3.0 * CUBIC * square))
    return values * half, slope


def lanes_of(shape):
    return lax.broadcasted_iota(jnp.int32, shape, len(shape) - 1)


def layer_norm(rows, channels):
    mean = jnp.sum(rows, axis=-1, keepdims=True) * (1.0 / channels)
    center = jnp.where(lanes_of(rows.shape) < channels, rows - mean, 0.0)
    scale = lax.rsqrt(jnp.sum(center * center, axis=-1, keepdims=True) * (1.0 / channels) + EPSILON)
    return center * scale, scale


def norm_back(grad_norm, normed, scale, channels):
    mean_grad = jnp.sum(grad_norm, axis=-1, keepdims=True) * (1.0 / channels)
    mean_cross = jnp.sum(grad_norm * normed, axis=-1, keepdims=True) * (1.0 / channels)
    return (grad_norm - mean_grad - normed * mean_cross) * scale


def choose(entries, slot, which, own, got):
    entry = entries[slot, which]
    held = jnp.maximum(entry, 0)
    place, source = held % 2, held // 2
    from_own = jnp.where((entry >= 0) & (source == 0), 1.0, 0.0)
    from_got = jnp.where((entry >= 0) & (source != 0), 1.0, 0.0)
    return own[place].astype(F32) * from_own + got[place].astype(F32) * from_got


def mask_lanes(mask, slot, filled):
    column = lax.broadcasted_iota(jnp.int32, (SIDE, SIDE * C1), 0) * C1
    lane = lanes_of((SIDE, SIDE * C1))
    spread = jnp.where((lane >= column) & (lane < column + C1), 1.0, 0.0).astype(BF16)
    own = (mask[slot].astype(F32) * jnp.where(filled > slot, 1.0, 0.0)).astype(BF16)
    return product(own, spread)


def rims_kernel(count, state, mask, west, east):
    for slot in range(2):
        masked = state[slot].astype(F32) * mask_lanes(mask, slot, count[0, 0])
        for k in range(3):
            west[slot, k] = masked[:, C1 * k : C1 * (k + 1)].astype(BF16)
            column = SIDE - 3 + k
            east[slot, k] = masked[:, C1 * column : C1 * (column + 1)].astype(BF16)


def to_blocks(values, wide, striped, lined, cat, slot):
    for t in range(25):
        striped[t] = values[:, LANES * t : LANES * (t + 1)]
    for a in range(2):
        for t in range(25):
            lined[:, LANES * t : LANES * (t + 1)] = striped[t, pl.ds(a, HALF, stride=2), :]
        for column in range(HALF):
            row = slot * 64 + column * HALF
            cat[row : row + HALF, C2 * a : C2 * (a + 1)] = lined[:, C2 * column : C2 * (column + 1)]


def before_kernel(count, state, mask, cotangent, w_up, field, mask_cat, cot_cat, change, mask_two, wide, striped, lined, held):
    field[...] = jnp.zeros(field.shape, F32)
    lane = lanes_of((SIDE, LANES))
    wide[...] = jnp.zeros(wide.shape, F32)
    for slot in range(2):
        spread = mask_lanes(mask, slot, count[0, 0])
        to_blocks(spread, wide, striped, lined, mask_cat, slot)
        to_blocks(cotangent[slot].astype(F32) * spread, wide, striped, lined, held, slot)
        wide[:, : SIDE * C1] = state[slot].astype(F32) * spread
        for column in range(SIDE):
            part = wide[:, C1 * column : C1 * column + 256]
            field[slot, 0, 3 + column, 3:19, :] = part[:, :LANES]
            field[slot, 1, 3 + column, 3:19, :] = jnp.where(lane < C1 - LANES, part[:, LANES:], 0.0)
    cot_cat[...] = held[...].astype(BF16)
    wet = mask_cat[:, 0:1]
    for k in range(1, 4):
        wet = jnp.maximum(wet, mask_cat[:, C1 * k : C1 * k + 1])
    mask_two[...] = jnp.broadcast_to(wet, (LANES, LANES))
    change[...] = (wet * product_nt(cot_cat[...], w_up[...])).astype(BF16)


def add_columns(entries, out, slot, side, channels, west, west_got, east, east_got):
    tiles = -(-channels // LANES)
    for which, start, own, got in ((0, 0, east, west_got), (1, side + 3, west, east_got)):
        value = choose(entries, slot, which, own, got)
        for t in range(tiles):
            width = min(LANES, channels - LANES * t)
            out[slot, t, start : start + 3, 3 : 3 + side, :width] = value[:, :, LANES * t : LANES * t + width]


def strips_of(out, slot, side, channels, top, bottom):
    for t in range(-(-channels // LANES)):
        width = min(LANES, channels - LANES * t)
        top[slot, :, :, LANES * t : LANES * t + width] = out[slot, t, :, 3:6, :width].astype(BF16)
        bottom[slot, :, :, LANES * t : LANES * t + width] = out[slot, t, :, side : side + 3, :width].astype(BF16)


def add_rows(entries, out, slot, side, channels, top, top_got, bottom, bottom_got):
    for which, start, own, got in ((2, 0, bottom, top_got), (3, side + 3, top, bottom_got)):
        value = choose(entries, slot, which, own, got)
        for t in range(-(-channels // LANES)):
            width = min(LANES, channels - LANES * t)
            out[slot, t, :, start : start + 3, :width] = value[:, :, LANES * t : LANES * t + width]


def strips_one_kernel(entries, field, west, west_got, east, east_got, out, top, bottom):
    out[...] = field[...]
    for slot in range(2):
        add_columns(entries, out, slot, SIDE, C1, west, west_got, east, east_got)
        strips_of(out, slot, SIDE, C1, top, bottom)


def strips_two_kernel(entries, rows, west, west_got, east, east_got, out, top, bottom):
    out[...] = jnp.zeros(out.shape, F32)
    for slot in range(2):
        for t in range(4):
            width = min(LANES, C2 - LANES * t)
            for column in range(HALF):
                start = slot * 64 + column * HALF
                out[slot, t, 3 + column, 3 : 3 + HALF, :width] = rows[start : start + HALF, LANES * t : LANES * t + width].astype(F32)
        add_columns(entries, out, slot, HALF, C2, west, west_got, east, east_got)
        strips_of(out, slot, HALF, C2, top, bottom)


def load_taps(kernel, taps, channels):
    tiles = -(-channels // LANES)
    taps[...] = jnp.zeros(taps.shape, F32)
    for t in range(tiles):
        width = min(LANES, channels - LANES * t)
        for p in range(7):
            taps[t, 7 * p : 7 * p + 7, :width] = kernel[p, :, LANES * t : LANES * t + width].astype(F32)


def conv_one(field, taps, out):
    def body(index, carry):
        slot, t = index // 2, index % 2
        for a in range(2):
            total = jnp.zeros((SIDE, HALF, LANES), F32)
            for p in range(7):
                for q in range(7):
                    window = field[slot, t, q : q + SIDE, pl.ds(a + p, HALF, stride=2), :]
                    total = total + window * taps[t, pl.ds(7 * p + q, 1), :][None]
            out[t, a, slot] = total
        return carry

    lax.fori_loop(0, 4, body, 0)


def conv_two(field, taps, out, flipped):
    def body(index, carry):
        slot, t = index // 4, index % 4
        total = jnp.zeros((HALF, HALF, LANES), F32)
        for p in range(7):
            for q in range(7):
                tap = 48 - (7 * p + q) if flipped else 7 * p + q
                total = total + field[slot, t, q : q + HALF, p : p + HALF, :] * taps[t, pl.ds(tap, 1), :][None]
        out[t, slot] = total
        return carry

    lax.fori_loop(0, 8, body, 0)


def first_kernel(entries, field, top, top_got, bottom, bottom_got, kern, w_in, w_out, w_down, mask_cat, mask_two,
                 out, normed, scales, blocks, coarse, west, east, taps, conv, held):
    out[...] = field[...]
    for slot in range(2):
        add_rows(entries, out, slot, SIDE, C1, top, top_got, bottom, bottom_got)
    load_taps(kern, taps, C1)
    conv_one(out, taps, conv)
    for a in range(2):
        for co in range(2):
            k = 2 * a + co
            rows, base = [], []
            for slot in range(2):
                for column in range(HALF):
                    place = 2 * column + co
                    rows.append(jnp.concatenate([conv[t, a, slot, place] for t in range(2)], axis=1))
                    base.append(jnp.concatenate([out[slot, t, 3 + place, pl.ds(3 + a, HALF, stride=2), :] for t in range(2)], axis=1))
            values, scale = layer_norm(jnp.concatenate(rows, axis=0), C1)
            normed[LANES * k : LANES * (k + 1), :] = values
            scales[LANES * k : LANES * (k + 1), :] = jnp.broadcast_to(scale, (LANES, LANES))
            hidden, _ = gelu_parts(product(values[:, :C1].astype(BF16), w_in[...]))
            branch = product_nt(hidden.astype(BF16), w_out[...])
            held[:, C1 * k : C1 * (k + 1)] = jnp.concatenate(base, axis=0)[:, :C1] + branch
    blocks[...] = (mask_cat[...] * held[...]).astype(BF16)
    wet = jnp.concatenate([mask_two[...]] * 4, axis=1)[:, :C2]
    rough = wet * product_nt(blocks[...], w_down[...])
    coarse[...] = rough.astype(BF16)
    send_rims(rough, west, east)


def send_rims(values, west, east):
    for slot in range(2):
        for k in range(3):
            start = slot * 64 + k * HALF
            west[slot, k] = values[start : start + HALF].astype(BF16)
            start = slot * 64 + (HALF - 3 + k) * HALF
            east[slot, k] = values[start : start + HALF].astype(BF16)


def rows_two(conv):
    return jnp.concatenate([conv[t].reshape(LANES, LANES) for t in range(4)], axis=1)


def second_kernel(entries, field, top, top_got, bottom, bottom_got, kern, w_in, w_out, coarse, change, mask_two,
                  out, normed_b, hidden, grad_pre, level, back, west, east, taps, conv):
    out[...] = field[...]
    for slot in range(2):
        add_rows(entries, out, slot, HALF, C2, top, top_got, bottom, bottom_got)
    load_taps(kern, taps, C2)
    conv_two(out, taps, conv, False)
    values, scale = layer_norm(rows_two(conv), C2)
    values = values[:, :C2]
    normed_b[...] = values.astype(BF16)
    act, slope = gelu_parts(product(normed_b[...], w_in[...]))
    hidden[...] = act.astype(BF16)
    grad_pre[...] = (product(change[...], w_out[...]) * slope).astype(BF16)
    wet = jnp.concatenate([mask_two[...]] * 4, axis=1)[:, :C2]
    level[...] = (wet * (coarse[...].astype(F32) + product_nt(hidden[...], w_out[...]))).astype(BF16)
    reverse = norm_back(product_nt(grad_pre[...], w_in[...]), values, scale, C2)
    back[...] = reverse.astype(BF16)
    send_rims(reverse, west, east)


def predict_kernel(blocks, level, w_up, mask_cat, prediction, held, lined, striped):
    held[...] = mask_cat[...] * (blocks[...].astype(F32) + product(level[...], w_up[...]))
    for slot in range(2):
        for a in range(2):
            for column in range(HALF):
                row = slot * 64 + column * HALF
                lined[:, C2 * column : C2 * (column + 1)] = held[row : row + HALF, C2 * a : C2 * (a + 1)]
            for t in range(25):
                striped[t, pl.ds(a, HALF, stride=2), :] = lined[:, LANES * t : LANES * (t + 1)]
        for t in range(25):
            prediction[slot, :, LANES * t : LANES * (t + 1)] = striped[t].astype(BF16)


def hold(held, value):
    rows, width = value.shape
    for t in range(-(-width // LANES)):
        part = value[:, LANES * t : min(width, LANES * (t + 1))]
        if part.shape[1] < LANES:
            held[t, :rows, :] = jnp.zeros((rows, LANES), F32)
        held[t, :rows, : part.shape[1]] = part


def lay_flat(flat, source, first_entry, rows, width, first_row):
    unit = UNIT // width
    count = rows // unit
    base = first_entry // LANES - first_row
    tiles = -(-width // LANES)
    lane = lax.broadcasted_iota(jnp.int32, (count, LANES), 1)
    parts = {}
    for a in range(unit):
        for t in range(tiles):
            value = source[t, pl.ds(a, count, stride=unit), :]
            place = first_entry % LANES + width * a + LANES * t
            shift = place % LANES
            if shift:
                value = pltpu.roll(value, shift, 1)
                low = jnp.where(lane >= shift, value, 0.0)
                high = jnp.where(lane < shift, value, 0.0)
                parts.setdefault(place // LANES, []).append(low)
                if not (t == tiles - 1 and shift + width - LANES * t <= LANES):
                    parts.setdefault(place // LANES + 1, []).append(high)
            else:
                parts.setdefault(place // LANES, []).append(value)
    merged = {j: functools.reduce(jnp.add, values) for j, values in parts.items()}
    for j in range(1, 25):
        flat[pl.ds(base + j, count, stride=25), :] = merged[j]
    head = merged[0]
    if 25 in merged:
        tail = merged[25]
        row = lax.broadcasted_iota(jnp.int32, (count, LANES), 0)
        before = pltpu.roll(tail, 1, 0) if count % 8 == 0 else jnp.concatenate([tail[-1:], tail[:-1]], axis=0)
        head = head + jnp.where(row > 0, before, 0.0)
    opening = flat[base : base + 1, :]
    flat[pl.ds(base, count, stride=25), :] = head
    flat[base : base + 1, :] = flat[base : base + 1, :] + opening
    if 25 in merged:
        flat[base + 25 * count : base + 25 * count + 1, :] = tail[count - 1 : count, :]
    else:
        flat[base + 25 * count : base + 25 * count + 1, :] = jnp.zeros((1, LANES), jnp.float32)


def clear_taps(held, tiles, rows):
    for t in range(tiles):
        held[t, 48:rows, :] = jnp.zeros((rows - 48, LANES), F32)


def grads_two_kernel(core, field, back, normed_b, hidden, grad_pre, level, change, cot_cat, keep, send, flat, held, sums):
    flat[0:64, :] = jnp.zeros((64, LANES), F32)
    clear_taps(held, 4, 56)
    for t in range(4):
        width = min(LANES, C2 - LANES * t)
        deltas = []
        for slot in range(2):
            delta = back[64 * slot : 64 * (slot + 1), LANES * t : LANES * t + width].astype(F32)
            if width < LANES:
                delta = jnp.concatenate([delta, jnp.zeros((64, LANES - width), F32)], axis=1)
            deltas.append(delta.reshape(HALF, HALF, LANES))
        for p in range(7):
            for q in range(7):
                total = jnp.zeros((HALF, LANES), F32)
                for slot in range(2):
                    total = total + jnp.sum(field[slot, t, q : q + HALF, p : p + HALF, :] * deltas[slot], axis=0)
                sums[7 * p + q] = total
        held[t, :49, :] = jnp.sum(sums[...], axis=1)
    lay_flat(flat, held, 649800, 56, C2, SPLIT_ROW)
    hold(held, product_tn(normed_b[...], grad_pre[...]))
    lay_flat(flat, held, 669400, C2, 4 * C2, SPLIT_ROW)
    hold(held, product_tn(hidden[...], change[...]))
    lay_flat(flat, held, 1309400, 4 * C2, C2, SPLIT_ROW)
    hold(held, product_tn(level[...], cot_cat[...]))
    lay_flat(flat, held, 1949400, C2, 4 * C1, SPLIT_ROW)
    last = 17730 - SPLIT_ROW
    flat[last:, :] = jnp.zeros((17920 + 8 - SPLIT_ROW - last, LANES), F32)
    split_out(core[0], flat, keep, send, 9, 32, SPLIT)


def split_out(core, flat, keep, send, first, stop, first_pair):
    def write(even, odd):
        if first % 2:
            even[:, :, 0] = jnp.zeros((4, 2, HELD, LANES), BF16)
        for block in range(first, stop):
            target = odd if block % 2 else even
            for xl in range(2):
                for y in range(4):
                    start = (block - first) * BLOCK + (xl * 4 + y) * PIECE
                    target[y, xl, block // 2 - first_pair] = flat[start : start + HELD, :].astype(BF16)

    @pl.when(core == 0)
    def _():
        write(keep, send)

    @pl.when(core != 0)
    def _():
        write(send, keep)


def last_kernel(core, entries, delta, top, top_got, bottom, bottom_got, kern, change, mask_two, mask_cat, cot_cat, blocks,
                w_down, w_in, w_out, normed, scales, field, keep, send,
                out, taps, conv, held_cat, rough, hidden, grad_pre, fine, back, sums, flat, held):
    out[...] = delta[...]
    for slot in range(2):
        add_rows(entries, out, slot, HALF, C2, top, top_got, bottom, bottom_got)
    load_taps(kern, taps, C2)
    conv_two(out, taps, conv, True)
    wet = jnp.concatenate([mask_two[...]] * 4, axis=1)[:, :C2]
    rough[...] = (wet * (change[...].astype(F32) + rows_two(conv)[:, :C2])).astype(BF16)
    held_cat[...] = mask_cat[...] * (cot_cat[...].astype(F32) + product(rough[...], w_down[...]))
    flat[0:8, :] = jnp.zeros((8, LANES), F32)
    for k in range(4):
        a, co = k // 2, k % 2
        rows = slice(LANES * k, LANES * (k + 1))
        fine[rows, :] = held_cat[:, C1 * k : C1 * (k + 1)].astype(BF16)
        values = normed[rows, :]
        act, slope = gelu_parts(product(values[:, :C1].astype(BF16), w_in[...]))
        hidden[rows, :] = act.astype(BF16)
        grad_pre[rows, :] = (product(fine[rows, :], w_out[...]) * slope).astype(BF16)
        grad = product_nt(grad_pre[rows, :], w_in[...])
        reverse = norm_back(grad, values[:, :C1], scales[rows, 0:1], C1)
        for slot in range(2):
            for column in range(HALF):
                start = slot * 64 + column * HALF
                part = reverse[start : start + HALF]
                back[0, a, slot, 2 * column + co] = part[:, :LANES]
                back[1, a, slot, 2 * column + co] = jnp.concatenate([part[:, LANES:], jnp.zeros((HALF, 2 * LANES - C1), F32)], axis=1)
    clear_taps(held, 2, 64)
    for t in range(2):
        sums[...] = jnp.zeros(sums.shape, F32)

        def body(index, carry):
            slot, a = index // 2, index % 2
            part = back[t, a, slot]
            for p in range(7):
                for q in range(7):
                    window = field[slot, t, q : q + SIDE, pl.ds(a + p, HALF, stride=2), :]
                    sums[7 * p + q] = sums[7 * p + q] + jnp.sum(window * part, axis=0)
            return carry

        lax.fori_loop(0, 4, body, 0)
        held[t, :49, :] = jnp.sum(sums[...], axis=1)
    lay_flat(flat, held, 0, 64, C1, 0)
    hold(held, product_tn(normed[:, :C1].astype(BF16), grad_pre[...]))
    lay_flat(flat, held, 9800, C1, 4 * C1, 0)
    hold(held, product_tn(hidden[...], fine[...]))
    lay_flat(flat, held, 169800, 4 * C1, C1, 0)
    hold(held, product_tn(blocks[...], rough[...]))
    lay_flat(flat, held, 329800, 4 * C1, C2, 0)
    flat[5077:, :] = jnp.zeros((5608 - 5077, LANES), F32)
    split_out(core[0], flat, keep, send, 0, 10, 0)


def around(array, axes, step):
    size = 1
    for axis in axes:
        size *= lax.axis_size(axis)
    return lax.ppermute(array, axes, [(i, (i + step) % size) for i in range(size)])


def wide_sum(*parts):
    total = parts[0].astype(F32)
    for part in parts[1:]:
        total = total + part.astype(F32)
    return total.astype(BF16)


def other_core(send):
    return lax.ppermute(send, "c", [(0, 1), (1, 0)])


def y_parts(total):
    me = lax.axis_index("y")
    return [lax.dynamic_index_in_dim(total, (me + k) % 4, 0, keepdims=False) for k in range(4)]


def local(ocean_state, land_mask, wet_count, neighbours, kern_one, w_in_one, w_out_one, w_down, kern_two, w_in_two, w_out_two, w_up, cotangent):
    state, cot = ocean_state[0], cotangent[0]
    w_out_one, w_down, w_out_two = w_out_one.T, w_down.T, w_out_two.T
    mask = land_mask.reshape(2, SIDE, SIDE)
    entries = neighbours[0]
    core = lax.axis_index("c").reshape(1).astype(jnp.int32)
    rims_one, rims_two = (2, 3, SIDE, C1), (2, 3, HALF, C2)
    strip_one, strip_two = (2, 22, 3, C1), (2, 14, 3, C2)
    field_one, field_two = (2, 2, 22, 24, LANES), (2, 4, 14, 16, LANES)
    cat = (LANES, 4 * C1)
    west, east = call(rims_kernel, [(rims_one, BF16)] * 2, smem=1)(wet_count, state, mask)
    west_got, east_got = around(east, TILES, 1), around(west, TILES, -1)
    field, mask_cat, cot_cat, change, mask_two = call(
        before_kernel,
        [(field_one, F32), (cat, F32), (cat, BF16), ((LANES, C2), BF16), ((LANES, LANES), F32)],
        [((SIDE, 3328), F32), ((25, SIDE, LANES), F32), ((HALF, SIDE * C1), F32), (cat, F32)],
        smem=1,
    )(wet_count, state, mask, cot, w_up)
    field, top, bottom = call(strips_one_kernel, [(field_one, F32), (strip_one, BF16), (strip_one, BF16)], smem=1)(
        entries, field, west, west_got, east, east_got
    )
    top_got, bottom_got = around(bottom, LAT, 1), around(top, LAT, -1)
    field_one_own, normed_one, scales_one, blocks, coarse, west, east = call(
        first_kernel,
        [(field_one, F32), ((512, 256), F32), ((512, LANES), F32), (cat, BF16), ((LANES, C2), BF16), (rims_two, BF16), (rims_two, BF16)],
        [((2, 49, LANES), F32), ((2, 2, 2, SIDE, HALF, LANES), F32), (cat, F32)],
        smem=1,
    )(entries, field, top, top_got, bottom, bottom_got, kern_one, w_in_one, w_out_one, w_down, mask_cat, mask_two)

    def strips_two(rows, west, west_got, east, east_got):
        return call(strips_two_kernel, [(field_two, F32), (strip_two, BF16), (strip_two, BF16)], smem=1)(
            entries, rows, west, west_got, east, east_got
        )

    two = ((LANES, 4 * C2), BF16)
    slim = ((LANES, C2), BF16)
    west_got, east_got = around(east, TILES, 1), around(west, TILES, -1)
    field_two_own, top, bottom = strips_two(coarse, west, west_got, east, east_got)
    sides = field_two_own, top, around(bottom, LAT, 1), bottom, around(top, LAT, -1)
    field_in_two, normed_two, hidden_two, grad_pre_two, level, back, west, east = call(
        second_kernel,
        [(field_two, F32), slim, two, two, slim, slim, (rims_two, BF16), (rims_two, BF16)],
        [((4, 49, LANES), F32), ((4, 2, HALF, HALF, LANES), F32)],
        smem=1,
    )(entries, *sides, kern_two, w_in_two, w_out_two, coarse, change, mask_two)
    held = ((13, 1600, LANES), F32)
    west_got, east_got = around(east, TILES, 1), around(west, TILES, -1)
    keep_two, send_two = call(
        grads_two_kernel,
        [((4, 2, 12, HELD, LANES), BF16)] * 2,
        [((17920 + 8 - SPLIT_ROW, LANES), F32), held, ((49, HALF, LANES), F32)],
        smem=1,
    )(core, field_in_two, back, normed_two, hidden_two, grad_pre_two, level, change, cot_cat)
    west_got, east_got, send_two = lax.optimization_barrier((west_got, east_got, send_two))
    got_two = other_core(send_two)
    (prediction,) = call(
        predict_kernel,
        [((2, SIDE, SIDE * C1), BF16)],
        [(cat, F32), ((HALF, SIDE * C1), F32), ((25, SIDE, LANES), F32)],
    )(blocks, level, w_up, mask_cat)
    field, top, bottom = strips_two(back, west, west_got, east, east_got)
    top_got, bottom_got = around(bottom, LAT, 1), around(top, LAT, -1)
    top_got, bottom_got, total_two = lax.optimization_barrier((top_got, bottom_got, wide_sum(keep_two, got_two)))
    parts_two = y_parts(total_two)
    field, parts_two[1:] = lax.optimization_barrier((field, parts_two[1:]))
    sums_two = [parts_two[0]] + [around(parts_two[k], ("y",), k) for k in range(1, 4)]
    sides = field, top, top_got, bottom, bottom_got
    keep_one, send_one = call(
        last_kernel,
        [((4, 2, 5, HELD, LANES), BF16)] * 2,
        [
            (field_two, F32),
            ((4, 49, LANES), F32),
            ((4, 2, HALF, HALF, LANES), F32),
            (cat, F32),
            slim,
            ((512, 4 * C1), BF16),
            ((512, 4 * C1), BF16),
            ((512, C1), BF16),
            ((2, 2, 2, SIDE, HALF, LANES), F32),
            ((49, HALF, LANES), F32),
            ((5608, LANES), F32),
            ((7, 800, LANES), F32),
        ],
        smem=2,
    )(core, entries, *sides, kern_two, change, mask_two, mask_cat, cot_cat, blocks, w_down, w_in_one, w_out_one, normed_one, scales_one, field_one_own)
    return prediction[None], finish(keep_one, send_one, sums_two)


def finish(keep_one, send_one, sums_two):
    total_one = wide_sum(keep_one, other_core(send_one))
    total_one = lax.all_to_all(total_one, "y", 0, 0)
    first = wide_sum(*[total_one[k, :, :SPLIT] for k in range(4)])
    shared = wide_sum(*[total_one[k, :, SPLIT:] for k in range(4)], *[part[:, :1] for part in sums_two])
    second = wide_sum(*[part[:, 1:] for part in sums_two])
    total = jnp.concatenate([first, shared, second], axis=1).reshape(2, 8, 2, HELD, LANES)
    total = total.transpose(1, 2, 0, 3, 4).reshape(32, HELD, LANES)
    total = lax.all_to_all(total, ("z", "xh", "xl"), 0, 0)
    return total.astype(F32).sum(axis=0)[:PIECE].reshape(-1)


def solution(mesh):
    mesh = Mesh(mesh.devices.reshape(8, 2, 2, 2, 4), TILES + LAT)
    return jax.shard_map(
        local,
        mesh=mesh,
        in_specs=(
            P(LAT, TILES, None, None),
            P(LAT, TILES, None),
            P(LAT, TILES),
            P(LAT, TILES, None),
            P(),
            P(),
            P(),
            P(),
            P(),
            P(),
            P(),
            P(),
            P(LAT, TILES, None, None),
        ),
        out_specs=(P(LAT, TILES, None, None), P(TILES + LAT)),
        check_vma=False,
    )
```

```python
import functools

import jax
import jax.numpy as jnp
from jax import lax
from jax.experimental import pallas as pl
from jax.experimental.pallas import tpu as pltpu
from jax.sharding import Mesh
from jax.sharding import PartitionSpec as P

TILES = ("z", "xh", "c")
LAT = ("xl", "y")
EPSILON = 1e-06
TANH_SCALE = 0.7978845608028654
CUBIC = 0.044715
LANES = 128
PIECE = 70
HELD = 72
UNIT = 3200
BLOCK = 560
C1, C2 = 200, 400
SIDE, HALF = 16, 8
F32, BF16 = jnp.float32, jnp.bfloat16
SPLIT_ROW = 5040
SPLIT = 4


def call(body, outs, scratch=(), smem=0, room=16, us=1):
    def run(*args):
        vmem = pl.BlockSpec(memory_space=pltpu.VMEM)
        specs = [pl.BlockSpec(memory_space=pltpu.SMEM)] * smem + [vmem] * (len(args) - smem)
        return pl.pallas_call(
            body,
            out_shape=[jax.ShapeDtypeStruct(shape, kind) for shape, kind in outs],
            in_specs=specs,
            out_specs=[vmem] * len(outs),
            scratch_shapes=[pltpu.VMEM(shape, kind) for shape, kind in scratch],
            compiler_params=pltpu.CompilerParams(vmem_limit_bytes=room * 2**20),
            cost_estimate=pl.CostEstimate(flops=us * 10**9, bytes_accessed=10**6, transcendentals=0),
        )(*args)

    return run


def product(left, right):
    return jnp.dot(left, right, preferred_element_type=F32)


def product_nt(left, right):
    return lax.dot_general(left, right, (((1,), (1,)), ((), ())), preferred_element_type=F32)


def product_tn(left, right):
    return lax.dot_general(left, right, (((0,), (0,)), ((), ())), preferred_element_type=F32)


def gelu_parts(values):
    square = values * values
    inner = jnp.tanh(TANH_SCALE * (values + CUBIC * square * values))
    half = 0.5 * (1.0 + inner)
    slope = half + 0.5 * values * (1.0 - inner * inner) * (TANH_SCALE * (1.0 + 3.0 * CUBIC * square))
    return values * half, slope


def lanes_of(shape):
    return lax.broadcasted_iota(jnp.int32, shape, len(shape) - 1)


def layer_norm(rows, channels):
    mean = jnp.sum(rows, axis=-1, keepdims=True) * (1.0 / channels)
    center = jnp.where(lanes_of(rows.shape) < channels, rows - mean, 0.0)
    scale = lax.rsqrt(jnp.sum(center * center, axis=-1, keepdims=True) * (1.0 / channels) + EPSILON)
    return center * scale, scale


def norm_back(grad_norm, normed, scale, channels):
    mean_grad = jnp.sum(grad_norm, axis=-1, keepdims=True) * (1.0 / channels)
    mean_cross = jnp.sum(grad_norm * normed, axis=-1, keepdims=True) * (1.0 / channels)
    return (grad_norm - mean_grad - normed * mean_cross) * scale


def choose(entries, slot, which, own, got):
    entry = entries[slot, which]
    held = jnp.maximum(entry, 0)
    place, source = held % 2, held // 2
    from_own = jnp.where((entry >= 0) & (source == 0), 1.0, 0.0)
    from_got = jnp.where((entry >= 0) & (source != 0), 1.0, 0.0)
    return own[place].astype(F32) * from_own + got[place].astype(F32) * from_got


def mask_lanes(mask, slot, filled):
    column = lax.broadcasted_iota(jnp.int32, (SIDE, SIDE * C1), 0) * C1
    lane = lanes_of((SIDE, SIDE * C1))
    spread = jnp.where((lane >= column) & (lane < column + C1), 1.0, 0.0).astype(BF16)
    own = (mask[slot].astype(F32) * jnp.where(filled > slot, 1.0, 0.0)).astype(BF16)
    return product(own, spread)


def rims_kernel(count, state, mask, west, east):
    for slot in range(2):
        masked = state[slot].astype(F32) * mask_lanes(mask, slot, count[0, 0])
        for k in range(3):
            west[slot, k] = masked[:, C1 * k : C1 * (k + 1)].astype(BF16)
            column = SIDE - 3 + k
            east[slot, k] = masked[:, C1 * column : C1 * (column + 1)].astype(BF16)


def to_blocks(values, wide, striped, lined, cat, slot):
    for t in range(25):
        striped[t] = values[:, LANES * t : LANES * (t + 1)]
    for a in range(2):
        for t in range(25):
            lined[:, LANES * t : LANES * (t + 1)] = striped[t, pl.ds(a, HALF, stride=2), :]
        for column in range(HALF):
            row = slot * 64 + column * HALF
            cat[row : row + HALF, C2 * a : C2 * (a + 1)] = lined[:, C2 * column : C2 * (column + 1)]


def before_kernel(count, state, mask, cotangent, w_up, field, mask_cat, cot_cat, change, mask_two, wide, striped, lined, held):
    field[...] = jnp.zeros(field.shape, F32)
    lane = lanes_of((SIDE, LANES))
    wide[...] = jnp.zeros(wide.shape, F32)
    for slot in range(2):
        spread = mask_lanes(mask, slot, count[0, 0])
        to_blocks(spread, wide, striped, lined, mask_cat, slot)
        to_blocks(cotangent[slot].astype(F32) * spread, wide, striped, lined, held, slot)
        wide[:, : SIDE * C1] = state[slot].astype(F32) * spread
        for column in range(SIDE):
            part = wide[:, C1 * column : C1 * column + 256]
            field[slot, 0, 3 + column, 3:19, :] = part[:, :LANES]
            field[slot, 1, 3 + column, 3:19, :] = jnp.where(lane < C1 - LANES, part[:, LANES:], 0.0)
    cot_cat[...] = held[...].astype(BF16)
    wet = mask_cat[:, 0:1]
    for k in range(1, 4):
        wet = jnp.maximum(wet, mask_cat[:, C1 * k : C1 * k + 1])
    mask_two[...] = jnp.broadcast_to(wet, (LANES, LANES))
    change[...] = (wet * product_nt(cot_cat[...], w_up[...])).astype(BF16)


def add_columns(entries, out, slot, side, channels, west, west_got, east, east_got):
    tiles = -(-channels // LANES)
    for which, start, own, got in ((0, 0, east, west_got), (1, side + 3, west, east_got)):
        value = choose(entries, slot, which, own, got)
        for t in range(tiles):
            width = min(LANES, channels - LANES * t)
            out[slot, t, start : start + 3, 3 : 3 + side, :width] = value[:, :, LANES * t : LANES * t + width]


def strips_of(out, slot, side, channels, top, bottom):
    for t in range(-(-channels // LANES)):
        width = min(LANES, channels - LANES * t)
        top[slot, :, :, LANES * t : LANES * t + width] = out[slot, t, :, 3:6, :width].astype(BF16)
        bottom[slot, :, :, LANES * t : LANES * t + width] = out[slot, t, :, side : side + 3, :width].astype(BF16)


def add_rows(entries, out, slot, side, channels, top, top_got, bottom, bottom_got):
    for which, start, own, got in ((2, 0, bottom, top_got), (3, side + 3, top, bottom_got)):
        value = choose(entries, slot, which, own, got)
        for t in range(-(-channels // LANES)):
            width = min(LANES, channels - LANES * t)
            out[slot, t, :, start : start + 3, :width] = value[:, :, LANES * t : LANES * t + width]


def strips_one_kernel(entries, field, west, west_got, east, east_got, out, top, bottom):
    out[...] = field[...]
    for slot in range(2):
        add_columns(entries, out, slot, SIDE, C1, west, west_got, east, east_got)
        strips_of(out, slot, SIDE, C1, top, bottom)


def strips_two_kernel(entries, rows, west, west_got, east, east_got, out, top, bottom):
    out[...] = jnp.zeros(out.shape, F32)
    for slot in range(2):
        for t in range(4):
            width = min(LANES, C2 - LANES * t)
            for column in range(HALF):
                start = slot * 64 + column * HALF
                out[slot, t, 3 + column, 3 : 3 + HALF, :width] = rows[start : start + HALF, LANES * t : LANES * t + width].astype(F32)
        add_columns(entries, out, slot, HALF, C2, west, west_got, east, east_got)
        strips_of(out, slot, HALF, C2, top, bottom)


def load_taps(kernel, taps, channels):
    tiles = -(-channels // LANES)
    taps[...] = jnp.zeros(taps.shape, F32)
    for t in range(tiles):
        width = min(LANES, channels - LANES * t)
        for p in range(7):
            taps[t, 7 * p : 7 * p + 7, :width] = kernel[p, :, LANES * t : LANES * t + width].astype(F32)


def conv_one(field, taps, out):
    def body(index, carry):
        slot, t = index // 2, index % 2
        for a in range(2):
            total = jnp.zeros((SIDE, HALF, LANES), F32)
            for p in range(7):
                for q in range(7):
                    window = field[slot, t, q : q + SIDE, pl.ds(a + p, HALF, stride=2), :]
                    total = total + window * taps[t, pl.ds(7 * p + q, 1), :][None]
            out[t, a, slot] = total
        return carry

    lax.fori_loop(0, 4, body, 0)


def conv_two(field, taps, out, flipped):
    def body(index, carry):
        slot, t = index // 4, index % 4
        total = jnp.zeros((HALF, HALF, LANES), F32)
        for p in range(7):
            for q in range(7):
                tap = 48 - (7 * p + q) if flipped else 7 * p + q
                total = total + field[slot, t, q : q + HALF, p : p + HALF, :] * taps[t, pl.ds(tap, 1), :][None]
        out[t, slot] = total
        return carry

    lax.fori_loop(0, 8, body, 0)


def first_kernel(entries, field, top, top_got, bottom, bottom_got, kern, w_in, w_out, w_down, mask_cat, mask_two,
                 out, normed, scales, blocks, coarse, west, east, taps, conv, held):
    out[...] = field[...]
    for slot in range(2):
        add_rows(entries, out, slot, SIDE, C1, top, top_got, bottom, bottom_got)
    load_taps(kern, taps, C1)
    conv_one(out, taps, conv)
    for a in range(2):
        for co in range(2):
            k = 2 * a + co
            rows, base = [], []
            for slot in range(2):
                for column in range(HALF):
                    place = 2 * column + co
                    rows.append(jnp.concatenate([conv[t, a, slot, place] for t in range(2)], axis=1))
                    base.append(jnp.concatenate([out[slot, t, 3 + place, pl.ds(3 + a, HALF, stride=2), :] for t in range(2)], axis=1))
            values, scale = layer_norm(jnp.concatenate(rows, axis=0), C1)
            normed[LANES * k : LANES * (k + 1), :] = values
            scales[LANES * k : LANES * (k + 1), :] = jnp.broadcast_to(scale, (LANES, LANES))
            hidden, _ = gelu_parts(product(values[:, :C1].astype(BF16), w_in[...]))
            branch = product_nt(hidden.astype(BF16), w_out[...])
            held[:, C1 * k : C1 * (k + 1)] = jnp.concatenate(base, axis=0)[:, :C1] + branch
    blocks[...] = (mask_cat[...] * held[...]).astype(BF16)
    wet = jnp.concatenate([mask_two[...]] * 4, axis=1)[:, :C2]
    rough = wet * product_nt(blocks[...], w_down[...])
    coarse[...] = rough.astype(BF16)
    send_rims(rough, west, east)


def send_rims(values, west, east):
    for slot in range(2):
        for k in range(3):
            start = slot * 64 + k * HALF
            west[slot, k] = values[start : start + HALF].astype(BF16)
            start = slot * 64 + (HALF - 3 + k) * HALF
            east[slot, k] = values[start : start + HALF].astype(BF16)


def rows_two(conv):
    return jnp.concatenate([conv[t].reshape(LANES, LANES) for t in range(4)], axis=1)


def second_kernel(entries, field, top, top_got, bottom, bottom_got, kern, w_in, w_out, coarse, change, mask_two,
                  out, normed_b, hidden, grad_pre, level, back, west, east, taps, conv):
    out[...] = field[...]
    for slot in range(2):
        add_rows(entries, out, slot, HALF, C2, top, top_got, bottom, bottom_got)
    load_taps(kern, taps, C2)
    conv_two(out, taps, conv, False)
    values, scale = layer_norm(rows_two(conv), C2)
    values = values[:, :C2]
    normed_b[...] = values.astype(BF16)
    act, slope = gelu_parts(product(normed_b[...], w_in[...]))
    hidden[...] = act.astype(BF16)
    grad_pre[...] = (product(change[...], w_out[...]) * slope).astype(BF16)
    wet = jnp.concatenate([mask_two[...]] * 4, axis=1)[:, :C2]
    level[...] = (wet * (coarse[...].astype(F32) + product_nt(hidden[...], w_out[...]))).astype(BF16)
    reverse = norm_back(product_nt(grad_pre[...], w_in[...]), values, scale, C2)
    back[...] = reverse.astype(BF16)
    send_rims(reverse, west, east)


def predict_kernel(blocks, level, w_up, mask_cat, prediction, held, lined, striped):
    held[...] = mask_cat[...] * (blocks[...].astype(F32) + product(level[...], w_up[...]))
    for slot in range(2):
        for a in range(2):
            for column in range(HALF):
                row = slot * 64 + column * HALF
                lined[:, C2 * column : C2 * (column + 1)] = held[row : row + HALF, C2 * a : C2 * (a + 1)]
            for t in range(25):
                striped[t, pl.ds(a, HALF, stride=2), :] = lined[:, LANES * t : LANES * (t + 1)]
        for t in range(25):
            prediction[slot, :, LANES * t : LANES * (t + 1)] = striped[t].astype(BF16)


def hold(held, value):
    rows, width = value.shape
    for t in range(-(-width // LANES)):
        part = value[:, LANES * t : min(width, LANES * (t + 1))]
        if part.shape[1] < LANES:
            held[t, :rows, :] = jnp.zeros((rows, LANES), F32)
        held[t, :rows, : part.shape[1]] = part


def lay_flat(flat, source, first_entry, rows, width, first_row):
    unit = UNIT // width
    count = rows // unit
    base = first_entry // LANES - first_row
    tiles = -(-width // LANES)
    lane = lax.broadcasted_iota(jnp.int32, (count, LANES), 1)
    parts = {}
    for a in range(unit):
        for t in range(tiles):
            value = source[t, pl.ds(a, count, stride=unit), :]
            place = first_entry % LANES + width * a + LANES * t
            shift = place % LANES
            if shift:
                value = pltpu.roll(value, shift, 1)
                low = jnp.where(lane >= shift, value, 0.0)
                high = jnp.where(lane < shift, value, 0.0)
                parts.setdefault(place // LANES, []).append(low)
                if not (t == tiles - 1 and shift + width - LANES * t <= LANES):
                    parts.setdefault(place // LANES + 1, []).append(high)
            else:
                parts.setdefault(place // LANES, []).append(value)
    merged = {j: functools.reduce(jnp.add, values) for j, values in parts.items()}
    for j in range(1, 25):
        flat[pl.ds(base + j, count, stride=25), :] = merged[j]
    head = merged[0]
    if 25 in merged:
        tail = merged[25]
        row = lax.broadcasted_iota(jnp.int32, (count, LANES), 0)
        before = pltpu.roll(tail, 1, 0) if count % 8 == 0 else jnp.concatenate([tail[-1:], tail[:-1]], axis=0)
        head = head + jnp.where(row > 0, before, 0.0)
    opening = flat[base : base + 1, :]
    flat[pl.ds(base, count, stride=25), :] = head
    flat[base : base + 1, :] = flat[base : base + 1, :] + opening
    if 25 in merged:
        flat[base + 25 * count : base + 25 * count + 1, :] = tail[count - 1 : count, :]
    else:
        flat[base + 25 * count : base + 25 * count + 1, :] = jnp.zeros((1, LANES), jnp.float32)


def clear_taps(held, tiles, rows):
    for t in range(tiles):
        held[t, 48:rows, :] = jnp.zeros((rows - 48, LANES), F32)


def grads_two_kernel(field, back, normed_b, hidden, grad_pre, level, change, cot_cat, keep, send, flat, held, tall, sums):
    flat[0:64, :] = jnp.zeros((64, LANES), F32)
    clear_taps(held, 4, 56)
    for t in range(4):
        width = min(LANES, C2 - LANES * t)
        deltas = []
        for slot in range(2):
            delta = back[64 * slot : 64 * (slot + 1), LANES * t : LANES * t + width].astype(F32)
            if width < LANES:
                delta = jnp.concatenate([delta, jnp.zeros((64, LANES - width), F32)], axis=1)
            deltas.append(delta.reshape(HALF, HALF, LANES))
        for p in range(7):
            for q in range(7):
                total = jnp.zeros((HALF, LANES), F32)
                for slot in range(2):
                    total = total + jnp.sum(field[slot, t, q : q + HALF, p : p + HALF, :] * deltas[slot], axis=0)
                sums[7 * p + q] = total
        held[t, :49, :] = jnp.sum(sums[...], axis=1)
    lay_flat(flat, held, 649800, 56, C2, SPLIT_ROW)
    hold(held, product_tn(normed_b[...], grad_pre[...]))
    lay_flat(flat, held, 669400, C2, 4 * C2, SPLIT_ROW)
    hold(tall, product_tn(hidden[...], change[...]))
    lay_flat(flat, tall, 1309400, 4 * C2, C2, SPLIT_ROW)
    hold(held, product_tn(level[...], cot_cat[...]))
    lay_flat(flat, held, 1949400, C2, 4 * C1, SPLIT_ROW)
    last = 17730 - SPLIT_ROW
    flat[last:, :] = jnp.zeros((17920 + 8 - SPLIT_ROW - last, LANES), F32)
    keep[:8, 0] = jnp.zeros((8, HELD, LANES), BF16)
    send[:8, 0] = jnp.zeros((8, HELD, LANES), BF16)
    split_out(lax.axis_index("c"), flat, keep, send, 9, 32, store_two)


def split_out(core, flat, keep, send, first, stop, store):
    def write(even, odd):
        for block in range(first, stop):
            target = odd if block % 2 else even
            for xl in range(2):
                for y in range(4):
                    start = (block - first) * BLOCK + (xl * 4 + y) * PIECE
                    store(target, block // 4, block // 2 % 2, xl, y, flat[start : start + HELD, :].astype(BF16))

    @pl.when(core == 0)
    def _():
        write(keep, send)

    @pl.when(core != 0)
    def _():
        write(send, keep)


def store_two(target, z, xh, xl, y, value):
    target[8 * xh + 4 * xl + y, z - 2] = value


def store_one(target, z, xh, xl, y, value):
    target[8 * xh + 4 * xl + y, z] = value


def last_kernel(entries, delta, top, top_got, bottom, bottom_got, kern, change, mask_two, mask_cat, cot_cat, blocks,
                w_down, w_in, w_out, normed, scales, field, keep, send,
                out, taps, conv, held_cat, rough, hidden, grad_pre, fine, back, sums, flat, held):
    out[...] = delta[...]
    for slot in range(2):
        add_rows(entries, out, slot, HALF, C2, top, top_got, bottom, bottom_got)
    load_taps(kern, taps, C2)
    conv_two(out, taps, conv, True)
    wet = jnp.concatenate([mask_two[...]] * 4, axis=1)[:, :C2]
    rough[...] = (wet * (change[...].astype(F32) + rows_two(conv)[:, :C2])).astype(BF16)
    held_cat[...] = mask_cat[...] * (cot_cat[...].astype(F32) + product(rough[...], w_down[...]))
    flat[0:8, :] = jnp.zeros((8, LANES), F32)
    for k in range(4):
        a, co = k // 2, k % 2
        rows = slice(LANES * k, LANES * (k + 1))
        fine[rows, :] = held_cat[:, C1 * k : C1 * (k + 1)].astype(BF16)
        values = normed[rows, :]
        act, slope = gelu_parts(product(values[:, :C1].astype(BF16), w_in[...]))
        hidden[rows, :] = act.astype(BF16)
        grad_pre[rows, :] = (product(fine[rows, :], w_out[...]) * slope).astype(BF16)
        grad = product_nt(grad_pre[rows, :], w_in[...])
        reverse = norm_back(grad, values[:, :C1], scales[rows, 0:1], C1)
        for slot in range(2):
            for column in range(HALF):
                start = slot * 64 + column * HALF
                part = reverse[start : start + HALF]
                back[0, a, slot, 2 * column + co] = part[:, :LANES]
                back[1, a, slot, 2 * column + co] = jnp.concatenate([part[:, LANES:], jnp.zeros((HALF, 2 * LANES - C1), F32)], axis=1)
    clear_taps(held, 2, 64)
    for t in range(2):
        sums[...] = jnp.zeros(sums.shape, F32)

        def body(index, carry):
            slot, a = index // 2, index % 2
            part = back[t, a, slot]
            for p in range(7):
                for q in range(7):
                    window = field[slot, t, q : q + SIDE, pl.ds(a + p, HALF, stride=2), :]
                    sums[7 * p + q] = sums[7 * p + q] + jnp.sum(window * part, axis=0)
            return carry

        lax.fori_loop(0, 4, body, 0)
        held[t, :49, :] = jnp.sum(sums[...], axis=1)
    lay_flat(flat, held, 0, 64, C1, 0)
    hold(held, product_tn(normed[:, :C1].astype(BF16), grad_pre[...]))
    lay_flat(flat, held, 9800, C1, 4 * C1, 0)
    hold(held, product_tn(hidden[...], fine[...]))
    lay_flat(flat, held, 169800, 4 * C1, C1, 0)
    hold(held, product_tn(blocks[...], rough[...]))
    lay_flat(flat, held, 329800, 4 * C1, C2, 0)
    flat[5077:, :] = jnp.zeros((5608 - 5077, LANES), F32)
    keep[8:, 2] = jnp.zeros((8, HELD, LANES), BF16)
    send[8:, 2] = jnp.zeros((8, HELD, LANES), BF16)
    split_out(lax.axis_index("c"), flat, keep, send, 0, 10, store_one)


def around(array, axes, step):
    size = 1
    for axis in axes:
        size *= lax.axis_size(axis)
    return lax.ppermute(array, axes, [(i, (i + step) % size) for i in range(size)])


def wide_sum(*parts):
    total = parts[0].astype(F32)
    for part in parts[1:]:
        total = total + part.astype(F32)
    return total.astype(BF16)


def other_core(send):
    return lax.ppermute(send, "c", [(0, 1), (1, 0)])


def parts_kernel(first, second, keep, got, *parts):
    y, x = lax.axis_index("y"), 2 * lax.axis_index("xh") + lax.axis_index("xl")

    def total(place, z):
        return (keep[place, z].astype(F32) + got[place, z].astype(F32)).astype(BF16)

    for k in range(4):
        for other in range(4):
            for i, z in enumerate(first):
                parts[k][other, i] = total(4 * other + (y + k) % 4, z)
            for i, z in enumerate(second):
                parts[4 + k][other, i] = total(4 * (x ^ k) + other, z)


def exchange(parts):
    moved = {}
    for k in (1, 3, 2):
        moved[k] = around(parts[k], ("y",), k)
        moved[4 + k] = lax.ppermute(parts[4 + k], ("xh", "xl"), [(i, i ^ k) for i in range(4)])
    return [moved.get(k, parts[k]) for k in range(8)]


def cross_kernel(*refs):
    two, one, outs = refs[:8], refs[8:16], refs[16:]
    y, x = lax.axis_index("y"), 2 * lax.axis_index("xh") + lax.axis_index("xl")

    def total(terms):
        result = terms[0].astype(F32)
        for term in terms[1:]:
            result = result + term.astype(F32)
        return result.astype(BF16)

    for k in range(4):
        place = x ^ k
        outs[k][0] = total([one[j][place, 0] for j in range(4)])
        outs[k][1] = total([one[j][place, 1] for j in range(4)] + [two[j][place, 0] for j in range(4)])
        outs[k][2] = total([two[j][place, 1] for j in range(4)])
        outs[k][3] = total([two[j][place, 2] for j in range(4)])
        place = (y + k) % 4
        outs[4 + k][0] = total([one[4 + j][place, 0] for j in range(4)])
        for i in range(3):
            outs[4 + k][1 + i] = total([two[4 + j][place, i] for j in range(4)])


def cross(parts):
    moved = {}
    for k in (1, 3, 2):
        moved[k] = lax.ppermute(parts[k], ("xh", "xl"), [(i, i ^ k) for i in range(4)])
        moved[4 + k] = around(parts[4 + k], ("y",), k)
    return [moved.get(k, parts[k]) for k in range(8)]


def merge_kernel(*refs):
    parts, out = refs[:8], refs[8]
    for base, held in ((0, (0, 2, 3, 4)), (4, (1, 5, 6, 7))):
        for i, z in enumerate(held):
            total = parts[base][i].astype(F32)
            for k in range(1, 4):
                total = total + parts[base + k][i].astype(F32)
            out[z] = total.astype(BF16)


def final_kernel(parts, out):
    total = parts[0].astype(F32)
    for k in range(1, parts.shape[0]):
        total = total + parts[k].astype(F32)
    out[...] = total


def local(ocean_state, land_mask, wet_count, neighbours, kern_one, w_in_one, w_out_one, w_down, kern_two, w_in_two, w_out_two, w_up, cotangent):
    state, cot = ocean_state[0], cotangent[0]
    w_out_one, w_down, w_out_two = w_out_one.T, w_down.T, w_out_two.T
    mask = land_mask.reshape(2, SIDE, SIDE)
    entries = neighbours[0]
    rims_one, rims_two = (2, 3, SIDE, C1), (2, 3, HALF, C2)
    strip_one, strip_two = (2, 22, 3, C1), (2, 14, 3, C2)
    field_one, field_two = (2, 2, 22, 24, LANES), (2, 4, 14, 16, LANES)
    cat = (LANES, 4 * C1)
    west, east = call(rims_kernel, [(rims_one, BF16)] * 2, smem=1)(wet_count, state, mask)
    west_got, east_got = around(east, TILES, 1), around(west, TILES, -1)
    field, mask_cat, cot_cat, change, mask_two = call(
        before_kernel,
        [(field_one, F32), (cat, F32), (cat, BF16), ((LANES, C2), BF16), ((LANES, LANES), F32)],
        [((SIDE, 3328), F32), ((25, SIDE, LANES), F32), ((HALF, SIDE * C1), F32), (cat, F32)],
        room=16, us=2, smem=1,
    )(wet_count, state, mask, cot, w_up)
    field, top, bottom = call(strips_one_kernel, [(field_one, F32), (strip_one, BF16), (strip_one, BF16)], smem=1)(
        entries, field, west, west_got, east, east_got
    )
    top_got, bottom_got = around(bottom, LAT, 1), around(top, LAT, -1)
    field_one_own, normed_one, scales_one, blocks, coarse, west, east = call(
        first_kernel,
        [(field_one, F32), ((512, 256), F32), ((512, LANES), F32), (cat, BF16), ((LANES, C2), BF16), (rims_two, BF16), (rims_two, BF16)],
        [((2, 49, LANES), F32), ((2, 2, 2, SIDE, HALF, LANES), F32), (cat, F32)],
        room=16, us=6, smem=1,
    )(entries, field, top, top_got, bottom, bottom_got, kern_one, w_in_one, w_out_one, w_down, mask_cat, mask_two)

    def strips_two(rows, west, west_got, east, east_got):
        return call(strips_two_kernel, [(field_two, F32), (strip_two, BF16), (strip_two, BF16)], smem=1)(
            entries, rows, west, west_got, east, east_got
        )

    two = ((LANES, 4 * C2), BF16)
    slim = ((LANES, C2), BF16)
    west_got, east_got = around(east, TILES, 1), around(west, TILES, -1)
    field_two_own, top, bottom = strips_two(coarse, west, west_got, east, east_got)
    sides = field_two_own, top, around(bottom, LAT, 1), bottom, around(top, LAT, -1)
    field_in_two, normed_two, hidden_two, grad_pre_two, level, back, west, east = call(
        second_kernel,
        [(field_two, F32), slim, two, two, slim, slim, (rims_two, BF16), (rims_two, BF16)],
        [((4, 49, LANES), F32), ((4, 2, HALF, HALF, LANES), F32)],
        room=16, us=6, smem=1,
    )(entries, *sides, kern_two, w_in_two, w_out_two, coarse, change, mask_two)
    west_got, east_got = around(east, TILES, 1), around(west, TILES, -1)
    keep_two, send_two = call(
        grads_two_kernel,
        [((16, 6, HELD, LANES), BF16)] * 2,
        [((17920 + 8 - SPLIT_ROW, LANES), F32), ((13, C2, LANES), F32), ((4, 4 * C2, LANES), F32), ((49, HALF, LANES), F32)],
        room=16, us=7,
    )(field_in_two, back, normed_two, hidden_two, grad_pre_two, level, change, cot_cat)
    west_got, east_got, send_two = lax.optimization_barrier((west_got, east_got, send_two))
    got_two = other_core(send_two)
    (prediction,) = call(
        predict_kernel,
        [((2, SIDE, SIDE * C1), BF16)],
        [(cat, F32), ((HALF, SIDE * C1), F32), ((25, SIDE, LANES), F32)],
    )(blocks, level, w_up, mask_cat)
    field, top, bottom = strips_two(back, west, west_got, east, east_got)
    top_got, bottom_got = around(bottom, LAT, 1), around(top, LAT, -1)
    parts = call(
        functools.partial(parts_kernel, (0, 1, 2), (3, 4, 5)), [((4, 3, HELD, LANES), BF16)] * 8, us=1
    )(keep_two, got_two)
    top_got, bottom_got, *parts = lax.optimization_barrier((top_got, bottom_got, *parts))
    parts_two = exchange(parts)
    sides = field, top, top_got, bottom, bottom_got
    keep_one, send_one = call(
        last_kernel,
        [((16, 3, HELD, LANES), BF16)] * 2,
        [
            (field_two, F32),
            ((4, 49, LANES), F32),
            ((4, 2, HALF, HALF, LANES), F32),
            (cat, F32),
            slim,
            ((512, 4 * C1), BF16),
            ((512, 4 * C1), BF16),
            ((512, C1), BF16),
            ((2, 2, 2, SIDE, HALF, LANES), F32),
            ((49, HALF, LANES), F32),
            ((5608, LANES), F32),
            ((7, 800, LANES), F32),
        ],
        room=16, us=10, smem=1,
    )(entries, *sides, kern_two, change, mask_two, mask_cat, cot_cat, blocks, w_down, w_in_one, w_out_one, normed_one, scales_one, field_one_own)
    send_one, *parts_two = lax.optimization_barrier((send_one, *parts_two))
    return prediction[None], finish(keep_one, send_one, parts_two)


def finish(keep_one, send_one, parts_two):
    parts = call(
        functools.partial(parts_kernel, (0, 2), (1,)),
        [((4, 2, HELD, LANES), BF16)] * 4 + [((4, 1, HELD, LANES), BF16)] * 4,
    )(keep_one, other_core(send_one))
    parts_one = exchange(parts)
    parts = call(cross_kernel, [((4, HELD, LANES), BF16)] * 8)(*parts_two, *parts_one)
    (total,) = call(merge_kernel, [((8, HELD, LANES), BF16)])(*cross(parts))
    total = lax.all_to_all(total, "z", 0, 0)
    (total,) = call(final_kernel, [((HELD, LANES), F32)])(total)
    return total[:PIECE].reshape(-1)


def solution(mesh):
    mesh = Mesh(mesh.devices.reshape(8, 2, 2, 2, 4), TILES + LAT)
    return jax.shard_map(
        local,
        mesh=mesh,
        in_specs=(
            P(LAT, TILES, None, None),
            P(LAT, TILES, None),
            P(LAT, TILES),
            P(LAT, TILES, None),
            P(),
            P(),
            P(),
            P(),
            P(),
            P(),
            P(),
            P(),
            P(LAT, TILES, None, None),
        ),
        out_specs=(P(LAT, TILES, None, None), P(TILES + LAT)),
        check_vma=False,
    )
```

```python
import functools

import jax
import jax.numpy as jnp
from jax import lax
from jax.experimental import pallas as pl
from jax.experimental.pallas import tpu as pltpu
from jax.sharding import Mesh
from jax.sharding import PartitionSpec as P

TILES = ("z", "xh", "c")
LAT = ("xl", "y")
EPSILON = 1e-06
TANH_SCALE = 0.7978845608028654
CUBIC = 0.044715
LANES = 128
PIECE = 70
HELD = 72
UNIT = 3200
BLOCK = 560
C1, C2 = 200, 400
SIDE, HALF = 16, 8
F32, BF16 = jnp.float32, jnp.bfloat16
SPLIT_ROW = 5040
SPLIT = 4


def call(body, outs, scratch=(), smem=0, room=16, us=1):
    def run(*args):
        vmem = pl.BlockSpec(memory_space=pltpu.VMEM)
        specs = [pl.BlockSpec(memory_space=pltpu.SMEM)] * smem + [vmem] * (len(args) - smem)
        return pl.pallas_call(
            body,
            out_shape=[jax.ShapeDtypeStruct(shape, kind) for shape, kind in outs],
            in_specs=specs,
            out_specs=[vmem] * len(outs),
            scratch_shapes=[pltpu.VMEM(shape, kind) for shape, kind in scratch],
            compiler_params=pltpu.CompilerParams(vmem_limit_bytes=room * 2**20),
            cost_estimate=pl.CostEstimate(flops=us * 10**9, bytes_accessed=10**6, transcendentals=0),
        )(*args)

    return run


def product(left, right):
    return jnp.dot(left, right, preferred_element_type=F32)


def product_nt(left, right):
    return lax.dot_general(left, right, (((1,), (1,)), ((), ())), preferred_element_type=F32)


def product_tn(left, right):
    return lax.dot_general(left, right, (((0,), (0,)), ((), ())), preferred_element_type=F32)


def gelu_parts(values):
    square = values * values
    inner = jnp.tanh(TANH_SCALE * (values + CUBIC * square * values))
    half = 0.5 * (1.0 + inner)
    slope = half + 0.5 * values * (1.0 - inner * inner) * (TANH_SCALE * (1.0 + 3.0 * CUBIC * square))
    return values * half, slope


def lanes_of(shape):
    return lax.broadcasted_iota(jnp.int32, shape, len(shape) - 1)


def layer_norm(rows, channels):
    mean = jnp.sum(rows, axis=-1, keepdims=True) * (1.0 / channels)
    center = jnp.where(lanes_of(rows.shape) < channels, rows - mean, 0.0)
    scale = lax.rsqrt(jnp.sum(center * center, axis=-1, keepdims=True) * (1.0 / channels) + EPSILON)
    return center * scale, scale


def norm_back(grad_norm, normed, scale, channels):
    mean_grad = jnp.sum(grad_norm, axis=-1, keepdims=True) * (1.0 / channels)
    mean_cross = jnp.sum(grad_norm * normed, axis=-1, keepdims=True) * (1.0 / channels)
    return (grad_norm - mean_grad - normed * mean_cross) * scale


def choose(entries, slot, which, own, got):
    entry = entries[slot, which]
    held = jnp.maximum(entry, 0)
    place, source = held % 2, held // 2
    from_own = jnp.where((entry >= 0) & (source == 0), 1.0, 0.0)
    from_got = jnp.where((entry >= 0) & (source != 0), 1.0, 0.0)
    return own[place].astype(F32) * from_own + got[place].astype(F32) * from_got


def mask_lanes(mask, slot, filled):
    cells = SIDE * SIDE
    row = lax.broadcasted_iota(jnp.int32, (SIDE, cells), 0) * SIDE
    lane = lanes_of((SIDE, cells))
    live = jnp.broadcast_to(mask[slot : slot + 1, :].astype(F32), (SIDE, cells))
    live = jnp.where((lane >= row) & (lane < row + SIDE) & (filled > slot), live, 0.0).astype(BF16)
    cell = lax.broadcasted_iota(jnp.int32, (cells, SIDE), 0) % SIDE
    pick = jnp.where(cell == lanes_of((cells, SIDE)), 1.0, 0.0).astype(BF16)
    column = lax.broadcasted_iota(jnp.int32, (SIDE, SIDE * C1), 0) * C1
    lane = lanes_of((SIDE, SIDE * C1))
    spread = jnp.where((lane >= column) & (lane < column + C1), 1.0, 0.0).astype(BF16)
    return product(product(live, pick).astype(BF16), spread)


def rims_kernel(count, state, mask, west, east):
    for slot in range(2):
        masked = state[slot].astype(F32) * mask_lanes(mask, slot, count[0, 0])
        for k in range(3):
            west[slot, k] = masked[:, C1 * k : C1 * (k + 1)].astype(BF16)
            column = SIDE - 3 + k
            east[slot, k] = masked[:, C1 * column : C1 * (column + 1)].astype(BF16)


def to_blocks(values, wide, striped, lined, cat, slot):
    for t in range(25):
        striped[t] = values[:, LANES * t : LANES * (t + 1)]
    for a in range(2):
        for t in range(25):
            lined[:, LANES * t : LANES * (t + 1)] = striped[t, pl.ds(a, HALF, stride=2), :]
        for column in range(HALF):
            row = slot * 64 + column * HALF
            cat[row : row + HALF, C2 * a : C2 * (a + 1)] = lined[:, C2 * column : C2 * (column + 1)]


def before_kernel(count, state, mask, cotangent, w_up, field, mask_cat, cot_cat, change, mask_two, wide, striped, lined, held):
    field[...] = jnp.zeros(field.shape, F32)
    lane = lanes_of((SIDE, LANES))
    wide[...] = jnp.zeros(wide.shape, F32)
    for slot in range(2):
        spread = mask_lanes(mask, slot, count[0, 0])
        to_blocks(spread, wide, striped, lined, mask_cat, slot)
        to_blocks(cotangent[slot].astype(F32) * spread, wide, striped, lined, held, slot)
        wide[:, : SIDE * C1] = state[slot].astype(F32) * spread
        for column in range(SIDE):
            part = wide[:, C1 * column : C1 * column + 256]
            field[slot, 0, 3 + column, 3:19, :] = part[:, :LANES]
            field[slot, 1, 3 + column, 3:19, :] = jnp.where(lane < C1 - LANES, part[:, LANES:], 0.0)
    cot_cat[...] = held[...].astype(BF16)
    wet = mask_cat[:, 0:1]
    for k in range(1, 4):
        wet = jnp.maximum(wet, mask_cat[:, C1 * k : C1 * k + 1])
    mask_two[...] = jnp.broadcast_to(wet, (LANES, LANES))
    change[...] = (wet * product_nt(cot_cat[...], w_up[...])).astype(BF16)


def add_columns(entries, out, slot, side, channels, west, west_got, east, east_got):
    tiles = -(-channels // LANES)
    for which, start, own, got in ((0, 0, east, west_got), (1, side + 3, west, east_got)):
        value = choose(entries, slot, which, own, got)
        for t in range(tiles):
            width = min(LANES, channels - LANES * t)
            out[slot, t, start : start + 3, 3 : 3 + side, :width] = value[:, :, LANES * t : LANES * t + width]


def across(entries, slot, which, code):
    entry = entries[slot, which]
    return jnp.where((entry >= 0) & (entry // 2 == code), 1.0, 0.0)


def strips_of(entries, out, side, channels, top, bottom):
    north = [across(entries, slot, 2, 3) for slot in range(2)]
    south = [across(entries, slot, 3, 4) for slot in range(2)]
    for t in range(-(-channels // LANES)):
        width = min(LANES, channels - LANES * t)
        span = slice(LANES * t, LANES * t + width)
        parts = [out[slot, t, :, 3:6, :width] * north[slot] for slot in range(2)]
        top[:, :, span] = (parts[0] + parts[1]).astype(BF16)
        parts = [out[slot, t, :, side : side + 3, :width] * south[slot] for slot in range(2)]
        bottom[:, :, span] = (parts[0] + parts[1]).astype(BF16)


def add_rows(entries, out, slot, side, channels, top_got, bottom_got):
    for which, code, start, inner, got in ((2, 3, 0, side, top_got), (3, 4, side + 3, 3, bottom_got)):
        entry = entries[slot, which]
        place = jnp.maximum(entry, 0) % 2
        from_own = jnp.where((entry >= 0) & (entry // 2 == 0), 1.0, 0.0)
        from_got = across(entries, slot, which, code)
        for t in range(-(-channels // LANES)):
            width = min(LANES, channels - LANES * t)
            own = out[place, t, :, inner : inner + 3, :width]
            value = got[:, :, LANES * t : LANES * t + width].astype(F32)
            out[slot, t, :, start : start + 3, :width] = own * from_own + value * from_got


def strips_one_kernel(entries, field, west, west_got, east, east_got, out, top, bottom):
    out[...] = field[...]
    for slot in range(2):
        add_columns(entries, out, slot, SIDE, C1, west, west_got, east, east_got)
    strips_of(entries, out, SIDE, C1, top, bottom)


def strips_two_kernel(entries, rows, west, west_got, east, east_got, out, top, bottom):
    out[...] = jnp.zeros(out.shape, F32)
    for slot in range(2):
        for t in range(4):
            width = min(LANES, C2 - LANES * t)
            for column in range(HALF):
                start = slot * 64 + column * HALF
                out[slot, t, 3 + column, 3 : 3 + HALF, :width] = rows[start : start + HALF, LANES * t : LANES * t + width].astype(F32)
        add_columns(entries, out, slot, HALF, C2, west, west_got, east, east_got)
    strips_of(entries, out, HALF, C2, top, bottom)


def load_taps(kernel, taps, channels):
    tiles = -(-channels // LANES)
    taps[...] = jnp.zeros(taps.shape, F32)
    for t in range(tiles):
        width = min(LANES, channels - LANES * t)
        for p in range(7):
            taps[t, 7 * p : 7 * p + 7, :width] = kernel[p, :, LANES * t : LANES * t + width].astype(F32)


def conv_one(field, taps, out):
    def body(index, carry):
        slot, t = index // 2, index % 2
        for a in range(2):
            total = jnp.zeros((SIDE, HALF, LANES), F32)
            for p in range(7):
                for q in range(7):
                    window = field[slot, t, q : q + SIDE, pl.ds(a + p, HALF, stride=2), :]
                    total = total + window * taps[t, pl.ds(7 * p + q, 1), :][None]
            out[t, a, slot] = total
        return carry

    lax.fori_loop(0, 4, body, 0)


def conv_two(field, taps, out, flipped):
    def body(index, carry):
        slot, t = index // 4, index % 4
        total = jnp.zeros((HALF, HALF, LANES), F32)
        for p in range(7):
            for q in range(7):
                tap = 48 - (7 * p + q) if flipped else 7 * p + q
                total = total + field[slot, t, q : q + HALF, p : p + HALF, :] * taps[t, pl.ds(tap, 1), :][None]
        out[t, slot] = total
        return carry

    lax.fori_loop(0, 8, body, 0)


def first_kernel(entries, field, top_got, bottom_got, kern, w_in, w_out, w_down, mask_cat, mask_two,
                 out, normed, scales, blocks, coarse, west, east, taps, conv, held):
    out[...] = field[...]
    for slot in range(2):
        add_rows(entries, out, slot, SIDE, C1, top_got, bottom_got)
    load_taps(kern, taps, C1)
    conv_one(out, taps, conv)
    for a in range(2):
        for co in range(2):
            k = 2 * a + co
            rows, base = [], []
            for slot in range(2):
                for column in range(HALF):
                    place = 2 * column + co
                    rows.append(jnp.concatenate([conv[t, a, slot, place] for t in range(2)], axis=1))
                    base.append(jnp.concatenate([out[slot, t, 3 + place, pl.ds(3 + a, HALF, stride=2), :] for t in range(2)], axis=1))
            values, scale = layer_norm(jnp.concatenate(rows, axis=0), C1)
            normed[LANES * k : LANES * (k + 1), :] = values
            scales[LANES * k : LANES * (k + 1), :] = jnp.broadcast_to(scale, (LANES, LANES))
            hidden, _ = gelu_parts(product(values[:, :C1].astype(BF16), w_in[...]))
            branch = product_nt(hidden.astype(BF16), w_out[...])
            held[:, C1 * k : C1 * (k + 1)] = jnp.concatenate(base, axis=0)[:, :C1] + branch
    blocks[...] = (mask_cat[...] * held[...]).astype(BF16)
    wet = jnp.concatenate([mask_two[...]] * 4, axis=1)[:, :C2]
    rough = wet * product_nt(blocks[...], w_down[...])
    coarse[...] = rough.astype(BF16)
    send_rims(rough, west, east)


def send_rims(values, west, east):
    for slot in range(2):
        for k in range(3):
            start = slot * 64 + k * HALF
            west[slot, k] = values[start : start + HALF].astype(BF16)
            start = slot * 64 + (HALF - 3 + k) * HALF
            east[slot, k] = values[start : start + HALF].astype(BF16)


def rows_two(conv):
    return jnp.concatenate([conv[t].reshape(LANES, LANES) for t in range(4)], axis=1)


def second_kernel(entries, field, top_got, bottom_got, kern, w_in, w_out, coarse, change, mask_two,
                  out, normed_b, hidden, grad_pre, level, back, west, east, taps, conv):
    out[...] = field[...]
    for slot in range(2):
        add_rows(entries, out, slot, HALF, C2, top_got, bottom_got)
    load_taps(kern, taps, C2)
    conv_two(out, taps, conv, False)
    values, scale = layer_norm(rows_two(conv), C2)
    values = values[:, :C2]
    normed_b[...] = values.astype(BF16)
    act, slope = gelu_parts(product(normed_b[...], w_in[...]))
    hidden[...] = act.astype(BF16)
    grad_pre[...] = (product(change[...], w_out[...]) * slope).astype(BF16)
    wet = jnp.concatenate([mask_two[...]] * 4, axis=1)[:, :C2]
    level[...] = (wet * (coarse[...].astype(F32) + product_nt(hidden[...], w_out[...]))).astype(BF16)
    reverse = norm_back(product_nt(grad_pre[...], w_in[...]), values, scale, C2)
    back[...] = reverse.astype(BF16)
    send_rims(reverse, west, east)


def predict_kernel(blocks, level, w_up, mask_cat, prediction, held, lined, striped):
    held[...] = mask_cat[...] * (blocks[...].astype(F32) + product(level[...], w_up[...]))
    for slot in range(2):
        for a in range(2):
            for column in range(HALF):
                row = slot * 64 + column * HALF
                lined[:, C2 * column : C2 * (column + 1)] = held[row : row + HALF, C2 * a : C2 * (a + 1)]
            for t in range(25):
                striped[t, pl.ds(a, HALF, stride=2), :] = lined[:, LANES * t : LANES * (t + 1)]
        for t in range(25):
            prediction[slot, :, LANES * t : LANES * (t + 1)] = striped[t].astype(BF16)


def hold(held, value):
    rows, width = value.shape
    for t in range(-(-width // LANES)):
        part = value[:, LANES * t : min(width, LANES * (t + 1))]
        if part.shape[1] < LANES:
            held[t, :rows, :] = jnp.zeros((rows, LANES), F32)
        held[t, :rows, : part.shape[1]] = part


def lay_flat(flat, source, first_entry, rows, width, first_row):
    unit = UNIT // width
    count = rows // unit
    base = first_entry // LANES - first_row
    tiles = -(-width // LANES)
    lane = lax.broadcasted_iota(jnp.int32, (count, LANES), 1)
    parts = {}
    for a in range(unit):
        for t in range(tiles):
            value = source[t, pl.ds(a, count, stride=unit), :]
            place = first_entry % LANES + width * a + LANES * t
            shift = place % LANES
            if shift:
                value = pltpu.roll(value, shift, 1)
                low = jnp.where(lane >= shift, value, 0.0)
                high = jnp.where(lane < shift, value, 0.0)
                parts.setdefault(place // LANES, []).append(low)
                if not (t == tiles - 1 and shift + width - LANES * t <= LANES):
                    parts.setdefault(place // LANES + 1, []).append(high)
            else:
                parts.setdefault(place // LANES, []).append(value)
    merged = {j: functools.reduce(jnp.add, values) for j, values in parts.items()}
    for j in range(1, 25):
        flat[pl.ds(base + j, count, stride=25), :] = merged[j]
    head = merged[0]
    if 25 in merged:
        tail = merged[25]
        row = lax.broadcasted_iota(jnp.int32, (count, LANES), 0)
        before = pltpu.roll(tail, 1, 0) if count % 8 == 0 else jnp.concatenate([tail[-1:], tail[:-1]], axis=0)
        head = head + jnp.where(row > 0, before, 0.0)
    opening = flat[base : base + 1, :]
    flat[pl.ds(base, count, stride=25), :] = head
    flat[base : base + 1, :] = flat[base : base + 1, :] + opening
    if 25 in merged:
        flat[base + 25 * count : base + 25 * count + 1, :] = tail[count - 1 : count, :]
    else:
        flat[base + 25 * count : base + 25 * count + 1, :] = jnp.zeros((1, LANES), jnp.float32)


def clear_taps(held, tiles, rows):
    for t in range(tiles):
        held[t, 48:rows, :] = jnp.zeros((rows - 48, LANES), F32)


def grads_two_kernel(field, back, normed_b, hidden, grad_pre, level, change, cot_cat, keep, send, flat, held, tall, sums):
    flat[0:64, :] = jnp.zeros((64, LANES), F32)
    clear_taps(held, 4, 56)
    for t in range(4):
        width = min(LANES, C2 - LANES * t)
        deltas = []
        for slot in range(2):
            delta = back[64 * slot : 64 * (slot + 1), LANES * t : LANES * t + width].astype(F32)
            if width < LANES:
                delta = jnp.concatenate([delta, jnp.zeros((64, LANES - width), F32)], axis=1)
            deltas.append(delta.reshape(HALF, HALF, LANES))
        for p in range(7):
            for q in range(7):
                total = jnp.zeros((HALF, LANES), F32)
                for slot in range(2):
                    total = total + jnp.sum(field[slot, t, q : q + HALF, p : p + HALF, :] * deltas[slot], axis=0)
                sums[7 * p + q] = total
        held[t, :49, :] = jnp.sum(sums[...], axis=1)
    lay_flat(flat, held, 649800, 56, C2, SPLIT_ROW)
    hold(held, product_tn(normed_b[...], grad_pre[...]))
    lay_flat(flat, held, 669400, C2, 4 * C2, SPLIT_ROW)
    hold(tall, product_tn(hidden[...], change[...]))
    lay_flat(flat, tall, 1309400, 4 * C2, C2, SPLIT_ROW)
    hold(held, product_tn(level[...], cot_cat[...]))
    lay_flat(flat, held, 1949400, C2, 4 * C1, SPLIT_ROW)
    last = 17730 - SPLIT_ROW
    flat[last:, :] = jnp.zeros((17920 + 8 - SPLIT_ROW - last, LANES), F32)
    keep[:8, 0] = jnp.zeros((8, HELD, LANES), BF16)
    send[:8, 0] = jnp.zeros((8, HELD, LANES), BF16)
    split_out(lax.axis_index("c"), flat, keep, send, 9, 32, store_two)


def split_out(core, flat, keep, send, first, stop, store):
    def write(even, odd):
        for block in range(first, stop):
            target = odd if block % 2 else even
            for xl in range(2):
                for y in range(4):
                    start = (block - first) * BLOCK + (xl * 4 + y) * PIECE
                    store(target, block // 4, block // 2 % 2, xl, y, flat[start : start + HELD, :].astype(BF16))

    @pl.when(core == 0)
    def _():
        write(keep, send)

    @pl.when(core != 0)
    def _():
        write(send, keep)


def store_two(target, z, xh, xl, y, value):
    target[8 * xh + 4 * xl + y, z - 2] = value


def store_one(target, z, xh, xl, y, value):
    target[8 * xh + 4 * xl + y, z] = value


def last_kernel(entries, delta, top_got, bottom_got, kern, change, mask_two, mask_cat, cot_cat, blocks,
                w_down, w_in, w_out, normed, scales, field, keep, send,
                out, taps, conv, held_cat, rough, hidden, grad_pre, fine, back, sums, flat, held):
    out[...] = delta[...]
    for slot in range(2):
        add_rows(entries, out, slot, HALF, C2, top_got, bottom_got)
    load_taps(kern, taps, C2)
    conv_two(out, taps, conv, True)
    wet = jnp.concatenate([mask_two[...]] * 4, axis=1)[:, :C2]
    rough[...] = (wet * (change[...].astype(F32) + rows_two(conv)[:, :C2])).astype(BF16)
    held_cat[...] = mask_cat[...] * (cot_cat[...].astype(F32) + product(rough[...], w_down[...]))
    flat[0:8, :] = jnp.zeros((8, LANES), F32)
    for k in range(4):
        a, co = k // 2, k % 2
        rows = slice(LANES * k, LANES * (k + 1))
        fine[rows, :] = held_cat[:, C1 * k : C1 * (k + 1)].astype(BF16)
        values = normed[rows, :]
        act, slope = gelu_parts(product(values[:, :C1].astype(BF16), w_in[...]))
        hidden[rows, :] = act.astype(BF16)
        grad_pre[rows, :] = (product(fine[rows, :], w_out[...]) * slope).astype(BF16)
        grad = product_nt(grad_pre[rows, :], w_in[...])
        reverse = norm_back(grad, values[:, :C1], scales[rows, 0:1], C1)
        for slot in range(2):
            for column in range(HALF):
                start = slot * 64 + column * HALF
                part = reverse[start : start + HALF]
                back[0, a, slot, 2 * column + co] = part[:, :LANES]
                back[1, a, slot, 2 * column + co] = jnp.concatenate([part[:, LANES:], jnp.zeros((HALF, 2 * LANES - C1), F32)], axis=1)
    clear_taps(held, 2, 64)
    for t in range(2):
        sums[...] = jnp.zeros(sums.shape, F32)

        def body(index, carry):
            slot, a = index // 2, index % 2
            part = back[t, a, slot]
            for p in range(7):
                for q in range(7):
                    window = field[slot, t, q : q + SIDE, pl.ds(a + p, HALF, stride=2), :]
                    sums[7 * p + q] = sums[7 * p + q] + jnp.sum(window * part, axis=0)
            return carry

        lax.fori_loop(0, 4, body, 0)
        held[t, :49, :] = jnp.sum(sums[...], axis=1)
    lay_flat(flat, held, 0, 64, C1, 0)
    hold(held, product_tn(normed[:, :C1].astype(BF16), grad_pre[...]))
    lay_flat(flat, held, 9800, C1, 4 * C1, 0)
    hold(held, product_tn(hidden[...], fine[...]))
    lay_flat(flat, held, 169800, 4 * C1, C1, 0)
    hold(held, product_tn(blocks[...], rough[...]))
    lay_flat(flat, held, 329800, 4 * C1, C2, 0)
    flat[5077:, :] = jnp.zeros((5608 - 5077, LANES), F32)
    keep[8:, 2] = jnp.zeros((8, HELD, LANES), BF16)
    send[8:, 2] = jnp.zeros((8, HELD, LANES), BF16)
    split_out(lax.axis_index("c"), flat, keep, send, 0, 10, store_one)


def around(array, axes, step):
    size = 1
    for axis in axes:
        size *= lax.axis_size(axis)
    return lax.ppermute(array, axes, [(i, (i + step) % size) for i in range(size)])


def wide_sum(*parts):
    total = parts[0].astype(F32)
    for part in parts[1:]:
        total = total + part.astype(F32)
    return total.astype(BF16)


def other_core(send):
    return lax.ppermute(send, "c", [(0, 1), (1, 0)])


def added(terms):
    result = terms[0].astype(F32)
    for term in terms[1:]:
        result = result + term.astype(F32)
    return result.astype(BF16)


def x_parts_kernel(*refs):
    parts, outs = refs[:-4], refs[-4:]
    x = 2 * lax.axis_index("xh") + lax.axis_index("xl")
    for k in range(4):
        for z in range(outs[k].shape[0]):
            outs[k][z] = added([part[x ^ k, z] for part in parts])


def y_parts_kernel(keep, got, *outs):
    y = lax.axis_index("y")
    for k in range(4):
        for x in range(4):
            place = 4 * x + (y + k) % 4
            for z in range(outs[k].shape[1]):
                outs[k][x, z] = added([keep[place, z], got[place, z]])


def x_first_kernel(keep, got, *outs):
    x = 2 * lax.axis_index("xh") + lax.axis_index("xl")
    for k in range(4):
        for y in range(4):
            place = 4 * (x ^ k) + y
            for z in range(3):
                outs[k][y, z] = added([keep[place, z], got[place, z]])


def y_second_kernel(*refs):
    parts, outs = refs[:4], refs[4:]
    y = lax.axis_index("y")
    for k in range(4):
        for z in range(3):
            outs[k][z] = added([part[(y + k) % 4, z] for part in parts])


def over_y(parts):
    return [parts[0]] + [around(parts[k], ("y",), k) for k in range(1, 4)]


def over_x(parts):
    return [parts[0]] + [lax.ppermute(parts[k], ("xh", "xl"), [(i, i ^ k) for i in range(4)]) for k in range(1, 4)]


def merge_kernel(*refs):
    one, two, out = refs[:4], refs[4:8], refs[8]
    for z in range(8):
        terms = []
        if z < 3:
            terms += [ref[z] for ref in one]
        if z >= 2:
            terms += [ref[z - 2] for ref in two]
        out[z] = added(terms)


def final_kernel(parts, out):
    total = parts[0].astype(F32)
    for k in range(1, parts.shape[0]):
        total = total + parts[k].astype(F32)
    out[...] = total


def local(ocean_state, land_mask, wet_count, neighbours, kern_one, w_in_one, w_out_one, w_down, kern_two, w_in_two, w_out_two, w_up, cotangent):
    state, cot = ocean_state[0], cotangent[0]
    w_out_one, w_down, w_out_two = w_out_one.T, w_down.T, w_out_two.T
    mask = land_mask[0]
    entries = neighbours[0]
    rims_one, rims_two = (2, 3, SIDE, C1), (2, 3, HALF, C2)
    strip_one, strip_two = (22, 3, C1), (14, 3, C2)
    field_one, field_two = (2, 2, 22, 24, LANES), (2, 4, 14, 16, LANES)
    cat = (LANES, 4 * C1)
    west, east = call(rims_kernel, [(rims_one, BF16)] * 2, smem=1)(wet_count, state, mask)
    west_got, east_got = around(east, TILES, 1), around(west, TILES, -1)
    field, mask_cat, cot_cat, change, mask_two = call(
        before_kernel,
        [(field_one, F32), (cat, F32), (cat, BF16), ((LANES, C2), BF16), ((LANES, LANES), F32)],
        [((SIDE, 3328), F32), ((25, SIDE, LANES), F32), ((HALF, SIDE * C1), F32), (cat, F32)],
        room=16, us=2, smem=1,
    )(wet_count, state, mask, cot, w_up)
    field, top, bottom = call(strips_one_kernel, [(field_one, F32), (strip_one, BF16), (strip_one, BF16)], smem=1)(
        entries, field, west, west_got, east, east_got
    )
    top_got, bottom_got = around(bottom, LAT, 1), around(top, LAT, -1)
    field_one_own, normed_one, scales_one, blocks, coarse, west, east = call(
        first_kernel,
        [(field_one, F32), ((512, 256), F32), ((512, LANES), F32), (cat, BF16), ((LANES, C2), BF16), (rims_two, BF16), (rims_two, BF16)],
        [((2, 49, LANES), F32), ((2, 2, 2, SIDE, HALF, LANES), F32), (cat, F32)],
        room=16, us=6, smem=1,
    )(entries, field, top_got, bottom_got, kern_one, w_in_one, w_out_one, w_down, mask_cat, mask_two)

    def strips_two(rows, west, west_got, east, east_got):
        return call(strips_two_kernel, [(field_two, F32), (strip_two, BF16), (strip_two, BF16)], smem=1)(
            entries, rows, west, west_got, east, east_got
        )

    two = ((LANES, 4 * C2), BF16)
    slim = ((LANES, C2), BF16)
    west_got, east_got = around(east, TILES, 1), around(west, TILES, -1)
    field_two_own, top, bottom = strips_two(coarse, west, west_got, east, east_got)
    sides = field_two_own, around(bottom, LAT, 1), around(top, LAT, -1)
    field_in_two, normed_two, hidden_two, grad_pre_two, level, back, west, east = call(
        second_kernel,
        [(field_two, F32), slim, two, two, slim, slim, (rims_two, BF16), (rims_two, BF16)],
        [((4, 49, LANES), F32), ((4, 2, HALF, HALF, LANES), F32)],
        room=16, us=6, smem=1,
    )(entries, *sides, kern_two, w_in_two, w_out_two, coarse, change, mask_two)
    west_got, east_got = around(east, TILES, 1), around(west, TILES, -1)
    keep_two, send_two = call(
        grads_two_kernel,
        [((16, 6, HELD, LANES), BF16)] * 2,
        [((17920 + 8 - SPLIT_ROW, LANES), F32), ((13, C2, LANES), F32), ((4, 4 * C2, LANES), F32), ((49, HALF, LANES), F32)],
        room=16, us=7,
    )(field_in_two, back, normed_two, hidden_two, grad_pre_two, level, change, cot_cat)
    west_got, east_got, send_two = lax.optimization_barrier((west_got, east_got, send_two))
    got_two = other_core(send_two)
    (prediction,) = call(
        predict_kernel,
        [((2, SIDE, SIDE * C1), BF16)],
        [(cat, F32), ((HALF, SIDE * C1), F32), ((25, SIDE, LANES), F32)],
    )(blocks, level, w_up, mask_cat)
    field, top, bottom = strips_two(back, west, west_got, east, east_got)
    top_got, bottom_got = around(bottom, LAT, 1), around(top, LAT, -1)
    parts = list(call(y_parts_kernel, [((4, 6, HELD, LANES), BF16)] * 4)(keep_two, got_two))
    top_got, bottom_got, *parts[1:] = lax.optimization_barrier((top_got, bottom_got, *parts[1:]))
    parts_two = over_y(parts)
    sides = field, top_got, bottom_got
    keep_one, send_one = call(
        last_kernel,
        [((16, 3, HELD, LANES), BF16)] * 2,
        [
            (field_two, F32),
            ((4, 49, LANES), F32),
            ((4, 2, HALF, HALF, LANES), F32),
            (cat, F32),
            slim,
            ((512, 4 * C1), BF16),
            ((512, 4 * C1), BF16),
            ((512, C1), BF16),
            ((2, 2, 2, SIDE, HALF, LANES), F32),
            ((49, HALF, LANES), F32),
            ((5608, LANES), F32),
            ((7, 800, LANES), F32),
        ],
        room=16, us=10, smem=1,
    )(entries, *sides, kern_two, change, mask_two, mask_cat, cot_cat, blocks, w_down, w_in_one, w_out_one, normed_one, scales_one, field_one_own)
    send_one, parts_two[1], parts_two[3] = lax.optimization_barrier((send_one, parts_two[1], parts_two[3]))
    return prediction[None], finish(keep_one, send_one, parts_two)


def finish(keep_one, send_one, parts_two):
    piece = ((3, HELD, LANES), BF16)
    parts = call(x_first_kernel, [((4, 3, HELD, LANES), BF16)] * 4)(keep_one, other_core(send_one))
    parts_one = over_x(parts)
    parts_two = call(x_parts_kernel, [((6, HELD, LANES), BF16)] * 4)(*parts_two)
    parts_one[1], _ = lax.optimization_barrier((parts_one[1], parts_two[1]))
    parts_two = over_x(parts_two)
    parts_one = over_y(call(y_second_kernel, [piece] * 4)(*parts_one))
    (total,) = call(merge_kernel, [((8, HELD, LANES), BF16)])(*parts_one, *parts_two)
    total = lax.all_to_all(total, "z", 0, 0)
    (total,) = call(final_kernel, [((HELD, LANES), F32)])(total)
    return total[:PIECE].reshape(-1)


def solution(mesh):
    mesh = Mesh(mesh.devices.reshape(8, 2, 2, 2, 4), TILES + LAT)
    return jax.shard_map(
        local,
        mesh=mesh,
        in_specs=(
            P(LAT, TILES, None, None),
            P(LAT, TILES, None),
            P(LAT, TILES),
            P(LAT, TILES, None),
            P(),
            P(),
            P(),
            P(),
            P(),
            P(),
            P(),
            P(),
            P(LAT, TILES, None, None),
        ),
        out_specs=(P(LAT, TILES, None, None), P(TILES + LAT)),
        check_vma=False,
    )
```

```python
import functools

import jax
import jax.numpy as jnp
from jax import lax
from jax.experimental import pallas as pl
from jax.experimental.pallas import tpu as pltpu
from jax.sharding import Mesh
from jax.sharding import PartitionSpec as P

TILES = ("z", "xh", "c")
LAT = ("xl", "y")
EPSILON = 1e-06
TANH_SCALE = 0.7978845608028654
CUBIC = 0.044715
LANES = 128
PIECE = 70
HELD = 72
UNIT = 3200
BLOCK = 560
C1, C2 = 200, 400
SIDE, HALF = 16, 8
F32, BF16 = jnp.float32, jnp.bfloat16
SPLIT_ROW = 5040
SPLIT = 4


def call(body, outs, scratch=(), smem=0, room=16, us=1):
    def run(*args):
        vmem = pl.BlockSpec(memory_space=pltpu.VMEM)
        specs = [pl.BlockSpec(memory_space=pltpu.SMEM)] * smem + [vmem] * (len(args) - smem)
        return pl.pallas_call(
            body,
            out_shape=[jax.ShapeDtypeStruct(shape, kind) for shape, kind in outs],
            in_specs=specs,
            out_specs=[vmem] * len(outs),
            scratch_shapes=[pltpu.VMEM(shape, kind) for shape, kind in scratch],
            compiler_params=pltpu.CompilerParams(vmem_limit_bytes=room * 2**20),
            cost_estimate=pl.CostEstimate(flops=us * 10**9, bytes_accessed=10**6, transcendentals=0),
        )(*args)

    return run


def product(left, right):
    return jnp.dot(left, right, preferred_element_type=F32)


def product_nt(left, right):
    return lax.dot_general(left, right, (((1,), (1,)), ((), ())), preferred_element_type=F32)


def product_tn(left, right):
    return lax.dot_general(left, right, (((0,), (0,)), ((), ())), preferred_element_type=F32)


def gelu_parts(values):
    square = values * values
    inner = jnp.tanh(TANH_SCALE * (values + CUBIC * square * values))
    half = 0.5 * (1.0 + inner)
    slope = half + 0.5 * values * (1.0 - inner * inner) * (TANH_SCALE * (1.0 + 3.0 * CUBIC * square))
    return values * half, slope


def lanes_of(shape):
    return lax.broadcasted_iota(jnp.int32, shape, len(shape) - 1)


def layer_norm(rows, channels):
    mean = jnp.sum(rows, axis=-1, keepdims=True) * (1.0 / channels)
    center = jnp.where(lanes_of(rows.shape) < channels, rows - mean, 0.0)
    scale = lax.rsqrt(jnp.sum(center * center, axis=-1, keepdims=True) * (1.0 / channels) + EPSILON)
    return center * scale, scale


def norm_back(grad_norm, normed, scale, channels):
    mean_grad = jnp.sum(grad_norm, axis=-1, keepdims=True) * (1.0 / channels)
    mean_cross = jnp.sum(grad_norm * normed, axis=-1, keepdims=True) * (1.0 / channels)
    return (grad_norm - mean_grad - normed * mean_cross) * scale


def choose(entries, slot, which, own, got):
    entry = entries[slot, which]
    held = jnp.maximum(entry, 0)
    place, source = held % 2, held // 2
    from_own = jnp.where((entry >= 0) & (source == 0), 1.0, 0.0)
    from_got = jnp.where((entry >= 0) & (source != 0), 1.0, 0.0)
    return own[place].astype(F32) * from_own + got[place].astype(F32) * from_got


def mask_lanes(mask, slot, filled):
    cells = SIDE * SIDE
    row = lax.broadcasted_iota(jnp.int32, (SIDE, cells), 0) * SIDE
    lane = lanes_of((SIDE, cells))
    live = jnp.broadcast_to(mask[slot : slot + 1, :].astype(F32), (SIDE, cells))
    live = jnp.where((lane >= row) & (lane < row + SIDE) & (filled > slot), live, 0.0).astype(BF16)
    cell = lax.broadcasted_iota(jnp.int32, (cells, SIDE), 0) % SIDE
    pick = jnp.where(cell == lanes_of((cells, SIDE)), 1.0, 0.0).astype(BF16)
    column = lax.broadcasted_iota(jnp.int32, (SIDE, SIDE * C1), 0) * C1
    lane = lanes_of((SIDE, SIDE * C1))
    spread = jnp.where((lane >= column) & (lane < column + C1), 1.0, 0.0).astype(BF16)
    return product(product(live, pick).astype(BF16), spread)


def rims_kernel(count, state, mask, west, east):
    for slot in range(2):
        masked = state[slot].astype(F32) * mask_lanes(mask, slot, count[0, 0])
        for k in range(3):
            west[slot, k] = masked[:, C1 * k : C1 * (k + 1)].astype(BF16)
            column = SIDE - 3 + k
            east[slot, k] = masked[:, C1 * column : C1 * (column + 1)].astype(BF16)


def to_blocks(values, wide, striped, lined, cat, slot):
    for t in range(25):
        striped[t] = values[:, LANES * t : LANES * (t + 1)]
    for a in range(2):
        for t in range(25):
            lined[:, LANES * t : LANES * (t + 1)] = striped[t, pl.ds(a, HALF, stride=2), :]
        for column in range(HALF):
            row = slot * 64 + column * HALF
            cat[row : row + HALF, C2 * a : C2 * (a + 1)] = lined[:, C2 * column : C2 * (column + 1)]


def before_kernel(count, state, mask, cotangent, w_up, field, mask_cat, cot_cat, change, mask_two, wide, striped, lined, held):
    field[...] = jnp.zeros(field.shape, F32)
    lane = lanes_of((SIDE, LANES))
    wide[...] = jnp.zeros(wide.shape, F32)
    for slot in range(2):
        spread = mask_lanes(mask, slot, count[0, 0])
        to_blocks(spread, wide, striped, lined, mask_cat, slot)
        to_blocks(cotangent[slot].astype(F32) * spread, wide, striped, lined, held, slot)
        wide[:, : SIDE * C1] = state[slot].astype(F32) * spread
        for column in range(SIDE):
            part = wide[:, C1 * column : C1 * column + 256]
            field[slot, 0, 3 + column, 3:19, :] = part[:, :LANES]
            field[slot, 1, 3 + column, 3:19, :] = jnp.where(lane < C1 - LANES, part[:, LANES:], 0.0)
    cot_cat[...] = held[...].astype(BF16)
    wet = mask_cat[:, 0:1]
    for k in range(1, 4):
        wet = jnp.maximum(wet, mask_cat[:, C1 * k : C1 * k + 1])
    mask_two[...] = jnp.broadcast_to(wet, (LANES, LANES))
    change[...] = (wet * product_nt(cot_cat[...], w_up[...])).astype(BF16)


def add_columns(entries, out, slot, side, channels, west, west_got, east, east_got):
    tiles = -(-channels // LANES)
    for which, start, own, got in ((0, 0, east, west_got), (1, side + 3, west, east_got)):
        value = choose(entries, slot, which, own, got)
        for t in range(tiles):
            width = min(LANES, channels - LANES * t)
            out[slot, t, start : start + 3, 3 : 3 + side, :width] = value[:, :, LANES * t : LANES * t + width]


def across(entries, slot, which, code):
    entry = entries[slot, which]
    return jnp.where((entry >= 0) & (entry // 2 == code), 1.0, 0.0)


def strips_of(entries, out, side, channels, top, bottom):
    north = [across(entries, slot, 2, 3) for slot in range(2)]
    south = [across(entries, slot, 3, 4) for slot in range(2)]
    for t in range(-(-channels // LANES)):
        width = min(LANES, channels - LANES * t)
        span = slice(LANES * t, LANES * t + width)
        parts = [out[slot, t, :, 3:6, :width] * north[slot] for slot in range(2)]
        top[:, :, span] = (parts[0] + parts[1]).astype(BF16)
        parts = [out[slot, t, :, side : side + 3, :width] * south[slot] for slot in range(2)]
        bottom[:, :, span] = (parts[0] + parts[1]).astype(BF16)


def add_rows(entries, out, slot, side, channels, top_got, bottom_got):
    for which, code, start, inner, got in ((2, 3, 0, side, top_got), (3, 4, side + 3, 3, bottom_got)):
        entry = entries[slot, which]
        place = jnp.maximum(entry, 0) % 2
        from_own = jnp.where((entry >= 0) & (entry // 2 == 0), 1.0, 0.0)
        from_got = across(entries, slot, which, code)
        for t in range(-(-channels // LANES)):
            width = min(LANES, channels - LANES * t)
            own = out[place, t, :, inner : inner + 3, :width]
            value = got[:, :, LANES * t : LANES * t + width].astype(F32)
            out[slot, t, :, start : start + 3, :width] = own * from_own + value * from_got


def strips_one_kernel(entries, field, west, west_got, east, east_got, out, top, bottom):
    out[...] = field[...]
    for slot in range(2):
        add_columns(entries, out, slot, SIDE, C1, west, west_got, east, east_got)
    strips_of(entries, out, SIDE, C1, top, bottom)


def strips_two_kernel(entries, rows, west, west_got, east, east_got, out, top, bottom):
    out[...] = jnp.zeros(out.shape, F32)
    for slot in range(2):
        for t in range(4):
            width = min(LANES, C2 - LANES * t)
            for column in range(HALF):
                start = slot * 64 + column * HALF
                out[slot, t, 3 + column, 3 : 3 + HALF, :width] = rows[start : start + HALF, LANES * t : LANES * t + width].astype(F32)
        add_columns(entries, out, slot, HALF, C2, west, west_got, east, east_got)
    strips_of(entries, out, HALF, C2, top, bottom)


def load_taps(kernel, taps, channels):
    tiles = -(-channels // LANES)
    taps[...] = jnp.zeros(taps.shape, F32)
    for t in range(tiles):
        width = min(LANES, channels - LANES * t)
        for p in range(7):
            taps[t, 7 * p : 7 * p + 7, :width] = kernel[p, :, LANES * t : LANES * t + width].astype(F32)


def conv_one(field, taps, out):
    def body(index, carry):
        slot, t = index // 2, index % 2
        for a in range(2):
            total = jnp.zeros((SIDE, HALF, LANES), F32)
            for p in range(7):
                for q in range(7):
                    window = field[slot, t, q : q + SIDE, pl.ds(a + p, HALF, stride=2), :]
                    total = total + window * taps[t, pl.ds(7 * p + q, 1), :][None]
            out[t, a, slot] = total
        return carry

    lax.fori_loop(0, 4, body, 0)


def conv_two(field, taps, out, flipped):
    def body(index, carry):
        slot, t = index // 4, index % 4
        total = jnp.zeros((HALF, HALF, LANES), F32)
        for p in range(7):
            for q in range(7):
                tap = 48 - (7 * p + q) if flipped else 7 * p + q
                total = total + field[slot, t, q : q + HALF, p : p + HALF, :] * taps[t, pl.ds(tap, 1), :][None]
        out[t, slot] = total
        return carry

    lax.fori_loop(0, 8, body, 0)


def first_kernel(entries, field, top_got, bottom_got, kern, w_in, w_out, w_down, mask_cat, mask_two,
                 out, normed, scales, blocks, coarse, west, east, taps, conv, held):
    out[...] = field[...]
    for slot in range(2):
        add_rows(entries, out, slot, SIDE, C1, top_got, bottom_got)
    load_taps(kern, taps, C1)
    conv_one(out, taps, conv)
    for a in range(2):
        for co in range(2):
            k = 2 * a + co
            rows, base = [], []
            for slot in range(2):
                for column in range(HALF):
                    place = 2 * column + co
                    rows.append(jnp.concatenate([conv[t, a, slot, place] for t in range(2)], axis=1))
                    base.append(jnp.concatenate([out[slot, t, 3 + place, pl.ds(3 + a, HALF, stride=2), :] for t in range(2)], axis=1))
            values, scale = layer_norm(jnp.concatenate(rows, axis=0), C1)
            normed[LANES * k : LANES * (k + 1), :] = values
            scales[LANES * k : LANES * (k + 1), :] = jnp.broadcast_to(scale, (LANES, LANES))
            hidden, _ = gelu_parts(product(values[:, :C1].astype(BF16), w_in[...]))
            branch = product_nt(hidden.astype(BF16), w_out[...])
            held[:, C1 * k : C1 * (k + 1)] = jnp.concatenate(base, axis=0)[:, :C1] + branch
    blocks[...] = (mask_cat[...] * held[...]).astype(BF16)
    wet = jnp.concatenate([mask_two[...]] * 4, axis=1)[:, :C2]
    rough = wet * product_nt(blocks[...], w_down[...])
    coarse[...] = rough.astype(BF16)
    send_rims(rough, west, east)


def send_rims(values, west, east):
    for slot in range(2):
        for k in range(3):
            start = slot * 64 + k * HALF
            west[slot, k] = values[start : start + HALF].astype(BF16)
            start = slot * 64 + (HALF - 3 + k) * HALF
            east[slot, k] = values[start : start + HALF].astype(BF16)


def rows_two(conv):
    return jnp.concatenate([conv[t].reshape(LANES, LANES) for t in range(4)], axis=1)


def second_kernel(entries, field, top_got, bottom_got, kern, w_in, w_out, coarse, change, mask_two,
                  out, normed_b, hidden, grad_pre, level, back, west, east, taps, conv):
    out[...] = field[...]
    for slot in range(2):
        add_rows(entries, out, slot, HALF, C2, top_got, bottom_got)
    load_taps(kern, taps, C2)
    conv_two(out, taps, conv, False)
    values, scale = layer_norm(rows_two(conv), C2)
    values = values[:, :C2]
    normed_b[...] = values.astype(BF16)
    act, slope = gelu_parts(product(normed_b[...], w_in[...]))
    hidden[...] = act.astype(BF16)
    grad_pre[...] = (product(change[...], w_out[...]) * slope).astype(BF16)
    wet = jnp.concatenate([mask_two[...]] * 4, axis=1)[:, :C2]
    level[...] = (wet * (coarse[...].astype(F32) + product_nt(hidden[...], w_out[...]))).astype(BF16)
    reverse = norm_back(product_nt(grad_pre[...], w_in[...]), values, scale, C2)
    back[...] = reverse.astype(BF16)
    send_rims(reverse, west, east)


def predict_kernel(blocks, level, w_up, mask_cat, prediction, held, lined, striped):
    held[...] = mask_cat[...] * (blocks[...].astype(F32) + product(level[...], w_up[...]))
    for slot in range(2):
        for a in range(2):
            for column in range(HALF):
                row = slot * 64 + column * HALF
                lined[:, C2 * column : C2 * (column + 1)] = held[row : row + HALF, C2 * a : C2 * (a + 1)]
            for t in range(25):
                striped[t, pl.ds(a, HALF, stride=2), :] = lined[:, LANES * t : LANES * (t + 1)]
        for t in range(25):
            prediction[slot, :, LANES * t : LANES * (t + 1)] = striped[t].astype(BF16)


def hold(held, value):
    rows, width = value.shape
    for t in range(-(-width // LANES)):
        part = value[:, LANES * t : min(width, LANES * (t + 1))]
        if part.shape[1] < LANES:
            held[t, :rows, :] = jnp.zeros((rows, LANES), F32)
        held[t, :rows, : part.shape[1]] = part


def lay_flat(flat, source, first_entry, rows, width, first_row):
    unit = UNIT // width
    count = rows // unit
    base = first_entry // LANES - first_row
    tiles = -(-width // LANES)
    lane = lax.broadcasted_iota(jnp.int32, (count, LANES), 1)
    parts = {}
    for a in range(unit):
        for t in range(tiles):
            value = source[t, pl.ds(a, count, stride=unit), :]
            place = first_entry % LANES + width * a + LANES * t
            shift = place % LANES
            if shift:
                value = pltpu.roll(value, shift, 1)
                low = jnp.where(lane >= shift, value, 0.0)
                high = jnp.where(lane < shift, value, 0.0)
                parts.setdefault(place // LANES, []).append(low)
                if not (t == tiles - 1 and shift + width - LANES * t <= LANES):
                    parts.setdefault(place // LANES + 1, []).append(high)
            else:
                parts.setdefault(place // LANES, []).append(value)
    merged = {j: functools.reduce(jnp.add, values) for j, values in parts.items()}
    for j in range(1, 25):
        flat[pl.ds(base + j, count, stride=25), :] = merged[j]
    head = merged[0]
    if 25 in merged:
        tail = merged[25]
        row = lax.broadcasted_iota(jnp.int32, (count, LANES), 0)
        before = pltpu.roll(tail, 1, 0) if count % 8 == 0 else jnp.concatenate([tail[-1:], tail[:-1]], axis=0)
        head = head + jnp.where(row > 0, before, 0.0)
    opening = flat[base : base + 1, :]
    flat[pl.ds(base, count, stride=25), :] = head
    flat[base : base + 1, :] = flat[base : base + 1, :] + opening
    if 25 in merged:
        flat[base + 25 * count : base + 25 * count + 1, :] = tail[count - 1 : count, :]
    else:
        flat[base + 25 * count : base + 25 * count + 1, :] = jnp.zeros((1, LANES), jnp.float32)


def clear_taps(held, tiles, rows):
    for t in range(tiles):
        held[t, 48:rows, :] = jnp.zeros((rows - 48, LANES), F32)


def grads_two_kernel(field, back, normed_b, hidden, grad_pre, level, change, cot_cat, keep, send, flat, held, tall, sums):
    flat[0:64, :] = jnp.zeros((64, LANES), F32)
    clear_taps(held, 4, 56)
    for t in range(4):
        width = min(LANES, C2 - LANES * t)
        deltas = []
        for slot in range(2):
            delta = back[64 * slot : 64 * (slot + 1), LANES * t : LANES * t + width].astype(F32)
            if width < LANES:
                delta = jnp.concatenate([delta, jnp.zeros((64, LANES - width), F32)], axis=1)
            deltas.append(delta.reshape(HALF, HALF, LANES))
        for p in range(7):
            for q in range(7):
                total = jnp.zeros((HALF, LANES), F32)
                for slot in range(2):
                    total = total + jnp.sum(field[slot, t, q : q + HALF, p : p + HALF, :] * deltas[slot], axis=0)
                sums[7 * p + q] = total
        held[t, :49, :] = jnp.sum(sums[...], axis=1)
    lay_flat(flat, held, 649800, 56, C2, SPLIT_ROW)
    hold(held, product_tn(normed_b[...], grad_pre[...]))
    lay_flat(flat, held, 669400, C2, 4 * C2, SPLIT_ROW)
    hold(tall, product_tn(hidden[...], change[...]))
    lay_flat(flat, tall, 1309400, 4 * C2, C2, SPLIT_ROW)
    hold(held, product_tn(level[...], cot_cat[...]))
    lay_flat(flat, held, 1949400, C2, 4 * C1, SPLIT_ROW)
    last = 17730 - SPLIT_ROW
    flat[last:, :] = jnp.zeros((17920 + 8 - SPLIT_ROW - last, LANES), F32)
    keep[:8, 0] = jnp.zeros((8, HELD, LANES), BF16)
    send[:8, 0] = jnp.zeros((8, HELD, LANES), BF16)
    split_out(lax.axis_index("c"), flat, keep, send, 9, 32, store_two)


def split_out(core, flat, keep, send, first, stop, store):
    def write(even, odd):
        for block in range(first, stop):
            target = odd if block % 2 else even
            for xl in range(2):
                for y in range(4):
                    start = (block - first) * BLOCK + (xl * 4 + y) * PIECE
                    store(target, block // 4, block // 2 % 2, xl, y, flat[start : start + HELD, :].astype(BF16))

    @pl.when(core == 0)
    def _():
        write(keep, send)

    @pl.when(core != 0)
    def _():
        write(send, keep)


def store_two(target, z, xh, xl, y, value):
    target[8 * xh + 4 * xl + y, z - 2] = value


def store_one(target, z, xh, xl, y, value):
    target[8 * xh + 4 * xl + y, z] = value


def last_kernel(entries, delta, top_got, bottom_got, kern, change, mask_two, mask_cat, cot_cat, blocks,
                w_down, w_in, w_out, normed, scales, field, keep, send,
                out, taps, conv, held_cat, rough, hidden, grad_pre, fine, back, sums, flat, held):
    out[...] = delta[...]
    for slot in range(2):
        add_rows(entries, out, slot, HALF, C2, top_got, bottom_got)
    load_taps(kern, taps, C2)
    conv_two(out, taps, conv, True)
    wet = jnp.concatenate([mask_two[...]] * 4, axis=1)[:, :C2]
    rough[...] = (wet * (change[...].astype(F32) + rows_two(conv)[:, :C2])).astype(BF16)
    held_cat[...] = mask_cat[...] * (cot_cat[...].astype(F32) + product(rough[...], w_down[...]))
    flat[0:8, :] = jnp.zeros((8, LANES), F32)
    for k in range(4):
        a, co = k // 2, k % 2
        rows = slice(LANES * k, LANES * (k + 1))
        fine[rows, :] = held_cat[:, C1 * k : C1 * (k + 1)].astype(BF16)
        values = normed[rows, :]
        act, slope = gelu_parts(product(values[:, :C1].astype(BF16), w_in[...]))
        hidden[rows, :] = act.astype(BF16)
        grad_pre[rows, :] = (product(fine[rows, :], w_out[...]) * slope).astype(BF16)
        grad = product_nt(grad_pre[rows, :], w_in[...])
        reverse = norm_back(grad, values[:, :C1], scales[rows, 0:1], C1)
        for slot in range(2):
            for column in range(HALF):
                start = slot * 64 + column * HALF
                part = reverse[start : start + HALF]
                back[0, a, slot, 2 * column + co] = part[:, :LANES]
                back[1, a, slot, 2 * column + co] = jnp.concatenate([part[:, LANES:], jnp.zeros((HALF, 2 * LANES - C1), F32)], axis=1)
    clear_taps(held, 2, 64)
    for t in range(2):
        sums[...] = jnp.zeros(sums.shape, F32)

        def body(index, carry):
            slot, a = index // 2, index % 2
            part = back[t, a, slot]
            for p in range(7):
                for q in range(7):
                    window = field[slot, t, q : q + SIDE, pl.ds(a + p, HALF, stride=2), :]
                    sums[7 * p + q] = sums[7 * p + q] + jnp.sum(window * part, axis=0)
            return carry

        lax.fori_loop(0, 4, body, 0)
        held[t, :49, :] = jnp.sum(sums[...], axis=1)
    lay_flat(flat, held, 0, 64, C1, 0)
    hold(held, product_tn(normed[:, :C1].astype(BF16), grad_pre[...]))
    lay_flat(flat, held, 9800, C1, 4 * C1, 0)
    hold(held, product_tn(hidden[...], fine[...]))
    lay_flat(flat, held, 169800, 4 * C1, C1, 0)
    hold(held, product_tn(blocks[...], rough[...]))
    lay_flat(flat, held, 329800, 4 * C1, C2, 0)
    flat[5077:, :] = jnp.zeros((5608 - 5077, LANES), F32)
    keep[8:, 2] = jnp.zeros((8, HELD, LANES), BF16)
    send[8:, 2] = jnp.zeros((8, HELD, LANES), BF16)
    split_out(lax.axis_index("c"), flat, keep, send, 0, 10, store_one)


def around(array, axes, step):
    size = 1
    for axis in axes:
        size *= lax.axis_size(axis)
    return lax.ppermute(array, axes, [(i, (i + step) % size) for i in range(size)])


def wide_sum(*parts):
    total = parts[0].astype(F32)
    for part in parts[1:]:
        total = total + part.astype(F32)
    return total.astype(BF16)


def other_core(send):
    return lax.ppermute(send, "c", [(0, 1), (1, 0)])


def added(terms):
    result = terms[0].astype(F32)
    for term in terms[1:]:
        result = result + term.astype(F32)
    return result.astype(BF16)


def x_parts_kernel(*refs):
    parts, outs = refs[:-4], refs[-4:]
    x = 2 * lax.axis_index("xh") + lax.axis_index("xl")
    for k in range(4):
        for z in range(outs[k].shape[0]):
            outs[k][z] = added([part[x ^ k, z] for part in parts])


def y_parts_kernel(keep, got, *outs):
    y = lax.axis_index("y")
    for k in range(4):
        for x in range(4):
            place = 4 * x + (y + k) % 4
            for z in range(outs[k].shape[1]):
                outs[k][x, z] = added([keep[place, z], got[place, z]])


def x_first_kernel(keep, got, *outs):
    x = 2 * lax.axis_index("xh") + lax.axis_index("xl")
    for k in range(4):
        for y in range(4):
            place = 4 * (x ^ k) + y
            for z in range(3):
                outs[k][y, z] = added([keep[place, z], got[place, z]])


def y_second_kernel(*refs):
    parts, outs = refs[:4], refs[4:]
    y = lax.axis_index("y")
    for k in range(4):
        for z in range(3):
            outs[k][z] = added([part[(y + k) % 4, z] for part in parts])


def over_y(parts):
    return [parts[0]] + [around(parts[k], ("y",), k) for k in range(1, 4)]


def over_x(parts):
    return [parts[0]] + [lax.ppermute(parts[k], ("xh", "xl"), [(i, i ^ k) for i in range(4)]) for k in range(1, 4)]


def merge_kernel(*refs):
    one, two, out = refs[:4], refs[4:8], refs[8]
    for z in range(8):
        terms = []
        if z < 3:
            terms += [ref[z] for ref in one]
        if z >= 2:
            terms += [ref[z - 2] for ref in two]
        out[z] = added(terms)


def final_kernel(parts, out):
    total = parts[0].astype(F32)
    for k in range(1, parts.shape[0]):
        total = total + parts[k].astype(F32)
    out[...] = total


def local(ocean_state, land_mask, wet_count, neighbours, kern_one, w_in_one, w_out_one, w_down, kern_two, w_in_two, w_out_two, w_up, cotangent):
    state, cot = ocean_state[0], cotangent[0]
    w_out_one, w_down, w_out_two = w_out_one.T, w_down.T, w_out_two.T
    mask = land_mask[0]
    entries = neighbours[0]
    rims_one, rims_two = (2, 3, SIDE, C1), (2, 3, HALF, C2)
    strip_one, strip_two = (22, 3, C1), (14, 3, C2)
    field_one, field_two = (2, 2, 22, 24, LANES), (2, 4, 14, 16, LANES)
    cat = (LANES, 4 * C1)
    west, east = call(rims_kernel, [(rims_one, BF16)] * 2, smem=1)(wet_count, state, mask)
    west_got, east_got = around(east, TILES, 1), around(west, TILES, -1)
    field, mask_cat, cot_cat, change, mask_two = call(
        before_kernel,
        [(field_one, F32), (cat, F32), (cat, BF16), ((LANES, C2), BF16), ((LANES, LANES), F32)],
        [((SIDE, 3328), F32), ((25, SIDE, LANES), F32), ((HALF, SIDE * C1), F32), (cat, F32)],
        room=16, us=2, smem=1,
    )(wet_count, state, mask, cot, w_up)
    field, top, bottom = call(strips_one_kernel, [(field_one, F32), (strip_one, BF16), (strip_one, BF16)], smem=1)(
        entries, field, west, west_got, east, east_got
    )
    top_got, bottom_got = around(bottom, LAT, 1), around(top, LAT, -1)
    field_one_own, normed_one, scales_one, blocks, coarse, west, east = call(
        first_kernel,
        [(field_one, F32), ((512, 256), F32), ((512, LANES), F32), (cat, BF16), ((LANES, C2), BF16), (rims_two, BF16), (rims_two, BF16)],
        [((2, 49, LANES), F32), ((2, 2, 2, SIDE, HALF, LANES), F32), (cat, F32)],
        room=16, us=6, smem=1,
    )(entries, field, top_got, bottom_got, kern_one, w_in_one, w_out_one, w_down, mask_cat, mask_two)

    def strips_two(rows, west, west_got, east, east_got):
        return call(strips_two_kernel, [(field_two, F32), (strip_two, BF16), (strip_two, BF16)], smem=1)(
            entries, rows, west, west_got, east, east_got
        )

    two = ((LANES, 4 * C2), BF16)
    slim = ((LANES, C2), BF16)
    west_got, east_got = around(east, TILES, 1), around(west, TILES, -1)
    field_two_own, top, bottom = strips_two(coarse, west, west_got, east, east_got)
    sides = field_two_own, around(bottom, LAT, 1), around(top, LAT, -1)
    field_in_two, normed_two, hidden_two, grad_pre_two, level, back, west, east = call(
        second_kernel,
        [(field_two, F32), slim, two, two, slim, slim, (rims_two, BF16), (rims_two, BF16)],
        [((4, 49, LANES), F32), ((4, 2, HALF, HALF, LANES), F32)],
        room=16, us=6, smem=1,
    )(entries, *sides, kern_two, w_in_two, w_out_two, coarse, change, mask_two)
    west_got, east_got = around(east, TILES, 1), around(west, TILES, -1)
    keep_two, send_two = call(
        grads_two_kernel,
        [((16, 6, HELD, LANES), BF16)] * 2,
        [((17920 + 8 - SPLIT_ROW, LANES), F32), ((13, C2, LANES), F32), ((4, 4 * C2, LANES), F32), ((49, HALF, LANES), F32)],
        room=16, us=7,
    )(field_in_two, back, normed_two, hidden_two, grad_pre_two, level, change, cot_cat)
    west_got, east_got, send_two = lax.optimization_barrier((west_got, east_got, send_two))
    got_two = other_core(send_two)
    (prediction,) = call(
        predict_kernel,
        [((2, SIDE, SIDE * C1), BF16)],
        [(cat, F32), ((HALF, SIDE * C1), F32), ((25, SIDE, LANES), F32)],
    )(blocks, level, w_up, mask_cat)
    field, top, bottom = strips_two(back, west, west_got, east, east_got)
    top_got, bottom_got = around(bottom, LAT, 1), around(top, LAT, -1)
    parts = list(call(y_parts_kernel, [((4, 6, HELD, LANES), BF16)] * 4)(keep_two, got_two))
    parts_two = over_y(parts)
    sides = field, top_got, bottom_got
    keep_one, send_one = call(
        last_kernel,
        [((16, 3, HELD, LANES), BF16)] * 2,
        [
            (field_two, F32),
            ((4, 49, LANES), F32),
            ((4, 2, HALF, HALF, LANES), F32),
            (cat, F32),
            slim,
            ((512, 4 * C1), BF16),
            ((512, 4 * C1), BF16),
            ((512, C1), BF16),
            ((2, 2, 2, SIDE, HALF, LANES), F32),
            ((49, HALF, LANES), F32),
            ((5608, LANES), F32),
            ((7, 800, LANES), F32),
        ],
        room=16, us=10, smem=1,
    )(entries, *sides, kern_two, change, mask_two, mask_cat, cot_cat, blocks, w_down, w_in_one, w_out_one, normed_one, scales_one, field_one_own)
    send_one, parts_two[1], parts_two[3] = lax.optimization_barrier((send_one, parts_two[1], parts_two[3]))
    return prediction[None], finish(keep_one, send_one, parts_two)


def finish(keep_one, send_one, parts_two):
    piece = ((3, HELD, LANES), BF16)
    parts = call(x_first_kernel, [((4, 3, HELD, LANES), BF16)] * 4)(keep_one, other_core(send_one))
    parts_one = over_x(parts)
    parts_two = call(x_parts_kernel, [((6, HELD, LANES), BF16)] * 4)(*parts_two)
    parts_one[1], _ = lax.optimization_barrier((parts_one[1], parts_two[1]))
    parts_two = over_x(parts_two)
    parts_one = over_y(call(y_second_kernel, [piece] * 4)(*parts_one))
    (total,) = call(merge_kernel, [((8, HELD, LANES), BF16)])(*parts_one, *parts_two)
    total = lax.all_to_all(total, "z", 0, 0)
    (total,) = call(final_kernel, [((HELD, LANES), F32)])(total)
    return total[:PIECE].reshape(-1)


def solution(mesh):
    mesh = Mesh(mesh.devices.reshape(8, 2, 2, 2, 4), TILES + LAT)
    return jax.shard_map(
        local,
        mesh=mesh,
        in_specs=(
            P(LAT, TILES, None, None),
            P(LAT, TILES, None),
            P(LAT, TILES),
            P(LAT, TILES, None),
            P(),
            P(),
            P(),
            P(),
            P(),
            P(),
            P(),
            P(),
            P(LAT, TILES, None, None),
        ),
        out_specs=(P(LAT, TILES, None, None), P(TILES + LAT)),
        check_vma=False,
    )
```

```python
import functools

import jax
import jax.numpy as jnp
from jax import lax
from jax.experimental import pallas as pl
from jax.experimental.pallas import tpu as pltpu
from jax.sharding import Mesh
from jax.sharding import PartitionSpec as P

TILES = ("z", "xh", "c")
LAT = ("xl", "y")
EPSILON = 1e-06
TANH_SCALE = 0.7978845608028654
CUBIC = 0.044715
LANES = 128
PIECE = 70
HELD = 72
UNIT = 3200
BLOCK = 560
C1, C2 = 200, 400
SIDE, HALF = 16, 8
F32, BF16 = jnp.float32, jnp.bfloat16
SPLIT_ROW = 5040
SPLIT = 4


def call(body, outs, scratch=(), smem=0, room=16, us=1):
    def run(*args):
        vmem = pl.BlockSpec(memory_space=pltpu.VMEM)
        specs = [pl.BlockSpec(memory_space=pltpu.SMEM)] * smem + [vmem] * (len(args) - smem)
        return pl.pallas_call(
            body,
            out_shape=[jax.ShapeDtypeStruct(shape, kind) for shape, kind in outs],
            in_specs=specs,
            out_specs=[vmem] * len(outs),
            scratch_shapes=[pltpu.VMEM(shape, kind) for shape, kind in scratch],
            compiler_params=pltpu.CompilerParams(vmem_limit_bytes=room * 2**20),
            cost_estimate=pl.CostEstimate(flops=us * 10**9, bytes_accessed=10**6, transcendentals=0),
        )(*args)

    return run


def product(left, right):
    return jnp.dot(left, right, preferred_element_type=F32)


def product_nt(left, right):
    return lax.dot_general(left, right, (((1,), (1,)), ((), ())), preferred_element_type=F32)


def product_tn(left, right):
    return lax.dot_general(left, right, (((0,), (0,)), ((), ())), preferred_element_type=F32)


def gelu_parts(values):
    square = values * values
    inner = jnp.tanh(TANH_SCALE * (values + CUBIC * square * values))
    half = 0.5 * (1.0 + inner)
    slope = half + 0.5 * values * (1.0 - inner * inner) * (TANH_SCALE * (1.0 + 3.0 * CUBIC * square))
    return values * half, slope


def lanes_of(shape):
    return lax.broadcasted_iota(jnp.int32, shape, len(shape) - 1)


def layer_norm(rows, channels):
    mean = jnp.sum(rows, axis=-1, keepdims=True) * (1.0 / channels)
    center = jnp.where(lanes_of(rows.shape) < channels, rows - mean, 0.0)
    scale = lax.rsqrt(jnp.sum(center * center, axis=-1, keepdims=True) * (1.0 / channels) + EPSILON)
    return center * scale, scale


def norm_back(grad_norm, normed, scale, channels):
    mean_grad = jnp.sum(grad_norm, axis=-1, keepdims=True) * (1.0 / channels)
    mean_cross = jnp.sum(grad_norm * normed, axis=-1, keepdims=True) * (1.0 / channels)
    return (grad_norm - mean_grad - normed * mean_cross) * scale


def choose(entries, slot, which, own, got):
    entry = entries[slot, which]
    held = jnp.maximum(entry, 0)
    place, source = held % 2, held // 2
    from_own = jnp.where((entry >= 0) & (source == 0), 1.0, 0.0)
    from_got = jnp.where((entry >= 0) & (source != 0), 1.0, 0.0)
    return own[place].astype(F32) * from_own + got[place].astype(F32) * from_got


def mask_lanes(mask, slot, filled):
    cells = SIDE * SIDE
    row = lax.broadcasted_iota(jnp.int32, (SIDE, cells), 0) * SIDE
    lane = lanes_of((SIDE, cells))
    live = jnp.broadcast_to(mask[slot : slot + 1, :].astype(F32), (SIDE, cells))
    live = jnp.where((lane >= row) & (lane < row + SIDE) & (filled > slot), live, 0.0).astype(BF16)
    cell = lax.broadcasted_iota(jnp.int32, (cells, SIDE), 0) % SIDE
    pick = jnp.where(cell == lanes_of((cells, SIDE)), 1.0, 0.0).astype(BF16)
    column = lax.broadcasted_iota(jnp.int32, (SIDE, SIDE * C1), 0) * C1
    lane = lanes_of((SIDE, SIDE * C1))
    spread = jnp.where((lane >= column) & (lane < column + C1), 1.0, 0.0).astype(BF16)
    return product(product(live, pick).astype(BF16), spread)


def rims_kernel(count, state, mask, west, east):
    for slot in range(2):
        masked = state[slot].astype(F32) * mask_lanes(mask, slot, count[0, 0])
        for k in range(3):
            west[slot, k] = masked[:, C1 * k : C1 * (k + 1)].astype(BF16)
            column = SIDE - 3 + k
            east[slot, k] = masked[:, C1 * column : C1 * (column + 1)].astype(BF16)


def to_blocks(values, wide, striped, lined, cat, slot):
    for t in range(25):
        striped[t] = values[:, LANES * t : LANES * (t + 1)]
    for a in range(2):
        for t in range(25):
            lined[:, LANES * t : LANES * (t + 1)] = striped[t, pl.ds(a, HALF, stride=2), :]
        for column in range(HALF):
            row = slot * 64 + column * HALF
            cat[row : row + HALF, C2 * a : C2 * (a + 1)] = lined[:, C2 * column : C2 * (column + 1)]


def before_kernel(count, state, mask, cotangent, w_up, field, mask_cat, cot_cat, change, mask_two, wide, striped, lined, held):
    field[...] = jnp.zeros(field.shape, F32)
    lane = lanes_of((SIDE, LANES))
    wide[...] = jnp.zeros(wide.shape, F32)
    for slot in range(2):
        spread = mask_lanes(mask, slot, count[0, 0])
        to_blocks(spread, wide, striped, lined, mask_cat, slot)
        to_blocks(cotangent[slot].astype(F32) * spread, wide, striped, lined, held, slot)
        wide[:, : SIDE * C1] = state[slot].astype(F32) * spread
        for column in range(SIDE):
            part = wide[:, C1 * column : C1 * column + 256]
            field[slot, 0, 3 + column, 3:19, :] = part[:, :LANES]
            field[slot, 1, 3 + column, 3:19, :] = jnp.where(lane < C1 - LANES, part[:, LANES:], 0.0)
    cot_cat[...] = held[...].astype(BF16)
    wet = mask_cat[:, 0:1]
    for k in range(1, 4):
        wet = jnp.maximum(wet, mask_cat[:, C1 * k : C1 * k + 1])
    mask_two[...] = jnp.broadcast_to(wet, (LANES, LANES))
    change[...] = (wet * product_nt(cot_cat[...], w_up[...])).astype(BF16)


def add_columns(entries, out, slot, side, channels, west, west_got, east, east_got):
    tiles = -(-channels // LANES)
    for which, start, own, got in ((0, 0, east, west_got), (1, side + 3, west, east_got)):
        value = choose(entries, slot, which, own, got)
        for t in range(tiles):
            width = min(LANES, channels - LANES * t)
            out[slot, t, start : start + 3, 3 : 3 + side, :width] = value[:, :, LANES * t : LANES * t + width]


def across(entries, slot, which, code):
    entry = entries[slot, which]
    return jnp.where((entry >= 0) & (entry // 2 == code), 1.0, 0.0)


def strips_of(entries, out, side, channels, top, bottom):
    north = [across(entries, slot, 2, 3) for slot in range(2)]
    south = [across(entries, slot, 3, 4) for slot in range(2)]
    for t in range(-(-channels // LANES)):
        width = min(LANES, channels - LANES * t)
        span = slice(LANES * t, LANES * t + width)
        parts = [out[slot, t, :, 3:6, :width] * north[slot] for slot in range(2)]
        top[:, :, span] = (parts[0] + parts[1]).astype(BF16)
        parts = [out[slot, t, :, side : side + 3, :width] * south[slot] for slot in range(2)]
        bottom[:, :, span] = (parts[0] + parts[1]).astype(BF16)


def add_rows(entries, out, slot, side, channels, top_got, bottom_got):
    for which, code, start, inner, got in ((2, 3, 0, side, top_got), (3, 4, side + 3, 3, bottom_got)):
        entry = entries[slot, which]
        place = jnp.maximum(entry, 0) % 2
        from_own = jnp.where((entry >= 0) & (entry // 2 == 0), 1.0, 0.0)
        from_got = across(entries, slot, which, code)
        for t in range(-(-channels // LANES)):
            width = min(LANES, channels - LANES * t)
            own = out[place, t, :, inner : inner + 3, :width]
            value = got[:, :, LANES * t : LANES * t + width].astype(F32)
            out[slot, t, :, start : start + 3, :width] = own * from_own + value * from_got


def strips_one_kernel(entries, field, west, west_got, east, east_got, out, top, bottom):
    out[...] = field[...]
    for slot in range(2):
        add_columns(entries, out, slot, SIDE, C1, west, west_got, east, east_got)
    strips_of(entries, out, SIDE, C1, top, bottom)


def strips_two_kernel(entries, rows, west, west_got, east, east_got, out, top, bottom):
    out[...] = jnp.zeros(out.shape, F32)
    for slot in range(2):
        for t in range(4):
            width = min(LANES, C2 - LANES * t)
            for column in range(HALF):
                start = slot * 64 + column * HALF
                out[slot, t, 3 + column, 3 : 3 + HALF, :width] = rows[start : start + HALF, LANES * t : LANES * t + width].astype(F32)
        add_columns(entries, out, slot, HALF, C2, west, west_got, east, east_got)
    strips_of(entries, out, HALF, C2, top, bottom)


def load_taps(kernel, taps, channels):
    tiles = -(-channels // LANES)
    taps[...] = jnp.zeros(taps.shape, F32)
    for t in range(tiles):
        width = min(LANES, channels - LANES * t)
        for p in range(7):
            taps[t, 7 * p : 7 * p + 7, :width] = kernel[p, :, LANES * t : LANES * t + width].astype(F32)


def conv_one(field, taps, out):
    def body(index, carry):
        slot, t = index // 2, index % 2
        for a in range(2):
            total = jnp.zeros((SIDE, HALF, LANES), F32)
            for p in range(7):
                for q in range(7):
                    window = field[slot, t, q : q + SIDE, pl.ds(a + p, HALF, stride=2), :]
                    total = total + window * taps[t, pl.ds(7 * p + q, 1), :][None]
            out[t, a, slot] = total
        return carry

    lax.fori_loop(0, 4, body, 0)


def conv_two(field, taps, out, flipped):
    def body(index, carry):
        slot, t = index // 4, index % 4
        total = jnp.zeros((HALF, HALF, LANES), F32)
        for p in range(7):
            for q in range(7):
                tap = 48 - (7 * p + q) if flipped else 7 * p + q
                total = total + field[slot, t, q : q + HALF, p : p + HALF, :] * taps[t, pl.ds(tap, 1), :][None]
        out[t, slot] = total
        return carry

    lax.fori_loop(0, 8, body, 0)


def first_kernel(entries, field, top_got, bottom_got, kern, w_in, w_out, w_down, mask_cat, mask_two,
                 out, normed, scales, blocks, coarse, west, east, taps, conv, held):
    out[...] = field[...]
    for slot in range(2):
        add_rows(entries, out, slot, SIDE, C1, top_got, bottom_got)
    load_taps(kern, taps, C1)
    conv_one(out, taps, conv)
    for a in range(2):
        for co in range(2):
            k = 2 * a + co
            rows, base = [], []
            for slot in range(2):
                for column in range(HALF):
                    place = 2 * column + co
                    rows.append(jnp.concatenate([conv[t, a, slot, place] for t in range(2)], axis=1))
                    base.append(jnp.concatenate([out[slot, t, 3 + place, pl.ds(3 + a, HALF, stride=2), :] for t in range(2)], axis=1))
            values, scale = layer_norm(jnp.concatenate(rows, axis=0), C1)
            normed[LANES * k : LANES * (k + 1), :] = values
            scales[LANES * k : LANES * (k + 1), :] = jnp.broadcast_to(scale, (LANES, LANES))
            hidden, _ = gelu_parts(product(values[:, :C1].astype(BF16), w_in[...]))
            branch = product_nt(hidden.astype(BF16), w_out[...])
            held[:, C1 * k : C1 * (k + 1)] = jnp.concatenate(base, axis=0)[:, :C1] + branch
    blocks[...] = (mask_cat[...] * held[...]).astype(BF16)
    wet = jnp.concatenate([mask_two[...]] * 4, axis=1)[:, :C2]
    rough = wet * product_nt(blocks[...], w_down[...])
    coarse[...] = rough.astype(BF16)
    send_rims(rough, west, east)


def send_rims(values, west, east):
    for slot in range(2):
        for k in range(3):
            start = slot * 64 + k * HALF
            west[slot, k] = values[start : start + HALF].astype(BF16)
            start = slot * 64 + (HALF - 3 + k) * HALF
            east[slot, k] = values[start : start + HALF].astype(BF16)


def rows_two(conv):
    return jnp.concatenate([conv[t].reshape(LANES, LANES) for t in range(4)], axis=1)


def second_kernel(entries, field, top_got, bottom_got, kern, w_in, w_out, coarse, change, mask_two,
                  out, normed_b, hidden, grad_pre, level, back, west, east, taps, conv):
    out[...] = field[...]
    for slot in range(2):
        add_rows(entries, out, slot, HALF, C2, top_got, bottom_got)
    load_taps(kern, taps, C2)
    conv_two(out, taps, conv, False)
    values, scale = layer_norm(rows_two(conv), C2)
    values = values[:, :C2]
    normed_b[...] = values.astype(BF16)
    act, slope = gelu_parts(product(normed_b[...], w_in[...]))
    hidden[...] = act.astype(BF16)
    grad_pre[...] = (product(change[...], w_out[...]) * slope).astype(BF16)
    wet = jnp.concatenate([mask_two[...]] * 4, axis=1)[:, :C2]
    level[...] = (wet * (coarse[...].astype(F32) + product_nt(hidden[...], w_out[...]))).astype(BF16)
    reverse = norm_back(product_nt(grad_pre[...], w_in[...]), values, scale, C2)
    back[...] = reverse.astype(BF16)
    send_rims(reverse, west, east)


def predict_kernel(blocks, level, w_up, mask_cat, prediction, held, lined, striped):
    held[...] = mask_cat[...] * (blocks[...].astype(F32) + product(level[...], w_up[...]))
    for slot in range(2):
        for a in range(2):
            for column in range(HALF):
                row = slot * 64 + column * HALF
                lined[:, C2 * column : C2 * (column + 1)] = held[row : row + HALF, C2 * a : C2 * (a + 1)]
            for t in range(25):
                striped[t, pl.ds(a, HALF, stride=2), :] = lined[:, LANES * t : LANES * (t + 1)]
        for t in range(25):
            prediction[slot, :, LANES * t : LANES * (t + 1)] = striped[t].astype(BF16)


def hold(held, value):
    rows, width = value.shape
    for t in range(-(-width // LANES)):
        part = value[:, LANES * t : min(width, LANES * (t + 1))]
        if part.shape[1] < LANES:
            held[t, :rows, :] = jnp.zeros((rows, LANES), F32)
        held[t, :rows, : part.shape[1]] = part


def lay_flat(flat, source, first_entry, rows, width, first_row):
    unit = UNIT // width
    count = rows // unit
    base = first_entry // LANES - first_row
    tiles = -(-width // LANES)
    lane = lax.broadcasted_iota(jnp.int32, (count, LANES), 1)
    parts = {}
    for a in range(unit):
        for t in range(tiles):
            value = source[t, pl.ds(a, count, stride=unit), :]
            place = first_entry % LANES + width * a + LANES * t
            shift = place % LANES
            if shift:
                value = pltpu.roll(value, shift, 1)
                low = jnp.where(lane >= shift, value, 0.0)
                high = jnp.where(lane < shift, value, 0.0)
                parts.setdefault(place // LANES, []).append(low)
                if not (t == tiles - 1 and shift + width - LANES * t <= LANES):
                    parts.setdefault(place // LANES + 1, []).append(high)
            else:
                parts.setdefault(place // LANES, []).append(value)
    merged = {j: functools.reduce(jnp.add, values) for j, values in parts.items()}
    for j in range(1, 25):
        flat[pl.ds(base + j, count, stride=25), :] = merged[j]
    head = merged[0]
    if 25 in merged:
        tail = merged[25]
        row = lax.broadcasted_iota(jnp.int32, (count, LANES), 0)
        before = pltpu.roll(tail, 1, 0) if count % 8 == 0 else jnp.concatenate([tail[-1:], tail[:-1]], axis=0)
        head = head + jnp.where(row > 0, before, 0.0)
    opening = flat[base : base + 1, :]
    flat[pl.ds(base, count, stride=25), :] = head
    flat[base : base + 1, :] = flat[base : base + 1, :] + opening
    if 25 in merged:
        flat[base + 25 * count : base + 25 * count + 1, :] = tail[count - 1 : count, :]
    else:
        flat[base + 25 * count : base + 25 * count + 1, :] = jnp.zeros((1, LANES), jnp.float32)


def clear_taps(held, tiles, rows):
    for t in range(tiles):
        held[t, 48:rows, :] = jnp.zeros((rows - 48, LANES), F32)


def grads_two_kernel(field, back, normed_b, hidden, grad_pre, level, change, cot_cat, keep, send, carry, flat, held, tall, sums):
    flat[0:64, :] = jnp.zeros((64, LANES), F32)
    clear_taps(held, 4, 56)
    for t in range(4):
        width = min(LANES, C2 - LANES * t)
        deltas = []
        for slot in range(2):
            delta = back[64 * slot : 64 * (slot + 1), LANES * t : LANES * t + width].astype(F32)
            if width < LANES:
                delta = jnp.concatenate([delta, jnp.zeros((64, LANES - width), F32)], axis=1)
            deltas.append(delta.reshape(HALF, HALF, LANES))
        for p in range(7):
            for q in range(7):
                total = jnp.zeros((HALF, LANES), F32)
                for slot in range(2):
                    total = total + jnp.sum(field[slot, t, q : q + HALF, p : p + HALF, :] * deltas[slot], axis=0)
                sums[7 * p + q] = total
        held[t, :49, :] = jnp.sum(sums[...], axis=1)
    lay_flat(flat, held, 649800, 56, C2, SPLIT_ROW)
    hold(held, product_tn(normed_b[...], grad_pre[...]))
    lay_flat(flat, held, 669400, C2, 4 * C2, SPLIT_ROW)
    hold(tall, product_tn(hidden[...], change[...]))
    lay_flat(flat, tall, 1309400, 4 * C2, C2, SPLIT_ROW)
    hold(held, product_tn(level[...], cot_cat[...]))
    lay_flat(flat, held, 1949400, C2, 4 * C1, SPLIT_ROW)
    last = 17730 - SPLIT_ROW
    flat[last:, :] = jnp.zeros((17920 + 8 - SPLIT_ROW - last, LANES), F32)
    carry[...] = flat[0:BLOCK, :]
    keep[:8, 0] = jnp.zeros((8, HELD, LANES), BF16)
    send[:8, 0] = jnp.zeros((8, HELD, LANES), BF16)
    split_out(lax.axis_index("c"), flat, keep, send, 9, 32, store_two)


def split_out(core, flat, keep, send, first, stop, store):
    def write(even, odd):
        for block in range(first, stop):
            target = odd if block % 2 else even
            for xl in range(2):
                for y in range(4):
                    start = (block - first) * BLOCK + (xl * 4 + y) * PIECE
                    store(target, block // 4, block // 2 % 2, xl, y, flat[start : start + HELD, :].astype(BF16))

    @pl.when(core == 0)
    def _():
        write(keep, send)

    @pl.when(core != 0)
    def _():
        write(send, keep)


def store_two(target, z, xh, xl, y, value):
    target[8 * xh + 4 * xl + y, z - 2] = value


def store_one(target, z, xh, xl, y, value):
    target[8 * xh + 4 * xl + y, z] = value


def last_kernel(entries, delta, top_got, bottom_got, kern, change, mask_two, mask_cat, cot_cat, blocks,
                w_down, w_in, w_out, normed, scales, field, carry, keep, send,
                out, taps, conv, held_cat, rough, hidden, grad_pre, fine, back, sums, flat, held):
    out[...] = delta[...]
    for slot in range(2):
        add_rows(entries, out, slot, HALF, C2, top_got, bottom_got)
    load_taps(kern, taps, C2)
    conv_two(out, taps, conv, True)
    wet = jnp.concatenate([mask_two[...]] * 4, axis=1)[:, :C2]
    rough[...] = (wet * (change[...].astype(F32) + rows_two(conv)[:, :C2])).astype(BF16)
    held_cat[...] = mask_cat[...] * (cot_cat[...].astype(F32) + product(rough[...], w_down[...]))
    flat[0:8, :] = jnp.zeros((8, LANES), F32)
    for k in range(4):
        a, co = k // 2, k % 2
        rows = slice(LANES * k, LANES * (k + 1))
        fine[rows, :] = held_cat[:, C1 * k : C1 * (k + 1)].astype(BF16)
        values = normed[rows, :]
        act, slope = gelu_parts(product(values[:, :C1].astype(BF16), w_in[...]))
        hidden[rows, :] = act.astype(BF16)
        grad_pre[rows, :] = (product(fine[rows, :], w_out[...]) * slope).astype(BF16)
        grad = product_nt(grad_pre[rows, :], w_in[...])
        reverse = norm_back(grad, values[:, :C1], scales[rows, 0:1], C1)
        for slot in range(2):
            for column in range(HALF):
                start = slot * 64 + column * HALF
                part = reverse[start : start + HALF]
                back[0, a, slot, 2 * column + co] = part[:, :LANES]
                back[1, a, slot, 2 * column + co] = jnp.concatenate([part[:, LANES:], jnp.zeros((HALF, 2 * LANES - C1), F32)], axis=1)
    clear_taps(held, 2, 64)
    for t in range(2):
        sums[...] = jnp.zeros(sums.shape, F32)

        def body(index, carry):
            slot, a = index // 2, index % 2
            part = back[t, a, slot]
            for p in range(7):
                for q in range(7):
                    window = field[slot, t, q : q + SIDE, pl.ds(a + p, HALF, stride=2), :]
                    sums[7 * p + q] = sums[7 * p + q] + jnp.sum(window * part, axis=0)
            return carry

        lax.fori_loop(0, 4, body, 0)
        held[t, :49, :] = jnp.sum(sums[...], axis=1)
    lay_flat(flat, held, 0, 64, C1, 0)
    hold(held, product_tn(normed[:, :C1].astype(BF16), grad_pre[...]))
    lay_flat(flat, held, 9800, C1, 4 * C1, 0)
    hold(held, product_tn(hidden[...], fine[...]))
    lay_flat(flat, held, 169800, 4 * C1, C1, 0)
    hold(held, product_tn(blocks[...], rough[...]))
    lay_flat(flat, held, 329800, 4 * C1, C2, 0)
    flat[5077:, :] = jnp.zeros((5608 - 5077, LANES), F32)
    flat[SPLIT_ROW : SPLIT_ROW + BLOCK, :] = flat[SPLIT_ROW : SPLIT_ROW + BLOCK, :] + carry[...]
    keep[8:, 2] = jnp.zeros((8, HELD, LANES), BF16)
    send[8:, 2] = jnp.zeros((8, HELD, LANES), BF16)
    split_out(lax.axis_index("c"), flat, keep, send, 0, 10, store_one)


def around(array, axes, step):
    size = 1
    for axis in axes:
        size *= lax.axis_size(axis)
    return lax.ppermute(array, axes, [(i, (i + step) % size) for i in range(size)])


def wide_sum(*parts):
    total = parts[0].astype(F32)
    for part in parts[1:]:
        total = total + part.astype(F32)
    return total.astype(BF16)


def other_core(send):
    return lax.ppermute(send, "c", [(0, 1), (1, 0)])


def added(terms):
    result = terms[0].astype(F32)
    for term in terms[1:]:
        result = result + term.astype(F32)
    return result.astype(BF16)


def x_parts_kernel(*refs):
    parts, outs = refs[:-4], refs[-4:]
    x = 2 * lax.axis_index("xh") + lax.axis_index("xl")
    for k in range(4):
        place = x ^ k
        first = added([part[jnp.maximum(6 * place - 2, 10)] for part in parts])
        outs[k][0] = jnp.where(place >= 2, first.astype(F32), 0.0).astype(BF16)
        for z in range(1, 6):
            index = jnp.where(place < 2, 5 * place + z - 1, 6 * place - 2 + z)
            outs[k][z] = added([part[index] for part in parts])


def y_parts_kernel(keep, got, *outs):
    y = lax.axis_index("y")
    for k in range(4):
        for x in range(4):
            place = 4 * x + (y + k) % 4
            for z in range(1 if x < 2 else 0, 6):
                index = 5 * x + z - 1 if x < 2 else 6 * x - 2 + z
                outs[k][index] = added([keep[place, z], got[place, z]])


def x_first_kernel(keep, got, *outs):
    x = 2 * lax.axis_index("xh") + lax.axis_index("xl")
    for k in range(4):
        for y in range(4):
            place = 4 * (x ^ k) + y
            for z in range(3):
                outs[k][y, z] = added([keep[place, z], got[place, z]])


def y_second_kernel(*refs):
    parts, outs = refs[:4], refs[4:]
    y = lax.axis_index("y")
    for k in range(4):
        for z in range(3):
            outs[k][z] = added([part[(y + k) % 4, z] for part in parts])


def over_y(parts):
    return [parts[0]] + [around(parts[k], ("y",), k) for k in range(1, 4)]


def over_x(parts):
    return [parts[0]] + [lax.ppermute(parts[k], ("xh", "xl"), [(i, i ^ k) for i in range(4)]) for k in range(1, 4)]


def merge_kernel(*refs):
    one, two, out = refs[:4], refs[4:8], refs[8]
    for z in range(8):
        terms = []
        if z < 3:
            terms += [ref[z] for ref in one]
        if z >= 2:
            terms += [ref[z - 2] for ref in two]
        out[z] = added(terms)


def final_kernel(parts, out):
    total = parts[0].astype(F32)
    for k in range(1, parts.shape[0]):
        total = total + parts[k].astype(F32)
    out[...] = total


def local(ocean_state, land_mask, wet_count, neighbours, kern_one, w_in_one, w_out_one, w_down, kern_two, w_in_two, w_out_two, w_up, cotangent):
    state, cot = ocean_state[0], cotangent[0]
    w_out_one, w_down, w_out_two = w_out_one.T, w_down.T, w_out_two.T
    mask = land_mask[0]
    entries = neighbours[0]
    rims_one, rims_two = (2, 3, SIDE, C1), (2, 3, HALF, C2)
    strip_one, strip_two = (22, 3, C1), (14, 3, C2)
    field_one, field_two = (2, 2, 22, 24, LANES), (2, 4, 14, 16, LANES)
    cat = (LANES, 4 * C1)
    west, east = call(rims_kernel, [(rims_one, BF16)] * 2, smem=1)(wet_count, state, mask)
    west_got, east_got = around(east, TILES, 1), around(west, TILES, -1)
    field, mask_cat, cot_cat, change, mask_two = call(
        before_kernel,
        [(field_one, F32), (cat, F32), (cat, BF16), ((LANES, C2), BF16), ((LANES, LANES), F32)],
        [((SIDE, 3328), F32), ((25, SIDE, LANES), F32), ((HALF, SIDE * C1), F32), (cat, F32)],
        room=16, us=2, smem=1,
    )(wet_count, state, mask, cot, w_up)
    field, top, bottom = call(strips_one_kernel, [(field_one, F32), (strip_one, BF16), (strip_one, BF16)], smem=1)(
        entries, field, west, west_got, east, east_got
    )
    top_got, bottom_got = around(bottom, LAT, 1), around(top, LAT, -1)
    field_one_own, normed_one, scales_one, blocks, coarse, west, east = call(
        first_kernel,
        [(field_one, F32), ((512, 256), F32), ((512, LANES), F32), (cat, BF16), ((LANES, C2), BF16), (rims_two, BF16), (rims_two, BF16)],
        [((2, 49, LANES), F32), ((2, 2, 2, SIDE, HALF, LANES), F32), (cat, F32)],
        room=16, us=6, smem=1,
    )(entries, field, top_got, bottom_got, kern_one, w_in_one, w_out_one, w_down, mask_cat, mask_two)

    def strips_two(rows, west, west_got, east, east_got):
        return call(strips_two_kernel, [(field_two, F32), (strip_two, BF16), (strip_two, BF16)], smem=1)(
            entries, rows, west, west_got, east, east_got
        )

    two = ((LANES, 4 * C2), BF16)
    slim = ((LANES, C2), BF16)
    west_got, east_got = around(east, TILES, 1), around(west, TILES, -1)
    field_two_own, top, bottom = strips_two(coarse, west, west_got, east, east_got)
    sides = field_two_own, around(bottom, LAT, 1), around(top, LAT, -1)
    field_in_two, normed_two, hidden_two, grad_pre_two, level, back, west, east = call(
        second_kernel,
        [(field_two, F32), slim, two, two, slim, slim, (rims_two, BF16), (rims_two, BF16)],
        [((4, 49, LANES), F32), ((4, 2, HALF, HALF, LANES), F32)],
        room=16, us=6, smem=1,
    )(entries, *sides, kern_two, w_in_two, w_out_two, coarse, change, mask_two)
    west_got, east_got = around(east, TILES, 1), around(west, TILES, -1)
    keep_two, send_two, carry = call(
        grads_two_kernel,
        [((16, 6, HELD, LANES), BF16)] * 2 + [((BLOCK, LANES), F32)],
        [((17920 + 8 - SPLIT_ROW, LANES), F32), ((13, C2, LANES), F32), ((4, 4 * C2, LANES), F32), ((49, HALF, LANES), F32)],
        room=16, us=7,
    )(field_in_two, back, normed_two, hidden_two, grad_pre_two, level, change, cot_cat)
    west_got, east_got, send_two = lax.optimization_barrier((west_got, east_got, send_two))
    got_two = other_core(send_two)
    (prediction,) = call(
        predict_kernel,
        [((2, SIDE, SIDE * C1), BF16)],
        [(cat, F32), ((HALF, SIDE * C1), F32), ((25, SIDE, LANES), F32)],
    )(blocks, level, w_up, mask_cat)
    field, top, bottom = strips_two(back, west, west_got, east, east_got)
    top_got, bottom_got = around(bottom, LAT, 1), around(top, LAT, -1)
    parts = list(call(y_parts_kernel, [((22, HELD, LANES), BF16)] * 4)(keep_two, got_two))
    parts_two = over_y(parts)
    sides = field, top_got, bottom_got
    keep_one, send_one = call(
        last_kernel,
        [((16, 3, HELD, LANES), BF16)] * 2,
        [
            (field_two, F32),
            ((4, 49, LANES), F32),
            ((4, 2, HALF, HALF, LANES), F32),
            (cat, F32),
            slim,
            ((512, 4 * C1), BF16),
            ((512, 4 * C1), BF16),
            ((512, C1), BF16),
            ((2, 2, 2, SIDE, HALF, LANES), F32),
            ((49, HALF, LANES), F32),
            ((5608, LANES), F32),
            ((7, 800, LANES), F32),
        ],
        room=16, us=10, smem=1,
    )(entries, *sides, kern_two, change, mask_two, mask_cat, cot_cat, blocks, w_down, w_in_one, w_out_one, normed_one, scales_one, field_one_own, carry)
    send_one, parts_two[1], parts_two[3] = lax.optimization_barrier((send_one, parts_two[1], parts_two[3]))
    return prediction[None], finish(keep_one, send_one, parts_two)


def finish(keep_one, send_one, parts_two):
    piece = ((3, HELD, LANES), BF16)
    parts = call(x_first_kernel, [((4, 3, HELD, LANES), BF16)] * 4)(keep_one, other_core(send_one))
    parts_one = over_x(parts)
    parts_two = call(x_parts_kernel, [((6, HELD, LANES), BF16)] * 4)(*parts_two)
    parts_one[1], _ = lax.optimization_barrier((parts_one[1], parts_two[1]))
    parts_two = over_x(parts_two)
    parts_one = over_y(call(y_second_kernel, [piece] * 4)(*parts_one))
    (total,) = call(merge_kernel, [((8, HELD, LANES), BF16)])(*parts_one, *parts_two)
    total = lax.all_to_all(total, "z", 0, 0)
    (total,) = call(final_kernel, [((HELD, LANES), F32)])(total)
    return total[:PIECE].reshape(-1)


def solution(mesh):
    mesh = Mesh(mesh.devices.reshape(8, 2, 2, 2, 4), TILES + LAT)
    return jax.shard_map(
        local,
        mesh=mesh,
        in_specs=(
            P(LAT, TILES, None, None),
            P(LAT, TILES, None),
            P(LAT, TILES),
            P(LAT, TILES, None),
            P(),
            P(),
            P(),
            P(),
            P(),
            P(),
            P(),
            P(),
            P(LAT, TILES, None, None),
        ),
        out_specs=(P(LAT, TILES, None, None), P(TILES + LAT)),
        check_vma=False,
    )
```

```python
import functools

import jax
import jax.numpy as jnp
from jax import lax
from jax.experimental import pallas as pl
from jax.experimental.pallas import tpu as pltpu
from jax.sharding import Mesh
from jax.sharding import PartitionSpec as P

TILES = ("z", "xh", "c")
LAT = ("xl", "y")
EPSILON = 1e-06
TANH_SCALE = 0.7978845608028654
CUBIC = 0.044715
LANES = 128
PIECE = 70
HELD = 72
UNIT = 3200
BLOCK = 560
C1, C2 = 200, 400
SIDE, HALF = 16, 8
F32, BF16 = jnp.float32, jnp.bfloat16
SPLIT_ROW = 5040
SPLIT = 4


def call(body, outs, scratch=(), smem=0, room=16, us=1):
    def run(*args):
        vmem = pl.BlockSpec(memory_space=pltpu.VMEM)
        specs = [pl.BlockSpec(memory_space=pltpu.SMEM)] * smem + [vmem] * (len(args) - smem)
        return pl.pallas_call(
            body,
            out_shape=[jax.ShapeDtypeStruct(shape, kind) for shape, kind in outs],
            in_specs=specs,
            out_specs=[vmem] * len(outs),
            scratch_shapes=[pltpu.VMEM(shape, kind) for shape, kind in scratch],
            compiler_params=pltpu.CompilerParams(vmem_limit_bytes=room * 2**20),
            cost_estimate=pl.CostEstimate(flops=us * 10**9, bytes_accessed=10**6, transcendentals=0),
        )(*args)

    return run


def product(left, right):
    return jnp.dot(left, right, preferred_element_type=F32)


def product_nt(left, right):
    return lax.dot_general(left, right, (((1,), (1,)), ((), ())), preferred_element_type=F32)


def product_tn(left, right):
    return lax.dot_general(left, right, (((0,), (0,)), ((), ())), preferred_element_type=F32)


def gelu_parts(values):
    square = values * values
    inner = jnp.tanh(TANH_SCALE * (values + CUBIC * square * values))
    half = 0.5 * (1.0 + inner)
    slope = half + 0.5 * values * (1.0 - inner * inner) * (TANH_SCALE * (1.0 + 3.0 * CUBIC * square))
    return values * half, slope


def lanes_of(shape):
    return lax.broadcasted_iota(jnp.int32, shape, len(shape) - 1)


def layer_norm(rows, channels):
    mean = jnp.sum(rows, axis=-1, keepdims=True) * (1.0 / channels)
    center = jnp.where(lanes_of(rows.shape) < channels, rows - mean, 0.0)
    scale = lax.rsqrt(jnp.sum(center * center, axis=-1, keepdims=True) * (1.0 / channels) + EPSILON)
    return center * scale, scale


def norm_back(grad_norm, normed, scale, channels):
    mean_grad = jnp.sum(grad_norm, axis=-1, keepdims=True) * (1.0 / channels)
    mean_cross = jnp.sum(grad_norm * normed, axis=-1, keepdims=True) * (1.0 / channels)
    return (grad_norm - mean_grad - normed * mean_cross) * scale


def choose(entries, slot, which, own, got):
    entry = entries[slot, which]
    held = jnp.maximum(entry, 0)
    place, source = held % 2, held // 2
    from_own = jnp.where((entry >= 0) & (source == 0), 1.0, 0.0)
    from_got = jnp.where((entry >= 0) & (source != 0), 1.0, 0.0)
    return own[place].astype(F32) * from_own + got[place].astype(F32) * from_got


def mask_lanes(mask, slot, filled):
    cells = SIDE * SIDE
    row = lax.broadcasted_iota(jnp.int32, (SIDE, cells), 0) * SIDE
    lane = lanes_of((SIDE, cells))
    live = jnp.broadcast_to(mask[slot : slot + 1, :].astype(F32), (SIDE, cells))
    live = jnp.where((lane >= row) & (lane < row + SIDE) & (filled > slot), live, 0.0).astype(BF16)
    cell = lax.broadcasted_iota(jnp.int32, (cells, SIDE), 0) % SIDE
    pick = jnp.where(cell == lanes_of((cells, SIDE)), 1.0, 0.0).astype(BF16)
    column = lax.broadcasted_iota(jnp.int32, (SIDE, SIDE * C1), 0) * C1
    lane = lanes_of((SIDE, SIDE * C1))
    spread = jnp.where((lane >= column) & (lane < column + C1), 1.0, 0.0).astype(BF16)
    return product(product(live, pick).astype(BF16), spread)


def rims_kernel(count, state, mask, west, east):
    for slot in range(2):
        masked = state[slot].astype(F32) * mask_lanes(mask, slot, count[0, 0])
        for k in range(3):
            west[slot, k] = masked[:, C1 * k : C1 * (k + 1)].astype(BF16)
            column = SIDE - 3 + k
            east[slot, k] = masked[:, C1 * column : C1 * (column + 1)].astype(BF16)


def to_blocks(values, wide, striped, lined, cat, slot):
    for t in range(25):
        striped[t] = values[:, LANES * t : LANES * (t + 1)]
    for a in range(2):
        for t in range(25):
            lined[:, LANES * t : LANES * (t + 1)] = striped[t, pl.ds(a, HALF, stride=2), :]
        for column in range(HALF):
            row = slot * 64 + column * HALF
            cat[row : row + HALF, C2 * a : C2 * (a + 1)] = lined[:, C2 * column : C2 * (column + 1)]


def before_kernel(count, state, mask, cotangent, w_up, field, mask_cat, cot_cat, change, mask_two, wide, striped, lined, held):
    field[...] = jnp.zeros(field.shape, F32)
    lane = lanes_of((SIDE, LANES))
    wide[...] = jnp.zeros(wide.shape, F32)
    for slot in range(2):
        spread = mask_lanes(mask, slot, count[0, 0])
        to_blocks(spread, wide, striped, lined, mask_cat, slot)
        to_blocks(cotangent[slot].astype(F32) * spread, wide, striped, lined, held, slot)
        wide[:, : SIDE * C1] = state[slot].astype(F32) * spread
        for column in range(SIDE):
            part = wide[:, C1 * column : C1 * column + 256]
            field[slot, 0, 3 + column, 3:19, :] = part[:, :LANES]
            field[slot, 1, 3 + column, 3:19, :] = jnp.where(lane < C1 - LANES, part[:, LANES:], 0.0)
    cot_cat[...] = held[...].astype(BF16)
    wet = mask_cat[:, 0:1]
    for k in range(1, 4):
        wet = jnp.maximum(wet, mask_cat[:, C1 * k : C1 * k + 1])
    mask_two[...] = jnp.broadcast_to(wet, (LANES, LANES))
    change[...] = (wet * product_nt(cot_cat[...], w_up[...])).astype(BF16)


def add_columns(entries, out, slot, side, channels, west, west_got, east, east_got):
    tiles = -(-channels // LANES)
    for which, start, own, got in ((0, 0, east, west_got), (1, side + 3, west, east_got)):
        value = choose(entries, slot, which, own, got)
        for t in range(tiles):
            width = min(LANES, channels - LANES * t)
            out[slot, t, start : start + 3, 3 : 3 + side, :width] = value[:, :, LANES * t : LANES * t + width]


def across(entries, slot, which, code):
    entry = entries[slot, which]
    return jnp.where((entry >= 0) & (entry // 2 == code), 1.0, 0.0)


def strips_of(entries, out, side, channels, top, bottom):
    north = [across(entries, slot, 2, 3) for slot in range(2)]
    south = [across(entries, slot, 3, 4) for slot in range(2)]
    for t in range(-(-channels // LANES)):
        width = min(LANES, channels - LANES * t)
        span = slice(LANES * t, LANES * t + width)
        parts = [out[slot, t, :, 3:6, :width] * north[slot] for slot in range(2)]
        top[:, :, span] = (parts[0] + parts[1]).astype(BF16)
        parts = [out[slot, t, :, side : side + 3, :width] * south[slot] for slot in range(2)]
        bottom[:, :, span] = (parts[0] + parts[1]).astype(BF16)


def add_rows(entries, out, slot, side, channels, top_got, bottom_got):
    for which, code, start, inner, got in ((2, 3, 0, side, top_got), (3, 4, side + 3, 3, bottom_got)):
        entry = entries[slot, which]
        place = jnp.maximum(entry, 0) % 2
        from_own = jnp.where((entry >= 0) & (entry // 2 == 0), 1.0, 0.0)
        from_got = across(entries, slot, which, code)
        for t in range(-(-channels // LANES)):
            width = min(LANES, channels - LANES * t)
            own = out[place, t, :, inner : inner + 3, :width]
            value = got[:, :, LANES * t : LANES * t + width].astype(F32)
            out[slot, t, :, start : start + 3, :width] = own * from_own + value * from_got


def strips_one_kernel(entries, field, west, west_got, east, east_got, out, top, bottom):
    out[...] = field[...]
    for slot in range(2):
        add_columns(entries, out, slot, SIDE, C1, west, west_got, east, east_got)
    strips_of(entries, out, SIDE, C1, top, bottom)


def strips_two_kernel(entries, rows, west, west_got, east, east_got, out, top, bottom):
    out[...] = jnp.zeros(out.shape, F32)
    for slot in range(2):
        for t in range(4):
            width = min(LANES, C2 - LANES * t)
            for column in range(HALF):
                start = slot * 64 + column * HALF
                out[slot, t, 3 + column, 3 : 3 + HALF, :width] = rows[start : start + HALF, LANES * t : LANES * t + width].astype(F32)
        add_columns(entries, out, slot, HALF, C2, west, west_got, east, east_got)
    strips_of(entries, out, HALF, C2, top, bottom)


def load_taps(kernel, taps, channels):
    tiles = -(-channels // LANES)
    taps[...] = jnp.zeros(taps.shape, F32)
    for t in range(tiles):
        width = min(LANES, channels - LANES * t)
        for p in range(7):
            taps[t, 7 * p : 7 * p + 7, :width] = kernel[p, :, LANES * t : LANES * t + width].astype(F32)


def conv_one(field, taps, out):
    def body(index, carry):
        slot, t = index // 2, index % 2
        for a in range(2):
            total = jnp.zeros((SIDE, HALF, LANES), F32)
            for p in range(7):
                for q in range(7):
                    window = field[slot, t, q : q + SIDE, pl.ds(a + p, HALF, stride=2), :]
                    total = total + window * taps[t, pl.ds(7 * p + q, 1), :][None]
            out[t, a, slot] = total
        return carry

    lax.fori_loop(0, 4, body, 0)


def conv_two(field, taps, out, flipped):
    def body(index, carry):
        slot, t = index // 4, index % 4
        total = jnp.zeros((HALF, HALF, LANES), F32)
        for p in range(7):
            for q in range(7):
                tap = 48 - (7 * p + q) if flipped else 7 * p + q
                total = total + field[slot, t, q : q + HALF, p : p + HALF, :] * taps[t, pl.ds(tap, 1), :][None]
        out[t, slot] = total
        return carry

    lax.fori_loop(0, 8, body, 0)


def first_kernel(entries, field, top_got, bottom_got, kern, w_in, w_out, w_down, mask_cat, mask_two,
                 out, normed, scales, blocks, coarse, west, east, taps, conv, held):
    out[...] = field[...]
    for slot in range(2):
        add_rows(entries, out, slot, SIDE, C1, top_got, bottom_got)
    load_taps(kern, taps, C1)
    conv_one(out, taps, conv)
    for a in range(2):
        for co in range(2):
            k = 2 * a + co
            rows, base = [], []
            for slot in range(2):
                for column in range(HALF):
                    place = 2 * column + co
                    rows.append(jnp.concatenate([conv[t, a, slot, place] for t in range(2)], axis=1))
                    base.append(jnp.concatenate([out[slot, t, 3 + place, pl.ds(3 + a, HALF, stride=2), :] for t in range(2)], axis=1))
            values, scale = layer_norm(jnp.concatenate(rows, axis=0), C1)
            normed[LANES * k : LANES * (k + 1), :] = values
            scales[LANES * k : LANES * (k + 1), :] = jnp.broadcast_to(scale, (LANES, LANES))
            hidden, _ = gelu_parts(product(values[:, :C1].astype(BF16), w_in[...]))
            branch = product_nt(hidden.astype(BF16), w_out[...])
            held[:, C1 * k : C1 * (k + 1)] = jnp.concatenate(base, axis=0)[:, :C1] + branch
    blocks[...] = (mask_cat[...] * held[...]).astype(BF16)
    wet = jnp.concatenate([mask_two[...]] * 4, axis=1)[:, :C2]
    rough = wet * product_nt(blocks[...], w_down[...])
    coarse[...] = rough.astype(BF16)
    send_rims(rough, west, east)


def send_rims(values, west, east):
    for slot in range(2):
        for k in range(3):
            start = slot * 64 + k * HALF
            west[slot, k] = values[start : start + HALF].astype(BF16)
            start = slot * 64 + (HALF - 3 + k) * HALF
            east[slot, k] = values[start : start + HALF].astype(BF16)


def rows_two(conv):
    return jnp.concatenate([conv[t].reshape(LANES, LANES) for t in range(4)], axis=1)


def second_kernel(entries, field, top_got, bottom_got, kern, w_in, w_out, coarse, change, mask_two,
                  out, normed_b, hidden, grad_pre, level, back, west, east, taps, conv):
    out[...] = field[...]
    for slot in range(2):
        add_rows(entries, out, slot, HALF, C2, top_got, bottom_got)
    load_taps(kern, taps, C2)
    conv_two(out, taps, conv, False)
    values, scale = layer_norm(rows_two(conv), C2)
    values = values[:, :C2]
    normed_b[...] = values.astype(BF16)
    act, slope = gelu_parts(product(normed_b[...], w_in[...]))
    hidden[...] = act.astype(BF16)
    grad_pre[...] = (product(change[...], w_out[...]) * slope).astype(BF16)
    wet = jnp.concatenate([mask_two[...]] * 4, axis=1)[:, :C2]
    level[...] = (wet * (coarse[...].astype(F32) + product_nt(hidden[...], w_out[...]))).astype(BF16)
    reverse = norm_back(product_nt(grad_pre[...], w_in[...]), values, scale, C2)
    back[...] = reverse.astype(BF16)
    send_rims(reverse, west, east)


def predict_kernel(blocks, level, w_up, mask_cat, prediction, held, lined, striped):
    held[...] = mask_cat[...] * (blocks[...].astype(F32) + product(level[...], w_up[...]))
    for slot in range(2):
        for a in range(2):
            for column in range(HALF):
                row = slot * 64 + column * HALF
                lined[:, C2 * column : C2 * (column + 1)] = held[row : row + HALF, C2 * a : C2 * (a + 1)]
            for t in range(25):
                striped[t, pl.ds(a, HALF, stride=2), :] = lined[:, LANES * t : LANES * (t + 1)]
        for t in range(25):
            prediction[slot, :, LANES * t : LANES * (t + 1)] = striped[t].astype(BF16)


def hold(held, value):
    rows, width = value.shape
    for t in range(-(-width // LANES)):
        part = value[:, LANES * t : min(width, LANES * (t + 1))]
        if part.shape[1] < LANES:
            held[t, :rows, :] = jnp.zeros((rows, LANES), F32)
        held[t, :rows, : part.shape[1]] = part


def lay_flat(flat, source, first_entry, rows, width, first_row):
    unit = UNIT // width
    count = rows // unit
    base = first_entry // LANES - first_row
    tiles = -(-width // LANES)
    lane = lax.broadcasted_iota(jnp.int32, (count, LANES), 1)
    parts = {}
    for a in range(unit):
        for t in range(tiles):
            value = source[t, pl.ds(a, count, stride=unit), :]
            place = first_entry % LANES + width * a + LANES * t
            shift = place % LANES
            if shift:
                value = pltpu.roll(value, shift, 1)
                low = jnp.where(lane >= shift, value, 0.0)
                high = jnp.where(lane < shift, value, 0.0)
                parts.setdefault(place // LANES, []).append(low)
                if not (t == tiles - 1 and shift + width - LANES * t <= LANES):
                    parts.setdefault(place // LANES + 1, []).append(high)
            else:
                parts.setdefault(place // LANES, []).append(value)
    merged = {j: functools.reduce(jnp.add, values) for j, values in parts.items()}
    for j in range(1, 25):
        flat[pl.ds(base + j, count, stride=25), :] = merged[j]
    head = merged[0]
    if 25 in merged:
        tail = merged[25]
        row = lax.broadcasted_iota(jnp.int32, (count, LANES), 0)
        before = pltpu.roll(tail, 1, 0) if count % 8 == 0 else jnp.concatenate([tail[-1:], tail[:-1]], axis=0)
        head = head + jnp.where(row > 0, before, 0.0)
    opening = flat[base : base + 1, :]
    flat[pl.ds(base, count, stride=25), :] = head
    flat[base : base + 1, :] = flat[base : base + 1, :] + opening
    if 25 in merged:
        flat[base + 25 * count : base + 25 * count + 1, :] = tail[count - 1 : count, :]
    else:
        flat[base + 25 * count : base + 25 * count + 1, :] = jnp.zeros((1, LANES), jnp.float32)


def clear_taps(held, tiles, rows):
    for t in range(tiles):
        held[t, 48:rows, :] = jnp.zeros((rows - 48, LANES), F32)


def grads_two_kernel(field, back, normed_b, hidden, grad_pre, level, change, cot_cat, keep, send, flat, held, tall, sums):
    flat[0:64, :] = jnp.zeros((64, LANES), F32)
    clear_taps(held, 4, 56)
    for t in range(4):
        width = min(LANES, C2 - LANES * t)
        deltas = []
        for slot in range(2):
            delta = back[64 * slot : 64 * (slot + 1), LANES * t : LANES * t + width].astype(F32)
            if width < LANES:
                delta = jnp.concatenate([delta, jnp.zeros((64, LANES - width), F32)], axis=1)
            deltas.append(delta.reshape(HALF, HALF, LANES))
        for p in range(7):
            for q in range(7):
                total = jnp.zeros((HALF, LANES), F32)
                for slot in range(2):
                    total = total + jnp.sum(field[slot, t, q : q + HALF, p : p + HALF, :] * deltas[slot], axis=0)
                sums[7 * p + q] = total
        held[t, :49, :] = jnp.sum(sums[...], axis=1)
    lay_flat(flat, held, 649800, 56, C2, SPLIT_ROW)
    hold(held, product_tn(normed_b[...], grad_pre[...]))
    lay_flat(flat, held, 669400, C2, 4 * C2, SPLIT_ROW)
    hold(tall, product_tn(hidden[...], change[...]))
    lay_flat(flat, tall, 1309400, 4 * C2, C2, SPLIT_ROW)
    hold(held, product_tn(level[...], cot_cat[...]))
    lay_flat(flat, held, 1949400, C2, 4 * C1, SPLIT_ROW)
    last = 17730 - SPLIT_ROW
    flat[last:, :] = jnp.zeros((17920 + 8 - SPLIT_ROW - last, LANES), F32)
    keep[:8, 0] = jnp.zeros((8, HELD, LANES), BF16)
    send[:8, 0] = jnp.zeros((8, HELD, LANES), BF16)
    split_out(lax.axis_index("c"), flat, keep, send, 9, 32, store_two)


def split_out(core, flat, keep, send, first, stop, store):
    def write(even, odd):
        for block in range(first, stop):
            target = odd if block % 2 else even
            for xl in range(2):
                for y in range(4):
                    start = (block - first) * BLOCK + (xl * 4 + y) * PIECE
                    store(target, block // 4, block // 2 % 2, xl, y, flat[start : start + HELD, :].astype(BF16))

    @pl.when(core == 0)
    def _():
        write(keep, send)

    @pl.when(core != 0)
    def _():
        write(send, keep)


def store_two(target, z, xh, xl, y, value):
    target[8 * xh + 4 * xl + y, z - 2] = value


def store_one(target, z, xh, xl, y, value):
    target[8 * xh + 4 * xl + y, z] = value


def last_kernel(entries, delta, top_got, bottom_got, kern, change, mask_two, mask_cat, cot_cat, blocks,
                w_down, w_in, w_out, normed, scales, field, keep, send,
                out, taps, conv, held_cat, rough, hidden, grad_pre, fine, back, sums, flat, held):
    out[...] = delta[...]
    for slot in range(2):
        add_rows(entries, out, slot, HALF, C2, top_got, bottom_got)
    load_taps(kern, taps, C2)
    conv_two(out, taps, conv, True)
    wet = jnp.concatenate([mask_two[...]] * 4, axis=1)[:, :C2]
    rough[...] = (wet * (change[...].astype(F32) + rows_two(conv)[:, :C2])).astype(BF16)
    held_cat[...] = mask_cat[...] * (cot_cat[...].astype(F32) + product(rough[...], w_down[...]))
    flat[0:8, :] = jnp.zeros((8, LANES), F32)
    for k in range(4):
        a, co = k // 2, k % 2
        rows = slice(LANES * k, LANES * (k + 1))
        fine[rows, :] = held_cat[:, C1 * k : C1 * (k + 1)].astype(BF16)
        values = normed[rows, :]
        act, slope = gelu_parts(product(values[:, :C1].astype(BF16), w_in[...]))
        hidden[rows, :] = act.astype(BF16)
        grad_pre[rows, :] = (product(fine[rows, :], w_out[...]) * slope).astype(BF16)
        grad = product_nt(grad_pre[rows, :], w_in[...])
        reverse = norm_back(grad, values[:, :C1], scales[rows, 0:1], C1)
        for slot in range(2):
            for column in range(HALF):
                start = slot * 64 + column * HALF
                part = reverse[start : start + HALF]
                back[0, a, slot, 2 * column + co] = part[:, :LANES]
                back[1, a, slot, 2 * column + co] = jnp.concatenate([part[:, LANES:], jnp.zeros((HALF, 2 * LANES - C1), F32)], axis=1)
    clear_taps(held, 2, 64)
    for t in range(2):
        sums[...] = jnp.zeros(sums.shape, F32)

        def body(index, carry):
            slot, a = index // 2, index % 2
            part = back[t, a, slot]
            for p in range(7):
                for q in range(7):
                    window = field[slot, t, q : q + SIDE, pl.ds(a + p, HALF, stride=2), :]
                    sums[7 * p + q] = sums[7 * p + q] + jnp.sum(window * part, axis=0)
            return carry

        lax.fori_loop(0, 4, body, 0)
        held[t, :49, :] = jnp.sum(sums[...], axis=1)
    lay_flat(flat, held, 0, 64, C1, 0)
    hold(held, product_tn(normed[:, :C1].astype(BF16), grad_pre[...]))
    lay_flat(flat, held, 9800, C1, 4 * C1, 0)
    hold(held, product_tn(hidden[...], fine[...]))
    lay_flat(flat, held, 169800, 4 * C1, C1, 0)
    hold(held, product_tn(blocks[...], rough[...]))
    lay_flat(flat, held, 329800, 4 * C1, C2, 0)
    flat[5077:, :] = jnp.zeros((5608 - 5077, LANES), F32)
    keep[8:, 2] = jnp.zeros((8, HELD, LANES), BF16)
    send[8:, 2] = jnp.zeros((8, HELD, LANES), BF16)
    split_out(lax.axis_index("c"), flat, keep, send, 0, 10, store_one)


def around(array, axes, step):
    size = 1
    for axis in axes:
        size *= lax.axis_size(axis)
    return lax.ppermute(array, axes, [(i, (i + step) % size) for i in range(size)])


def wide_sum(*parts):
    total = parts[0].astype(F32)
    for part in parts[1:]:
        total = total + part.astype(F32)
    return total.astype(BF16)


def other_core(send):
    return lax.ppermute(send, "c", [(0, 1), (1, 0)])


def added(terms):
    result = terms[0].astype(F32)
    for term in terms[1:]:
        result = result + term.astype(F32)
    return result.astype(BF16)


def x_parts_kernel(*refs):
    parts, outs = refs[:-4], refs[-4:]
    x = 2 * lax.axis_index("xh") + lax.axis_index("xl")
    for k in range(4):
        for z in range(outs[k].shape[0]):
            outs[k][z] = added([part[x ^ k, z] for part in parts])


def y_parts_kernel(keep, got, *outs):
    y = lax.axis_index("y")
    for k in range(4):
        for x in range(4):
            place = 4 * x + (y + k) % 4
            for z in range(outs[k].shape[1]):
                outs[k][x, z] = added([keep[place, z], got[place, z]])


def x_first_kernel(keep, got, *outs):
    x = 2 * lax.axis_index("xh") + lax.axis_index("xl")
    for k in range(4):
        for y in range(4):
            place = 4 * (x ^ k) + y
            for z in range(3):
                outs[k][y, z] = added([keep[place, z], got[place, z]])


def y_second_kernel(*refs):
    parts, outs = refs[:4], refs[4:]
    y = lax.axis_index("y")
    for k in range(4):
        for z in range(3):
            outs[k][z] = added([part[(y + k) % 4, z] for part in parts])


def over_y(parts):
    return [parts[0]] + [around(parts[k], ("y",), k) for k in range(1, 4)]


def over_x(parts):
    return [parts[0]] + [lax.ppermute(parts[k], ("xh", "xl"), [(i, i ^ k) for i in range(4)]) for k in range(1, 4)]


def merge_kernel(*refs):
    one, two, out = refs[:4], refs[4:8], refs[8]
    for z in range(8):
        terms = []
        if z < 3:
            terms += [ref[z] for ref in one]
        if z >= 2:
            terms += [ref[z - 2] for ref in two]
        out[z] = added(terms)


def final_kernel(parts, out):
    total = parts[0].astype(F32)
    for k in range(1, parts.shape[0]):
        total = total + parts[k].astype(F32)
    out[...] = total


def local(ocean_state, land_mask, wet_count, neighbours, kern_one, w_in_one, w_out_one, w_down, kern_two, w_in_two, w_out_two, w_up, cotangent):
    state, cot = ocean_state[0], cotangent[0]
    w_out_one, w_down, w_out_two = w_out_one.T, w_down.T, w_out_two.T
    mask = land_mask[0]
    entries = neighbours[0]
    rims_one, rims_two = (2, 3, SIDE, C1), (2, 3, HALF, C2)
    strip_one, strip_two = (22, 3, C1), (14, 3, C2)
    field_one, field_two = (2, 2, 22, 24, LANES), (2, 4, 14, 16, LANES)
    cat = (LANES, 4 * C1)
    west, east = call(rims_kernel, [(rims_one, BF16)] * 2, smem=1)(wet_count, state, mask)
    west_got, east_got = around(east, TILES, 1), around(west, TILES, -1)
    field, mask_cat, cot_cat, change, mask_two = call(
        before_kernel,
        [(field_one, F32), (cat, F32), (cat, BF16), ((LANES, C2), BF16), ((LANES, LANES), F32)],
        [((SIDE, 3328), F32), ((25, SIDE, LANES), F32), ((HALF, SIDE * C1), F32), (cat, F32)],
        room=16, us=2, smem=1,
    )(wet_count, state, mask, cot, w_up)
    field, top, bottom = call(strips_one_kernel, [(field_one, F32), (strip_one, BF16), (strip_one, BF16)], smem=1)(
        entries, field, west, west_got, east, east_got
    )
    top_got, bottom_got = around(bottom, LAT, 1), around(top, LAT, -1)
    field_one_own, normed_one, scales_one, blocks, coarse, west, east = call(
        first_kernel,
        [(field_one, F32), ((512, 256), F32), ((512, LANES), F32), (cat, BF16), ((LANES, C2), BF16), (rims_two, BF16), (rims_two, BF16)],
        [((2, 49, LANES), F32), ((2, 2, 2, SIDE, HALF, LANES), F32), (cat, F32)],
        room=16, us=6, smem=1,
    )(entries, field, top_got, bottom_got, kern_one, w_in_one, w_out_one, w_down, mask_cat, mask_two)

    def strips_two(rows, west, west_got, east, east_got):
        return call(strips_two_kernel, [(field_two, F32), (strip_two, BF16), (strip_two, BF16)], smem=1)(
            entries, rows, west, west_got, east, east_got
        )

    two = ((LANES, 4 * C2), BF16)
    slim = ((LANES, C2), BF16)
    west_got, east_got = around(east, TILES, 1), around(west, TILES, -1)
    field_two_own, top, bottom = strips_two(coarse, west, west_got, east, east_got)
    sides = field_two_own, around(bottom, LAT, 1), around(top, LAT, -1)
    field_in_two, normed_two, hidden_two, grad_pre_two, level, back, west, east = call(
        second_kernel,
        [(field_two, F32), slim, two, two, slim, slim, (rims_two, BF16), (rims_two, BF16)],
        [((4, 49, LANES), F32), ((4, 2, HALF, HALF, LANES), F32)],
        room=16, us=6, smem=1,
    )(entries, *sides, kern_two, w_in_two, w_out_two, coarse, change, mask_two)
    west_got, east_got = around(east, TILES, 1), around(west, TILES, -1)
    keep_two, send_two = call(
        grads_two_kernel,
        [((16, 6, HELD, LANES), BF16)] * 2,
        [((17920 + 8 - SPLIT_ROW, LANES), F32), ((13, C2, LANES), F32), ((4, 4 * C2, LANES), F32), ((49, HALF, LANES), F32)],
        room=16, us=7,
    )(field_in_two, back, normed_two, hidden_two, grad_pre_two, level, change, cot_cat)
    west_got, east_got, send_two = lax.optimization_barrier((west_got, east_got, send_two))
    got_two = other_core(send_two)
    (prediction,) = call(
        predict_kernel,
        [((2, SIDE, SIDE * C1), BF16)],
        [(cat, F32), ((HALF, SIDE * C1), F32), ((25, SIDE, LANES), F32)],
    )(blocks, level, w_up, mask_cat)
    field, top, bottom = strips_two(back, west, west_got, east, east_got)
    top_got, bottom_got = around(bottom, LAT, 1), around(top, LAT, -1)
    parts = list(call(y_parts_kernel, [((4, 6, HELD, LANES), BF16)] * 4)(keep_two, got_two))
    parts_two = over_y(parts)
    sides = field, top_got, bottom_got
    keep_one, send_one = call(
        last_kernel,
        [((16, 3, HELD, LANES), BF16)] * 2,
        [
            (field_two, F32),
            ((4, 49, LANES), F32),
            ((4, 2, HALF, HALF, LANES), F32),
            (cat, F32),
            slim,
            ((512, 4 * C1), BF16),
            ((512, 4 * C1), BF16),
            ((512, C1), BF16),
            ((2, 2, 2, SIDE, HALF, LANES), F32),
            ((49, HALF, LANES), F32),
            ((5608, LANES), F32),
            ((7, 800, LANES), F32),
        ],
        room=16, us=10, smem=1,
    )(entries, *sides, kern_two, change, mask_two, mask_cat, cot_cat, blocks, w_down, w_in_one, w_out_one, normed_one, scales_one, field_one_own)
    send_one, parts_two[1] = lax.optimization_barrier((send_one, parts_two[1]))
    return prediction[None], finish(keep_one, send_one, parts_two)


def finish(keep_one, send_one, parts_two):
    piece = ((3, HELD, LANES), BF16)
    parts = call(x_first_kernel, [((4, 3, HELD, LANES), BF16)] * 4)(keep_one, other_core(send_one))
    parts_one = over_x(parts)
    parts_two = call(x_parts_kernel, [((6, HELD, LANES), BF16)] * 4)(*parts_two)
    parts_one[1], _ = lax.optimization_barrier((parts_one[1], parts_two[1]))
    parts_two = over_x(parts_two)
    parts_one = over_y(call(y_second_kernel, [piece] * 4)(*parts_one))
    (total,) = call(merge_kernel, [((8, HELD, LANES), BF16)])(*parts_one, *parts_two)
    total = lax.all_to_all(total, "z", 0, 0)
    (total,) = call(final_kernel, [((HELD, LANES), F32)])(total)
    return total[:PIECE].reshape(-1)


def solution(mesh):
    mesh = Mesh(mesh.devices.reshape(8, 2, 2, 2, 4), TILES + LAT)
    return jax.shard_map(
        local,
        mesh=mesh,
        in_specs=(
            P(LAT, TILES, None, None),
            P(LAT, TILES, None),
            P(LAT, TILES),
            P(LAT, TILES, None),
            P(),
            P(),
            P(),
            P(),
            P(),
            P(),
            P(),
            P(),
            P(LAT, TILES, None, None),
        ),
        out_specs=(P(LAT, TILES, None, None), P(TILES + LAT)),
        check_vma=False,
    )
```
